32 devices in a mesh: kpt: 4 (over y, x), occ: 8 (over z, core).
Axes of the slice: x: 2, y: 2, z: 4, core: 2. Of those that a mesh axis runs over, the one named last changes fastest.
Arguments:
- factor: bfloat16 [2, 8, 8, 2, 256, 512], P(None, 'kpt', 'occ'), may hold values from -1.0546875 to 1.0546875
- partner: int32 [2, 8], replicated, may hold values from 0 to 7, as said below
- occ_energy: float32 [8, 8], replicated, may hold values from -3 to -0.5
- vir_sorted: float32 [8, 256], replicated, may hold values from 0.3 to 4.3, as said below
- vir_order: int32 [8, 256], replicated, may hold values from 0 to 255, each once within a row
Outputs:
- gradient_factor: bfloat16 [2, 8, 8, 2, 256, 512], P(None, 'kpt', 'occ')
The draws below stay inside these ranges and needn't reach their ends.
Inputs may be any that keep to these rules, and one draw needn't show every extreme that they name: With group g holding k-points g * 2 to (g + 1) * 2 - 1, partner[0, k] lies in group (k // 2) XOR 1 and partner[1, k] in group (k // 2) XOR 2; which k-point of that group is arbitrary, and several k-points may share one. `vir_sorted`: each row is ascending and begins with 0.3.
All inputs are finite; a program needn't handle non-finite values.
Results may differ from the reference program's by a relative error of at most 0.0037.
Values may be sent and summed in bfloat16 or wider, within the bound.
No kernel may reach another device: no remote copies, remote signals or barrier semaphores. Data moves between devices by JAX's collectives and lax.ppermute only.
A program may use at most 64 MiB of HBM per device.

```python
from functools import partial
import jax
import jax.numpy as jnp
from jax import lax

NV = 256
NAUX = 512
K_DEV = 2
NTR = 2
REACH = 1
NK = 8
NOCC = 8


def draw_partner(key, part):
    groups = NK // K_DEV
    point_ids = jnp.arange(NK, dtype=jnp.int32)
    group_of = point_ids // K_DEV
    first_slot = jnp.remainder(point_ids, K_DEV) == 0
    tables = []
    for transfer in range(NTR):
        flip_mask = 1 if transfer == 0 else groups // 2
        other_group = jnp.bitwise_xor(group_of, flip_mask)
        slots = jax.random.randint(jax.random.fold_in(key, 71 + transfer), (NK,), 0, K_DEV).astype(jnp.int32)
        if transfer == 1:
            to_last = jnp.logical_and(first_slot, group_of == groups // 2 - 1)
            to_first = jnp.logical_and(first_slot, group_of == groups // 2)
            slots = jnp.where(to_last, K_DEV - 1, slots)
            slots = jnp.where(to_first, 0, slots)
        table = other_group * K_DEV + slots
        tables.append(table.astype(jnp.int32))
    return jnp.stack(tables, axis=0)


def draw_vir_sorted(key, part):
    uniform_part = jax.random.uniform(jax.random.fold_in(key, 313), (NK, NV), jnp.float32)
    increments = 4.0 / NV * uniform_part
    running = jnp.cumsum(increments, axis=1)
    return (0.3 + running - running[:, 0:1]).astype(jnp.float32)


def levels(stream_key, extent, pieces, least, high):
    gain = 1.0
    for axis_at, blocks in pieces:
        draws = jax.random.uniform(jax.random.fold_in(jax.random.fold_in(stream_key, 6), axis_at), (blocks,), jnp.float32, least / len(pieces), high / len(pieces))
        gain = gain * jnp.repeat(jnp.exp(draws), extent[axis_at] // blocks).reshape((-1,) + (1,) * (len(extent) - 1 - axis_at))
    return gain


def normal_values(rng, dims, width, reach, pieces=(), kind=jnp.bfloat16):
    factor_of = levels(rng, dims, pieces, -0.22, 0.18) if pieces else 1.0
    result = jax.random.normal(rng, dims, jnp.float32) * width * factor_of
    return jnp.minimum(jnp.maximum(result, -reach), reach).astype(kind)


def setup_inputs(seed: int = 0) -> dict:
    key_list = jax.random.split(jax.random.key(seed), 6)
    factor = normal_values(key_list[0], (NTR, NK, NOCC, 2, NV, NAUX), ((2 * NAUX) ** -0.25), 1.0546875, ((1, 4), (2, 8)))
    partner = draw_partner(jax.random.fold_in(key_list[5], 71), 0)
    occ_energy = jnp.clip(jax.random.uniform(key_list[2], (NK, NOCC), jnp.float32, -3.0, -0.5), -3.0, -0.5)
    vir_sorted = draw_vir_sorted(jax.random.fold_in(key_list[5], 71), 0)
    vir_order = jax.vmap(lambda own: jax.random.permutation(own, NV))(jax.random.split(key_list[4], NK)).reshape((NK, NV)).astype(jnp.int32)
    return dict(factor=factor, partner=partner, occ_energy=occ_energy, vir_sorted=vir_sorted, vir_order=vir_order)


def virtual_energies(vir_sorted, vir_order):
    return jnp.take_along_axis(vir_sorted, vir_order, axis=1)


def point_gradient(factor_set, partner_row, occ_energy, virtual, point_id):
    partner_id = partner_row[point_id]
    own_block = factor_set[point_id].astype(jnp.float32)
    far_block = factor_set[partner_id].astype(jnp.float32)
    rotated = jnp.stack([own_block[:, 1], -own_block[:, 0]], axis=1)
    stacked = jnp.stack([own_block, rotated], axis=1)
    gradient = jnp.zeros(own_block.shape, jnp.float32)
    for offset in range(-REACH, REACH + 1):
        window = jnp.roll(far_block, -offset, axis=0)
        pair_ints = jnp.einsum("ircaq,icbq->irab", stacked, window)
        far_occ = jnp.roll(occ_energy[partner_id], -offset)
        denominator = occ_energy[point_id][:, None, None] + far_occ[:, None, None] - virtual[partner_id][None, :, None] - virtual[point_id][None, None, :]
        rounded = (pair_ints / denominator[:, None]).astype(jnp.bfloat16)
        amplitude = lax.optimization_barrier(rounded).astype(jnp.float32)
        real_part = amplitude[:, 0]
        imag_part = amplitude[:, 1]
        combined = jnp.stack([jnp.stack([real_part, -imag_part], axis=1), jnp.stack([imag_part, real_part], axis=1)], axis=1)
        gradient = gradient + jnp.einsum("ixcab,icbq->ixaq", combined, window)
    return gradient.astype(jnp.bfloat16)


def reference(factor, partner, occ_energy, vir_sorted, vir_order):
    virtual = virtual_energies(vir_sorted, vir_order)
    outputs = []
    for transfer in range(NTR):
        worker = partial(point_gradient, factor[transfer], partner[transfer], occ_energy, virtual)
        gradients = lax.map(worker, jnp.arange(NK, dtype=jnp.int32))
        outputs.append(gradients)
    return jnp.stack(outputs, axis=0)
```

```python
import functools

import jax
import jax.numpy as jnp
from jax import lax
from jax.experimental import pallas as pl
from jax.experimental.pallas import tpu as pltpu
from jax.sharding import PartitionSpec as P

F32 = jnp.float32
BF16 = jnp.bfloat16


def group_swap(block, bit):
    count = lax.axis_size("kpt")
    return lax.ppermute(block, "kpt", [(g, g ^ (1 << bit)) for g in range(count)])


def near_swap(block):
    count = lax.axis_size("occ")
    return lax.ppermute(block, "occ", [(i, i ^ 1) for i in range(count)])


def far_swap(block):
    count = lax.axis_size("occ")
    return lax.ppermute(
        block, "occ", [(i, (i + (1 if i % 2 else count - 1)) % count) for i in range(count)]
    )


def virtual_energies(vir_sorted, vir_order):
    ranks = jnp.arange(vir_sorted.shape[1], dtype=jnp.int32)
    matches = vir_order[:, :, None] == ranks[None, None, :]
    return jnp.sum(jnp.where(matches, vir_sorted[:, None, :], 0.0), axis=2)


def nt_dot(left, right):
    return lax.dot_general(left, right, (((1,), (1,)), ((), ())), preferred_element_type=F32)


def kernel(transfer, bit, kc, places, first, ids, partner, occ, *refs):
    row_ref, col_ref, own_ref = refs[:3]
    windows = refs[3 : 3 + len(places)]
    rest = refs[3 + len(places) :]
    out_ref = rest[-1]
    nv, naux = own_ref.shape[-2:]
    point = ids[0] * kc + pl.program_id(0)
    far_point = partner[transfer, point]
    orbit, total = ids[1], occ.shape[1]
    parity = lax.rem(orbit, 2)
    columns = {
        "own": orbit,
        "near": orbit + 1 - 2 * parity,
        "far": lax.rem(orbit + total - 1 + 2 * parity, total),
    }
    own = own_ref[...].reshape(2, nv, naux)
    real, imag = own[0], own[1]
    left = jnp.concatenate([real, imag], axis=0)
    right = jnp.concatenate([imag, -real], axis=0)
    gradient = None if first else rest[0][...].reshape(2 * nv, naux)
    for place, window_ref in zip(places, windows):
        window = window_ref[...].reshape(2, nv, naux)
        pair = nt_dot(left, window[0]) + nt_dot(right, window[1])
        level = occ[point, orbit] + occ[far_point, columns[place]]
        denominator = (level - col_ref[0]) - row_ref[0]
        real_part = (pair[:nv] / denominator).astype(BF16)
        imag_part = (pair[nv:] / denominator).astype(BF16)
        combined = jnp.concatenate(
            [
                jnp.concatenate([real_part, -imag_part], axis=1),
                jnp.concatenate([imag_part, real_part], axis=1),
            ],
            axis=0,
        )
        term = jnp.dot(combined, window.reshape(2 * nv, naux), preferred_element_type=F32)
        gradient = term if gradient is None else gradient + term
    out_ref[...] = gradient.reshape(out_ref.shape).astype(out_ref.dtype)


def contract(transfer, bit, scalars, rows, cols, factor, windows, base=None, result=None):
    _, kc, _, _, nv, naux = factor.shape
    final = base is not None
    places = [place for place, _ in windows]

    def own_at(k, *_):
        return (transfer, k, 0, 0, 0, 0)

    def slot_at(k, ids, partner, occ):
        far_group = jnp.bitwise_xor(ids[0], 1 << bit)
        return (partner[transfer, ids[0] * kc + k] - far_group * kc, 0, 0, 0, 0)

    own_block = (1, 1, 1, 2, nv, naux)
    term_block = (1, 2, nv, naux)
    term_spec = pl.BlockSpec(term_block, lambda k, *_: (k, 0, 0, 0))
    in_specs = [
        pl.BlockSpec((1, 1, nv), lambda k, ids, *_: (ids[0] * kc + k, 0, 0)),
        pl.BlockSpec((1, nv, 1), lambda k, ids, partner, _: (partner[transfer, ids[0] * kc + k], 0, 0)),
        pl.BlockSpec(own_block, own_at),
    ] + [pl.BlockSpec((1, 1, 2, nv, naux), slot_at)] * len(windows)
    operands = [rows, cols, factor] + [window for _, window in windows]
    aliases = {}
    if final:
        in_specs.append(term_spec)
        operands.append(base)
        out_shape = jax.ShapeDtypeStruct(factor.shape, BF16)
        out_spec = pl.BlockSpec(own_block, own_at)
        if result is not None:
            in_specs.append(pl.BlockSpec(memory_space=pl.ANY))
            aliases = {len(scalars) + len(operands): 0}
            operands.append(result)
    else:
        out_shape = jax.ShapeDtypeStruct((kc, 2, nv, naux), F32)
        out_spec = term_spec
    flops = kc * len(windows) * 16 * nv * nv * naux
    moved = kc * nv * naux * (4 * (1 + len(windows)) + (12 if final else 8))
    return pl.pallas_call(
        functools.partial(kernel, transfer, bit, kc, places, not final),
        out_shape=out_shape,
        grid_spec=pltpu.PrefetchScalarGridSpec(
            num_scalar_prefetch=len(scalars), grid=(kc,), in_specs=in_specs, out_specs=out_spec
        ),
        input_output_aliases=aliases,
        cost_estimate=pl.CostEstimate(flops=flops, bytes_accessed=moved, transcendentals=0),
        compiler_params=pltpu.CompilerParams(vmem_limit_bytes=24 * 1024 * 1024),
    )(*scalars, *operands)


def body(factor, partner, occ_energy, vir_sorted, vir_order):
    top_bit = lax.axis_size("kpt").bit_length() - 2
    ids = jnp.stack([lax.axis_index("kpt"), lax.axis_index("occ")]).astype(jnp.int32)
    scalars = (ids, partner, occ_energy)

    one, two = factor[0], factor[1]
    one_far_own = far_swap(one)
    one_swapped = group_swap(one, 0)
    two_swapped = group_swap(two, top_bit)
    one_far = group_swap(one_far_own, 0)
    two_far = far_swap(two_swapped)
    one_near = near_swap(one_swapped)
    two_near = near_swap(two_swapped)

    virtual = virtual_energies(vir_sorted, vir_order)
    rows, cols = virtual[:, None, :], virtual[:, :, None]
    call = functools.partial(contract, scalars=scalars, rows=rows, cols=cols, factor=factor)
    base_one = call(0, 0, windows=[("own", one_swapped), ("near", one_near)])
    base_two = call(1, top_bit, windows=[("own", two_swapped), ("near", two_near)])
    result = call(0, 0, windows=[("far", one_far)], base=base_one)
    return call(1, top_bit, windows=[("far", two_far)], base=base_two, result=result)


def solution(mesh):
    spec = P(None, "kpt", "occ", None, None, None)
    in_specs = (spec, P(), P(), P(), P())
    return jax.shard_map(body, mesh=mesh, in_specs=in_specs, out_specs=spec, check_vma=False)
```

```python
import functools

import jax
import jax.numpy as jnp
from jax import lax
from jax.experimental import pallas as pl
from jax.experimental.pallas import tpu as pltpu
from jax.sharding import PartitionSpec as P

F32 = jnp.float32
BF16 = jnp.bfloat16


def group_swap(block, bit):
    count = lax.axis_size("kpt")
    return lax.ppermute(block, "kpt", [(g, g ^ (1 << bit)) for g in range(count)])


def near_swap(block):
    count = lax.axis_size("occ")
    return lax.ppermute(block, "occ", [(i, i ^ 1) for i in range(count)])


def far_swap(block):
    count = lax.axis_size("occ")
    return lax.ppermute(
        block, "occ", [(i, (i + (1 if i % 2 else count - 1)) % count) for i in range(count)]
    )


def virtual_energies(vir_sorted, vir_order):
    ranks = jnp.arange(vir_sorted.shape[1], dtype=jnp.int32)
    matches = vir_order[:, :, None] == ranks[None, None, :]
    return jnp.sum(jnp.where(matches, vir_sorted[:, None, :], 0.0), axis=2)


def nt_dot(left, right):
    return lax.dot_general(left, right, (((1,), (1,)), ((), ())), preferred_element_type=F32)


def column_of(row):
    return jnp.transpose(jnp.broadcast_to(row, (8, row.shape[1])))[:, :1]


def kernel(transfer, bit, places, final, has_base, ids, partner, occ, virtual, factor, *refs):
    windows, rest = refs[: len(places)], refs[len(places) :]
    base = rest[0] if has_base else None
    _, kc, _, _, nv, naux = factor.shape
    total = occ.shape[1]
    group, orbit = ids[0], ids[1]
    far_group = jnp.bitwise_xor(group, 1 << bit)
    parity = lax.rem(orbit, 2)
    columns = {
        "own": orbit,
        "near": orbit + 1 - 2 * parity,
        "far": lax.rem(orbit + total - 1 + 2 * parity, total),
    }
    copies = []
    for k in range(kc):
        point = group * kc + k
        far_point = partner[transfer, point]
        slot = far_point - far_group * kc
        row = virtual[pl.ds(point, 1), :]
        column = column_of(virtual[pl.ds(far_point, 1), :])
        real, imag = factor[transfer, k, 0, 0], factor[transfer, k, 0, 1]
        left = jnp.concatenate([real, imag], axis=0)
        right = jnp.concatenate([imag, -real], axis=0)
        gradient = base[k].reshape(2 * nv, naux) if has_base else None
        for place, window_ref in zip(places, windows):
            window = window_ref[slot, 0]
            pair = nt_dot(left, window[0]) + nt_dot(right, window[1])
            level = occ[point, orbit] + occ[far_point, columns[place]]
            denominator = (level - column) - row
            real_part = (pair[:nv] / denominator).astype(BF16)
            imag_part = (pair[nv:] / denominator).astype(BF16)
            combined = jnp.concatenate(
                [
                    jnp.concatenate([real_part, -imag_part], axis=1),
                    jnp.concatenate([imag_part, real_part], axis=1),
                ],
                axis=0,
            )
            term = jnp.dot(combined, window.reshape(2 * nv, naux), preferred_element_type=F32)
            gradient = term if gradient is None else gradient + term
        gradient = gradient.reshape(2, nv, naux)
        if final:
            out, staged, sems = rest[-3:]
            staged[k] = gradient.astype(BF16)
            copy = pltpu.make_async_copy(staged.at[k], out.at[transfer, k, 0], sems.at[k])
            copy.start()
            copies.append(copy)
        else:
            rest[-1][k] = gradient
    for copy in copies:
        copy.wait()


def contract(transfer, bit, scalars, virtual, factor, windows, base=None, result=None, final=False):
    _, kc, _, _, nv, naux = factor.shape
    places = [place for place, _ in windows]
    vmem, smem = pl.BlockSpec(memory_space=pltpu.VMEM), pl.BlockSpec(memory_space=pltpu.SMEM)
    operands = [*scalars, virtual, factor] + [window for _, window in windows]
    in_specs = [smem] * len(scalars) + [vmem] * (2 + len(windows))
    aliases, scratch = {}, []
    if base is not None:
        in_specs.append(vmem)
        operands.append(base)
    if final:
        out_shape = jax.ShapeDtypeStruct(factor.shape, BF16)
        out_spec = pl.BlockSpec(memory_space=pl.ANY)
        scratch = [pltpu.VMEM((kc, 2, nv, naux), BF16), pltpu.SemaphoreType.DMA((kc,))]
        if result is not None:
            aliases = {len(operands): 0}
            in_specs.append(pl.BlockSpec(memory_space=pl.ANY))
            operands.append(result)
    else:
        out_shape = jax.ShapeDtypeStruct((kc, 2, nv, naux), F32)
        out_spec = vmem
        if base is not None:
            aliases = {len(operands) - 1: 0}
    flops = kc * len(windows) * 16 * nv * nv * naux
    moved = kc * nv * naux * (4 * (1 + len(windows)) + 8)
    return pl.pallas_call(
        functools.partial(kernel, transfer, bit, places, final, base is not None),
        out_shape=out_shape,
        in_specs=in_specs,
        out_specs=out_spec,
        scratch_shapes=scratch,
        input_output_aliases=aliases,
        cost_estimate=pl.CostEstimate(flops=flops, bytes_accessed=moved, transcendentals=0),
        compiler_params=pltpu.CompilerParams(vmem_limit_bytes=24 * 1024 * 1024),
    )(*operands)


def body(factor, partner, occ_energy, vir_sorted, vir_order):
    top_bit = lax.axis_size("kpt").bit_length() - 2
    ids = jnp.stack([lax.axis_index("kpt"), lax.axis_index("occ")]).astype(jnp.int32)
    scalars = (ids, partner, occ_energy)

    one, two = factor[0], factor[1]
    one_far_own = far_swap(one)
    one_swapped = group_swap(one, 0)
    two_swapped = group_swap(two, top_bit)
    one_far = group_swap(one_far_own, 0)
    two_far = far_swap(two_swapped)
    one_near = near_swap(one_swapped)
    two_near = near_swap(two_swapped)

    virtual = virtual_energies(vir_sorted, vir_order)
    call = functools.partial(contract, scalars=scalars, virtual=virtual, factor=factor)
    base_one = call(0, 0, windows=[("own", one_swapped), ("near", one_near)])
    base_two = call(1, top_bit, windows=[("own", two_swapped), ("near", two_near)])
    result = call(0, 0, windows=[("far", one_far)], base=base_one, final=True)
    return call(1, top_bit, windows=[("far", two_far)], base=base_two, result=result, final=True)


def solution(mesh):
    spec = P(None, "kpt", "occ", None, None, None)
    in_specs = (spec, P(), P(), P(), P())
    return jax.shard_map(body, mesh=mesh, in_specs=in_specs, out_specs=spec, check_vma=False)
```

```python
import functools

import jax
import jax.numpy as jnp
from jax import lax
from jax.experimental import pallas as pl
from jax.experimental.pallas import tpu as pltpu
from jax.sharding import PartitionSpec as P

F32 = jnp.float32
BF16 = jnp.bfloat16


def group_swap(block, bit):
    count = lax.axis_size("kpt")
    return lax.ppermute(block, "kpt", [(g, g ^ (1 << bit)) for g in range(count)])


def near_swap(block):
    count = lax.axis_size("occ")
    return lax.ppermute(block, "occ", [(i, i ^ 1) for i in range(count)])


def far_swap(block):
    count = lax.axis_size("occ")
    return lax.ppermute(
        block, "occ", [(i, (i + (1 if i % 2 else count - 1)) % count) for i in range(count)]
    )


def after(block, *others):
    return lax.optimization_barrier((block, *others))[0]


def virtual_energies(vir_sorted, vir_order):
    ranks = jnp.arange(vir_sorted.shape[1], dtype=jnp.int32)
    matches = vir_order[:, :, None] == ranks[None, None, :]
    return jnp.sum(jnp.where(matches, vir_sorted[:, None, :], 0.0), axis=2)


def column_of(row):
    return jnp.transpose(jnp.broadcast_to(row, (8, row.shape[1])))[:, :1]


def kernel(bits, units, final, has_base, ids, partner, occ, virtual, factor, *refs):
    windows, rest = refs[: len(units)], refs[len(units) :]
    base = rest[0] if has_base else None
    _, kc, _, _, nv, naux = factor.shape
    total = occ.shape[1]
    group, orbit = ids[0], ids[1]
    parity = lax.rem(orbit, 2)
    columns = {
        "own": orbit,
        "near": orbit + 1 - 2 * parity,
        "far": lax.rem(orbit + total - 1 + 2 * parity, total),
    }
    transfers = sorted({unit[0] for unit in units})

    def point_step(k, carry):
        point = group * kc + k
        for transfer in transfers:
            far_point = partner[transfer, point]
            slot = far_point - jnp.bitwise_xor(group, 1 << bits[transfer]) * kc
            row = virtual[pl.ds(point, 1), :]
            column = column_of(virtual[pl.ds(far_point, 1), :])
            left = factor[transfer, k, 0].reshape(2 * nv, naux)
            amplitudes, blocks = [], []
            for (at, place, start), window_ref in zip(units, windows):
                if at != transfer:
                    continue
                size = window_ref.shape[2]
                window = window_ref[slot].reshape(2 * size, naux)
                products = lax.dot_general(
                    left, window, (((1,), (1,)), ((), ())), preferred_element_type=F32
                )
                level = occ[point, orbit] + occ[far_point, columns[place]]
                inverse = 1.0 / ((level - column) - row[:, start : start + size])
                real_part = ((products[:nv, :size] + products[nv:, size:]) * inverse).astype(BF16)
                imag_part = ((products[nv:, :size] - products[:nv, size:]) * inverse).astype(BF16)
                amplitudes.append(
                    jnp.concatenate(
                        [
                            jnp.concatenate([real_part, -imag_part], axis=1),
                            jnp.concatenate([imag_part, real_part], axis=1),
                        ],
                        axis=0,
                    )
                )
                blocks.append(window)
            gradient = jnp.dot(
                jnp.concatenate(amplitudes, axis=1),
                jnp.concatenate(blocks, axis=0),
                preferred_element_type=F32,
            )
            gradient = gradient.reshape(2, nv, naux)
            if has_base:
                gradient = gradient + base[transfer, k]
            if final:
                out, staged, sems = rest[-3:]
                staged[k] = gradient.astype(BF16)
                pltpu.make_async_copy(staged.at[k], out.at[transfer, k, 0], sems.at[k]).start()
            else:
                rest[-1][transfer, k] = gradient
        return carry

    lax.fori_loop(0, kc, point_step, 0)
    if final:
        out, staged, sems = rest[-3:]
        for k in range(kc):
            pltpu.make_async_copy(staged.at[k], out.at[transfers[0], k, 0], sems.at[k]).wait()


def contract(bits, scalars, virtual, factor, terms, base=None, result=None, final=False):
    transfer_count, kc, _, _, nv, naux = factor.shape
    units = [term[:3] for term in terms]
    windows = [term[3] for term in terms]
    vmem, smem = pl.BlockSpec(memory_space=pltpu.VMEM), pl.BlockSpec(memory_space=pltpu.SMEM)
    operands = [*scalars, virtual, factor, *windows]
    in_specs = [smem] * len(scalars) + [vmem] * (2 + len(windows))
    aliases, scratch = {}, []
    if base is not None:
        in_specs.append(vmem)
        operands.append(base)
    if final:
        out_shape = jax.ShapeDtypeStruct(factor.shape, BF16)
        out_spec = pl.BlockSpec(memory_space=pl.ANY)
        scratch = [pltpu.VMEM((kc, 2, nv, naux), BF16), pltpu.SemaphoreType.DMA((kc,))]
        if result is not None:
            aliases = {len(operands): 0}
            in_specs.append(pl.BlockSpec(memory_space=pl.ANY))
            operands.append(result)
    else:
        out_shape = jax.ShapeDtypeStruct((transfer_count, kc, 2, nv, naux), F32)
        out_spec = vmem
        if base is not None:
            aliases = {len(operands) - 1: 0}
    size = sum(window.size for window in windows)
    return pl.pallas_call(
        functools.partial(kernel, bits, units, final, base is not None),
        out_shape=out_shape,
        in_specs=in_specs,
        out_specs=out_spec,
        scratch_shapes=scratch,
        input_output_aliases=aliases,
        cost_estimate=pl.CostEstimate(
            flops=8 * size * nv, bytes_accessed=2 * size + 4 * factor.size, transcendentals=0
        ),
        compiler_params=pltpu.CompilerParams(vmem_limit_bytes=24 * 1024 * 1024),
    )(*operands)


def body(factor, partner, occ_energy, vir_sorted, vir_order):
    bits = (0, lax.axis_size("kpt").bit_length() - 2)
    half = factor.shape[4] // 2
    ids = jnp.stack([lax.axis_index("kpt"), lax.axis_index("occ")]).astype(jnp.int32)
    scalars = (ids, partner, occ_energy)

    a = [factor[t, :, 0, :, :half] for t in range(2)]
    b = [factor[t, :, 0, :, half:] for t in range(2)]
    a_beside = [far_swap(a[t]) for t in range(2)]
    b_own = [group_swap(b[t], bits[t]) for t in range(2)]
    b_far = [far_swap(b_own[t]) for t in range(2)]
    a_own = [group_swap(after(a[t], b_own[t]), bits[t]) for t in range(2)]
    b_near = [near_swap(b_own[t]) for t in range(2)]
    a_near = [near_swap(a_own[t]) for t in range(2)]
    a_far = [group_swap(after(a_beside[t], a_own[t]), bits[t]) for t in range(2)]

    virtual = virtual_energies(vir_sorted, vir_order)
    call = functools.partial(contract, bits, scalars, virtual, factor)

    def terms(place, start, windows):
        return [(t, place, start, windows[t]) for t in range(2)]

    total = call(terms("own", half, b_own) + terms("near", half, b_near))
    total = call(terms("own", 0, a_own) + terms("near", 0, a_near), base=total)
    total = call(terms("far", 0, a_far), base=total)
    last = terms("far", half, b_far)
    result = call(last[:1], base=total, final=True)
    return call(last[1:], base=total, result=result, final=True)


def solution(mesh):
    spec = P(None, "kpt", "occ", None, None, None)
    in_specs = (spec, P(), P(), P(), P())
    return jax.shard_map(body, mesh=mesh, in_specs=in_specs, out_specs=spec, check_vma=False)
```

```python
import functools

import jax
import jax.numpy as jnp
from jax import lax
from jax.experimental import pallas as pl
from jax.experimental.pallas import tpu as pltpu
from jax.sharding import PartitionSpec as P

F32 = jnp.float32
BF16 = jnp.bfloat16
ANY = pl.BlockSpec(memory_space=pl.ANY)
VMEM = pl.BlockSpec(memory_space=pltpu.VMEM)
SMEM = pl.BlockSpec(memory_space=pltpu.SMEM)
PARAMS = pltpu.CompilerParams(vmem_limit_bytes=20 * 1024 * 1024)
COST = pl.CostEstimate(flops=0, bytes_accessed=0, transcendentals=0)


def group_swap(block, bit):
    count = lax.axis_size("kpt")
    return lax.ppermute(block, "kpt", [(g, g ^ (1 << bit)) for g in range(count)])


def near_swap(block):
    count = lax.axis_size("occ")
    return lax.ppermute(block, "occ", [(i, i ^ 1) for i in range(count)])


def far_swap(block):
    count = lax.axis_size("occ")
    return lax.ppermute(
        block, "occ", [(i, (i + (1 if i % 2 else count - 1)) % count) for i in range(count)]
    )


def virtual_energies(vir_sorted, vir_order):
    ranks = jnp.arange(vir_sorted.shape[1], dtype=jnp.int32)
    matches = vir_order[:, :, None] == ranks[None, None, :]
    return jnp.sum(jnp.where(matches, vir_sorted[:, None, :], 0.0), axis=2)


def column_of(row):
    return jnp.transpose(jnp.broadcast_to(row, (8, row.shape[1])))[:, :1]


def pack_kernel(bits, early, partner, factor, *refs):
    *wholes, part, sems = refs
    half = part.shape[2]
    kc = factor.shape[1]
    group = lax.axis_index("kpt")
    copies = []
    for transfer, bit in enumerate(bits):
        far_group = jnp.bitwise_xor(group, 1 << bit)
        slots = [partner[transfer, far_group * kc + k] - group * kc for k in range(kc)]
        for at, (t, k, h) in enumerate(early):
            if t == transfer:
                source = factor.at[transfer, slots[k], 0, :, pl.ds(h * half, half), :]
                copies.append((source, part.at[at]))
        for k in range(kc):
            copies.append((factor.at[transfer, slots[k], 0], wholes[transfer].at[k]))
    copies = [
        pltpu.make_async_copy(source, target, sems.at[at])
        for at, (source, target) in enumerate(copies)
    ]
    for copy in copies:
        copy.start()
    for copy in copies:
        copy.wait()


def pack(bits, early, partner, factor):
    _, kc, _, parts, nv, naux = factor.shape
    shapes = [(kc, parts, nv, naux)] * len(bits)
    shapes.append((len(early), parts, nv // 2, naux))
    copies = len(early) + kc * len(bits)
    return pl.pallas_call(
        functools.partial(pack_kernel, bits, early),
        out_shape=[jax.ShapeDtypeStruct(shape, BF16) for shape in shapes],
        in_specs=[SMEM, ANY],
        out_specs=[VMEM] * len(shapes),
        scratch_shapes=[pltpu.SemaphoreType.DMA((copies,))],
        cost_estimate=COST,
        compiler_params=PARAMS,
    )(partner, factor)


def inverse_kernel(bits, partner, occ, virtual, out):
    _, _, kc, nv, _ = out.shape
    total = occ.shape[1]
    group, orbit = lax.axis_index("kpt"), lax.axis_index("occ")
    parity = lax.rem(orbit, 2)
    columns = (orbit, orbit + 1 - 2 * parity, lax.rem(orbit + total - 1 + 2 * parity, total))

    def point_step(k, carry):
        point = group * kc + k
        row = virtual[pl.ds(point, 1), :]
        for transfer in range(len(bits)):
            far_point = partner[transfer, point]
            column = column_of(virtual[pl.ds(far_point, 1), :])
            for place, index in enumerate(columns):
                level = occ[point, orbit] + occ[far_point, index]
                out[transfer, place, k] = 1.0 / ((level - column) - row)
        return carry

    lax.fori_loop(0, kc, point_step, 0)


def inverses(bits, partner, occ_energy, virtual, kc):
    nv = virtual.shape[1]
    return pl.pallas_call(
        functools.partial(inverse_kernel, bits),
        out_shape=jax.ShapeDtypeStruct((len(bits), 3, kc, nv, nv), F32),
        in_specs=[SMEM, SMEM, VMEM],
        out_specs=VMEM,
        cost_estimate=COST,
        compiler_params=PARAMS,
    )(partner, occ_energy, virtual)


def gradient_sum(own, terms, base):
    _, nv, naux = own.shape
    left = own.reshape(2 * nv, naux)
    amplitudes, blocks = [], []
    for window, inverse in terms:
        size = window.shape[1]
        window = window.reshape(2 * size, naux)
        products = lax.dot_general(
            left, window, (((1,), (1,)), ((), ())), preferred_element_type=F32
        )
        real_part = ((products[:nv, :size] + products[nv:, size:]) * inverse).astype(BF16)
        imag_part = ((products[nv:, :size] - products[:nv, size:]) * inverse).astype(BF16)
        upper = jnp.concatenate([real_part, -imag_part], axis=1)
        lower = jnp.concatenate([imag_part, real_part], axis=1)
        amplitudes.append(jnp.concatenate([upper, lower], axis=0))
        blocks.append(window)
    gradient = jnp.dot(
        jnp.concatenate(amplitudes, axis=1),
        jnp.concatenate(blocks, axis=0),
        preferred_element_type=F32,
    ).reshape(2, nv, naux)
    return gradient if base is None else gradient + base


def first_kernel(transfers, factor, inverse, *refs):
    owns, nears, out = refs[:transfers], refs[transfers:-1], refs[-1]

    def point_step(k, carry):
        for t in range(transfers):
            terms = [(owns[t][k], inverse[t, 0, k]), (nears[t][k], inverse[t, 1, k])]
            out[t, k] = gradient_sum(factor[t, k, 0], terms, None)
        return carry

    lax.fori_loop(0, factor.shape[1], point_step, 0)


def first_terms(factor, inverse, owns, nears):
    transfers, kc, _, parts, nv, naux = factor.shape
    operands = [factor, inverse, *owns, *nears]
    return pl.pallas_call(
        functools.partial(first_kernel, transfers),
        out_shape=jax.ShapeDtypeStruct((transfers, kc, parts, nv, naux), F32),
        in_specs=[VMEM] * len(operands),
        out_specs=VMEM,
        cost_estimate=COST,
        compiler_params=PARAMS,
    )(*operands)


def far_kernel(sources, ends, keep, has_result, factor, inverse, *refs):
    count = len(sources)
    windows, total = refs[:count], refs[count]
    kept = refs[count + 1 + has_result] if keep else None
    half = windows[0].shape[2]
    out, staged, sems = refs[-3:]
    copies = []
    for t in range(factor.shape[0]):
        for k in range(factor.shape[1]):
            terms = [
                (window[at], inverse[t, 2, k, :, unit[2] * half : (unit[2] + 1) * half])
                for window, units in zip(windows, sources)
                for at, unit in enumerate(units)
                if unit[:2] == (t, k)
            ]
            if not terms:
                continue
            gradient = gradient_sum(factor[t, k, 0], terms, total[t, k])
            if (t, k) in ends:
                at = len(copies)
                staged[at] = gradient.astype(BF16)
                copy = pltpu.make_async_copy(staged.at[at], out.at[t, k, 0], sems.at[at])
                copy.start()
                copies.append(copy)
            else:
                kept[t, k] = gradient
    for copy in copies:
        copy.wait()


def far_terms(sources, ends, keep, factor, inverse, windows, total, result=None):
    _, _, _, parts, nv, naux = factor.shape
    operands = [factor, inverse, *windows, total]
    in_specs = [VMEM] * len(operands)
    aliases = {}
    if keep:
        aliases[len(operands) - 1] = 0
    if result is not None:
        aliases[len(operands)] = int(keep)
        operands.append(result)
        in_specs.append(ANY)
    out_shape = [jax.ShapeDtypeStruct(factor.shape, BF16)]
    out_specs = [ANY]
    if keep:
        out_shape.insert(0, jax.ShapeDtypeStruct(total.shape, F32))
        out_specs.insert(0, VMEM)
    return pl.pallas_call(
        functools.partial(far_kernel, sources, ends, keep, result is not None),
        out_shape=out_shape,
        in_specs=in_specs,
        out_specs=out_specs,
        scratch_shapes=[
            pltpu.VMEM((len(ends), parts, nv, naux), BF16),
            pltpu.SemaphoreType.DMA((len(ends),)),
        ],
        input_output_aliases=aliases,
        cost_estimate=COST,
        compiler_params=PARAMS,
    )(*operands)


def body(factor, partner, occ_energy, vir_sorted, vir_order):
    transfers, kc = factor.shape[:2]
    half = factor.shape[4] // 2
    bits = (0, lax.axis_size("kpt").bit_length() - 2)
    order = [[(t, k, h) for h in range(2) for k in range(kc)] for t in range(transfers)]
    cuts = [kc + kc // 2, kc]
    early = [order[t][: cuts[t]] for t in range(transfers)]
    late = order[0][cuts[0] :] + order[1][cuts[1] :]
    late_ends = {unit[:2] for unit in late}
    early_ends = {unit[:2] for unit in order[0] + order[1]} - late_ends

    *wholes, part = pack(bits, early[0] + early[1], partner, factor)
    beside = far_swap(part)
    owns = [group_swap(wholes[t], bits[t]) for t in range(transfers)]
    late_block = jnp.concatenate(
        [owns[0][cuts[0] - kc :, :, half:], owns[1][cuts[1] - kc :, :, half:]]
    )
    late_window = far_swap(late_block)
    beside, _ = lax.optimization_barrier((beside, late_block))
    nears = [near_swap(owns[t]) for t in range(transfers)]
    early_windows = [
        group_swap(beside[: cuts[0]], bits[0]),
        group_swap(beside[cuts[0] :], bits[1]),
    ]

    virtual = virtual_energies(vir_sorted, vir_order)
    inverse = inverses(bits, partner, occ_energy, virtual, kc)
    total = first_terms(factor, inverse, owns, nears)
    total, result = far_terms(early, early_ends, True, factor, inverse, early_windows, total)
    (result,) = far_terms([late], late_ends, False, factor, inverse, [late_window], total, result)
    return result


def solution(mesh):
    spec = P(None, "kpt", "occ", None, None, None)
    in_specs = (spec, P(), P(), P(), P())
    return jax.shard_map(body, mesh=mesh, in_specs=in_specs, out_specs=spec, check_vma=False)
```

```python
import functools

import jax
import jax.numpy as jnp
from jax import lax
from jax.experimental import pallas as pl
from jax.experimental.pallas import tpu as pltpu
from jax.sharding import PartitionSpec as P

F32 = jnp.float32
BF16 = jnp.bfloat16
ANY = pl.BlockSpec(memory_space=pl.ANY)
VMEM = pl.BlockSpec(memory_space=pltpu.VMEM)
SMEM = pl.BlockSpec(memory_space=pltpu.SMEM)
PARAMS = pltpu.CompilerParams(vmem_limit_bytes=20 * 1024 * 1024)
COST = pl.CostEstimate(flops=0, bytes_accessed=0, transcendentals=0)


def group_swap(block, bit):
    count = lax.axis_size("kpt")
    return lax.ppermute(block, "kpt", [(g, g ^ (1 << bit)) for g in range(count)])


def near_swap(block):
    count = lax.axis_size("occ")
    return lax.ppermute(block, "occ", [(i, i ^ 1) for i in range(count)])


def far_swap(block):
    count = lax.axis_size("occ")
    return lax.ppermute(
        block, "occ", [(i, (i + (1 if i % 2 else count - 1)) % count) for i in range(count)]
    )


def virtual_energies(vir_sorted, vir_order):
    ranks = jnp.arange(vir_sorted.shape[1], dtype=jnp.int32)
    matches = vir_order[:, :, None] == ranks[None, None, :]
    return jnp.sum(jnp.where(matches, vir_sorted[:, None, :], 0.0), axis=2)


def column_of(row):
    return jnp.transpose(jnp.broadcast_to(row, (8, row.shape[1])))[:, :1]


def pack_kernel(bits, partner, factor, early, *refs):
    lates, sems = refs[:-1], refs[-1]
    kc, half = factor.shape[1], early.shape[2]
    group = lax.axis_index("kpt")
    copies = []
    for transfer, bit in enumerate(bits):
        far_group = jnp.bitwise_xor(group, 1 << bit)
        for k in range(kc):
            slot = partner[transfer, far_group * kc + k] - group * kc
            block = factor.at[transfer, slot, 0]
            targets = (early.at[transfer * kc + k], lates[transfer].at[k])
            for h, target in enumerate(targets):
                source = block.at[:, pl.ds(h * half, half), :]
                copies.append(pltpu.make_async_copy(source, target, sems.at[len(copies)]))
                copies[-1].start()
    for copy in copies:
        copy.wait()


def pack(bits, partner, factor):
    transfers, kc, _, parts, nv, naux = factor.shape
    counts = [transfers * kc] + [kc] * transfers
    return pl.pallas_call(
        functools.partial(pack_kernel, bits),
        out_shape=[jax.ShapeDtypeStruct((n, parts, nv // 2, naux), BF16) for n in counts],
        in_specs=[SMEM, ANY],
        out_specs=[VMEM] * len(counts),
        scratch_shapes=[pltpu.SemaphoreType.DMA((2 * transfers * kc,))],
        cost_estimate=COST,
        compiler_params=PARAMS,
    )(
        pltpu.with_memory_space_constraint(partner, pltpu.HBM),
        pltpu.with_memory_space_constraint(factor, pltpu.HBM),
    )


def inverse_kernel(bits, partner, occ, virtual, out):
    _, _, kc, nv, _ = out.shape
    total = occ.shape[1]
    group, orbit = lax.axis_index("kpt"), lax.axis_index("occ")
    parity = lax.rem(orbit, 2)
    columns = (orbit, orbit + 1 - 2 * parity, lax.rem(orbit + total - 1 + 2 * parity, total))

    def point_step(k, carry):
        point = group * kc + k
        row = virtual[pl.ds(point, 1), :]
        for transfer in range(len(bits)):
            far_point = partner[transfer, point]
            column = column_of(virtual[pl.ds(far_point, 1), :])
            for place, index in enumerate(columns):
                level = occ[point, orbit] + occ[far_point, index]
                out[transfer, place, k] = 1.0 / ((level - column) - row)
        return carry

    lax.fori_loop(0, kc, point_step, 0)


def inverses(bits, partner, occ_energy, virtual, kc):
    nv = virtual.shape[1]
    return pl.pallas_call(
        functools.partial(inverse_kernel, bits),
        out_shape=jax.ShapeDtypeStruct((len(bits), 3, kc, nv, nv), F32),
        in_specs=[SMEM, SMEM, VMEM],
        out_specs=VMEM,
        cost_estimate=COST,
        compiler_params=PARAMS,
    )(partner, occ_energy, virtual)


def gradient_sum(own, terms, base):
    _, nv, naux = own.shape
    left = own.reshape(2 * nv, naux)
    amplitudes, blocks = [], []
    for window, inverse in terms:
        size = window.shape[1]
        window = window.reshape(2 * size, naux)
        products = lax.dot_general(
            left, window, (((1,), (1,)), ((), ())), preferred_element_type=F32
        )
        real_part = ((products[:nv, :size] + products[nv:, size:]) * inverse).astype(BF16)
        imag_part = ((products[nv:, :size] - products[:nv, size:]) * inverse).astype(BF16)
        upper = jnp.concatenate([real_part, -imag_part], axis=1)
        lower = jnp.concatenate([imag_part, real_part], axis=1)
        amplitudes.append(jnp.concatenate([upper, lower], axis=0))
        blocks.append(window)
    gradient = jnp.dot(
        jnp.concatenate(amplitudes, axis=1),
        jnp.concatenate(blocks, axis=0),
        preferred_element_type=F32,
    ).reshape(2, nv, naux)
    return gradient if base is None else gradient + base


def half_of(h, half):
    return slice(h * half, (h + 1) * half)


def first_kernel(factor, inverse, *refs):
    transfers, kc = factor.shape[:2]
    owns, nears, out = refs[: 2 * transfers], refs[2 * transfers : -1], refs[-1]
    half = nears[0].shape[2]

    def point_step(k, carry):
        for t in range(transfers):
            terms = []
            for h in range(2):
                rows = half_of(h, half)
                terms.append((owns[h * transfers + t][k], inverse[t, 0, k, :, rows]))
                terms.append((nears[h][t * kc + k], inverse[t, 1, k, :, rows]))
            out[t, k] = gradient_sum(factor[t, k, 0], terms, None)
        return carry

    lax.fori_loop(0, kc, point_step, 0)


def first_terms(factor, inverse, owns, nears):
    transfers, kc, _, parts, nv, naux = factor.shape
    operands = [factor, inverse, *owns, *nears]
    return pl.pallas_call(
        first_kernel,
        out_shape=jax.ShapeDtypeStruct((transfers, kc, parts, nv, naux), F32),
        in_specs=[VMEM] * len(operands),
        out_specs=VMEM,
        cost_estimate=COST,
        compiler_params=PARAMS,
    )(*operands)


def early_kernel(factor, inverse, *refs):
    windows, total, out = refs[:-2], refs[-2], refs[-1]
    half = windows[0].shape[2]

    def point_step(k, carry):
        for t, window in enumerate(windows):
            terms = [(window[k], inverse[t, 2, k, :, half_of(0, half)])]
            out[t, k] = gradient_sum(factor[t, k, 0], terms, total[t, k])
        return carry

    lax.fori_loop(0, factor.shape[1], point_step, 0)


def early_terms(factor, inverse, windows, total):
    operands = [factor, inverse, *windows, total]
    return pl.pallas_call(
        early_kernel,
        out_shape=jax.ShapeDtypeStruct(total.shape, F32),
        in_specs=[VMEM] * len(operands),
        out_specs=VMEM,
        input_output_aliases={len(operands) - 1: 0},
        cost_estimate=COST,
        compiler_params=PARAMS,
    )(*operands)


def last_kernel(factor, inverse, window, total, out, staged, sems):
    transfers, kc = factor.shape[:2]
    half = window.shape[2]
    copies = []
    for t in range(transfers):
        for k in range(kc):
            at = t * kc + k
            terms = [(window[at], inverse[t, 2, k, :, half_of(1, half)])]
            staged[at] = gradient_sum(factor[t, k, 0], terms, total[t, k]).astype(BF16)
            copies.append(pltpu.make_async_copy(staged.at[at], out.at[t, k, 0], sems.at[at]))
            copies[-1].start()
    for copy in copies:
        copy.wait()


def last_terms(factor, inverse, window, total):
    count = window.shape[0]
    _, _, _, parts, nv, naux = factor.shape
    return pl.pallas_call(
        last_kernel,
        out_shape=jax.ShapeDtypeStruct(factor.shape, BF16),
        in_specs=[VMEM] * 4,
        out_specs=ANY,
        scratch_shapes=[
            pltpu.VMEM((count, parts, nv, naux), BF16),
            pltpu.SemaphoreType.DMA((count,)),
        ],
        cost_estimate=COST,
        compiler_params=PARAMS,
    )(factor, inverse, window, total)


def body(factor, partner, occ_energy, vir_sorted, vir_order):
    transfers, kc = factor.shape[:2]
    bits = (0, lax.axis_size("kpt").bit_length() - 2)

    part, *lates = pack(bits, partner, factor)
    beside = far_swap(part)
    late_own = [group_swap(lates[t], bits[t]) for t in range(transfers)]
    early_own = [group_swap(part[t * kc : (t + 1) * kc], bits[t]) for t in range(transfers)]
    late_block = jnp.concatenate(late_own)
    late_far = far_swap(late_block)
    late_near = near_swap(late_block)
    early_near = near_swap(jnp.concatenate(lax.optimization_barrier((*early_own, late_block))[:-1]))
    early_far = [group_swap(beside[t * kc : (t + 1) * kc], bits[t]) for t in range(transfers)]

    virtual = virtual_energies(vir_sorted, vir_order)
    inverse = inverses(bits, partner, occ_energy, virtual, kc)
    total = first_terms(factor, inverse, early_own + late_own, [early_near, late_near])
    total = early_terms(factor, inverse, early_far, total)
    return last_terms(factor, inverse, late_far, total)


def solution(mesh):
    spec = P(None, "kpt", "occ", None, None, None)
    in_specs = (spec, P(), P(), P(), P())
    return jax.shard_map(body, mesh=mesh, in_specs=in_specs, out_specs=spec, check_vma=False)
```

```python
import functools

import jax
import jax.numpy as jnp
from jax import lax
from jax.experimental import pallas as pl
from jax.experimental.pallas import tpu as pltpu
from jax.sharding import PartitionSpec as P

F32 = jnp.float32
BF16 = jnp.bfloat16
ANY = pl.BlockSpec(memory_space=pl.ANY)
VMEM = pl.BlockSpec(memory_space=pltpu.VMEM)
SMEM = pl.BlockSpec(memory_space=pltpu.SMEM)
PARAMS = pltpu.CompilerParams(vmem_limit_bytes=20 * 1024 * 1024)
WORK = 16
COST = pl.CostEstimate(flops=0, bytes_accessed=0, transcendentals=0)


def group_swap(block, bit):
    count = lax.axis_size("kpt")
    return lax.ppermute(block, "kpt", [(g, g ^ (1 << bit)) for g in range(count)])


def near_swap(block):
    count = lax.axis_size("occ")
    return lax.ppermute(block, "occ", [(i, i ^ 1) for i in range(count)])


def far_swap(block):
    count = lax.axis_size("occ")
    return lax.ppermute(
        block, "occ", [(i, (i + (1 if i % 2 else count - 1)) % count) for i in range(count)]
    )


def after(block, *others):
    return lax.optimization_barrier((block, *others))[0]


def virtual_energies(vir_sorted, vir_order):
    ranks = jnp.arange(vir_sorted.shape[1], dtype=jnp.int32)
    matches = vir_order[:, :, None] == ranks[None, None, :]
    return jnp.sum(jnp.where(matches, vir_sorted[:, None, :], 0.0), axis=2)


def column_of(row):
    return jnp.transpose(jnp.broadcast_to(row, (8, row.shape[1])))[:, :1]


def pack_kernel(bits, h, partner, factor, *refs):
    outs, sems = refs[:-1], refs[-1]
    kc, half = factor.shape[1], outs[0].shape[2]
    targets = [out.at[n] for out in outs for n in range(out.shape[0])]
    group = lax.axis_index("kpt")
    copies = []
    for transfer, bit in enumerate(bits):
        far_group = jnp.bitwise_xor(group, 1 << bit)
        for k in range(kc):
            slot = partner[transfer, far_group * kc + k] - group * kc
            source = factor.at[transfer, slot, 0, :, pl.ds(h * half, half), :]
            at = transfer * kc + k
            copies.append(pltpu.make_async_copy(source, targets[at], sems.at[at]))
            copies[-1].start()
    for copy in copies:
        copy.wait()


def pack(bits, h, counts, partner, factor, work):
    _, _, _, parts, nv, naux = factor.shape
    return pl.pallas_call(
        functools.partial(pack_kernel, bits, h),
        out_shape=[jax.ShapeDtypeStruct((n, parts, nv // 2, naux), BF16) for n in counts],
        in_specs=[SMEM, ANY],
        out_specs=[VMEM] * len(counts),
        scratch_shapes=[pltpu.SemaphoreType.DMA((sum(counts),))],
        cost_estimate=pl.CostEstimate(flops=0, bytes_accessed=work, transcendentals=0),
        compiler_params=PARAMS,
    )(
        pltpu.with_memory_space_constraint(partner, pltpu.HBM),
        pltpu.with_memory_space_constraint(factor, pltpu.HBM),
    )


def inverse_kernel(bits, partner, occ, virtual, out):
    _, _, kc, nv, _ = out.shape
    total = occ.shape[1]
    group, orbit = lax.axis_index("kpt"), lax.axis_index("occ")
    parity = lax.rem(orbit, 2)
    columns = (orbit, orbit + 1 - 2 * parity, lax.rem(orbit + total - 1 + 2 * parity, total))

    def point_step(k, carry):
        point = group * kc + k
        row = virtual[pl.ds(point, 1), :]
        for transfer in range(len(bits)):
            far_point = partner[transfer, point]
            column = column_of(virtual[pl.ds(far_point, 1), :])
            for place, index in enumerate(columns):
                level = occ[point, orbit] + occ[far_point, index]
                out[transfer, place, k] = 1.0 / ((level - column) - row)
        return carry

    lax.fori_loop(0, kc, point_step, 0)


def inverses(bits, partner, occ_energy, virtual, kc):
    nv = virtual.shape[1]
    return pl.pallas_call(
        functools.partial(inverse_kernel, bits),
        out_shape=jax.ShapeDtypeStruct((len(bits), 3, kc, nv, nv), F32),
        in_specs=[SMEM, SMEM, VMEM],
        out_specs=VMEM,
        cost_estimate=COST,
        compiler_params=PARAMS,
    )(partner, occ_energy, virtual)


def gradient_sum(own, terms, base):
    _, nv, naux = own.shape
    left = own.reshape(2 * nv, naux)
    amplitudes, blocks = [], []
    for window, inverse in terms:
        size = window.shape[1]
        window = window.reshape(2 * size, naux)
        products = lax.dot_general(
            left, window, (((1,), (1,)), ((), ())), preferred_element_type=F32
        )
        real_part = ((products[:nv, :size] + products[nv:, size:]) * inverse).astype(BF16)
        imag_part = ((products[nv:, :size] - products[:nv, size:]) * inverse).astype(BF16)
        upper = jnp.concatenate([real_part, -imag_part], axis=1)
        lower = jnp.concatenate([imag_part, real_part], axis=1)
        amplitudes.append(jnp.concatenate([upper, lower], axis=0))
        blocks.append(window)
    gradient = jnp.dot(
        jnp.concatenate(amplitudes, axis=1),
        jnp.concatenate(blocks, axis=0),
        preferred_element_type=F32,
    ).reshape(2, nv, naux)
    return gradient if base is None else gradient + base


def half_of(h, half):
    return slice(h * half, (h + 1) * half)


def first_kernel(factor, inverse, *refs):
    transfers, kc = factor.shape[:2]
    owns, near, out = refs[: 2 * transfers], refs[-2], refs[-1]
    half = near.shape[2]

    def point_step(k, carry):
        for t in range(transfers):
            first, second = half_of(0, half), half_of(1, half)
            terms = [
                (owns[t][k], inverse[t, 0, k, :, first]),
                (owns[transfers + t][k], inverse[t, 0, k, :, second]),
                (near[t * kc + k], inverse[t, 1, k, :, first]),
            ]
            out[t, k] = gradient_sum(factor[t, k, 0], terms, None)
        return carry

    lax.fori_loop(0, kc, point_step, 0)


def first_terms(factor, inverse, owns, near):
    transfers, kc, _, parts, nv, naux = factor.shape
    operands = [factor, inverse, *owns, near]
    return pl.pallas_call(
        first_kernel,
        out_shape=jax.ShapeDtypeStruct((transfers, kc, parts, nv, naux), F32),
        in_specs=[VMEM] * len(operands),
        out_specs=VMEM,
        cost_estimate=COST,
        compiler_params=PARAMS,
    )(*operands)


def second_kernel(factor, inverse, near, *refs):
    fars, total, out = refs[:-2], refs[-2], refs[-1]
    kc, half = factor.shape[1], near.shape[2]

    def point_step(k, carry):
        for t, far in enumerate(fars):
            terms = [
                (near[t * kc + k], inverse[t, 1, k, :, half_of(1, half)]),
                (far[k], inverse[t, 2, k, :, half_of(0, half)]),
            ]
            out[t, k] = gradient_sum(factor[t, k, 0], terms, total[t, k])
        return carry

    lax.fori_loop(0, kc, point_step, 0)


def second_terms(factor, inverse, near, fars, total):
    operands = [factor, inverse, near, *fars, total]
    return pl.pallas_call(
        second_kernel,
        out_shape=jax.ShapeDtypeStruct(total.shape, F32),
        in_specs=[VMEM] * len(operands),
        out_specs=VMEM,
        input_output_aliases={len(operands) - 1: 0},
        cost_estimate=COST,
        compiler_params=PARAMS,
    )(*operands)


def last_kernel(factor, inverse, window, total, out, staged, sems):
    transfers, kc = factor.shape[:2]
    half = window.shape[2]
    copies = []
    for t in range(transfers):
        for k in range(kc):
            at = t * kc + k
            terms = [(window[at], inverse[t, 2, k, :, half_of(1, half)])]
            staged[at] = gradient_sum(factor[t, k, 0], terms, total[t, k]).astype(BF16)
            copies.append(pltpu.make_async_copy(staged.at[at], out.at[t, k, 0], sems.at[at]))
            copies[-1].start()
    for copy in copies:
        copy.wait()


def last_terms(factor, inverse, window, total):
    count = window.shape[0]
    _, _, _, parts, nv, naux = factor.shape
    return pl.pallas_call(
        last_kernel,
        out_shape=jax.ShapeDtypeStruct(factor.shape, BF16),
        in_specs=[VMEM] * 4,
        out_specs=ANY,
        scratch_shapes=[
            pltpu.VMEM((count, parts, nv, naux), BF16),
            pltpu.SemaphoreType.DMA((count,)),
        ],
        cost_estimate=COST,
        compiler_params=PARAMS,
    )(factor, inverse, window, total)


def body(factor, partner, occ_energy, vir_sorted, vir_order):
    transfers, kc = factor.shape[:2]
    bits = (0, lax.axis_size("kpt").bit_length() - 2)

    (part,) = pack(bits, 0, [transfers * kc], partner, factor, 0)
    beside = far_swap(part)
    lates = pack(bits, 1, [kc] * transfers, after(partner, part), factor, WORK * factor.size)
    late_own = [group_swap(lates[t], bits[t]) for t in range(transfers)]
    early_own = [group_swap(part[t * kc : (t + 1) * kc], bits[t]) for t in range(transfers)]
    late_block = jnp.concatenate(late_own)
    late_far = far_swap(late_block)
    late_near = near_swap(late_block)
    early_block = jnp.concatenate(early_own)
    early_near = jnp.concatenate(
        [near_swap(after(early_block[:-1], beside)), near_swap(early_block[-1:])]
    )
    early_far = [group_swap(beside[t * kc : (t + 1) * kc], bits[t]) for t in range(transfers)]

    virtual = virtual_energies(vir_sorted, vir_order)
    inverse = inverses(bits, partner, occ_energy, virtual, kc)
    total = first_terms(factor, inverse, early_own + late_own, early_near)
    total = second_terms(factor, inverse, late_near, early_far, total)
    return last_terms(factor, inverse, late_far, total)


def solution(mesh):
    spec = P(None, "kpt", "occ", None, None, None)
    in_specs = (spec, P(), P(), P(), P())
    return jax.shard_map(body, mesh=mesh, in_specs=in_specs, out_specs=spec, check_vma=False)
```

```python
import functools

import jax
import jax.numpy as jnp
from jax import lax
from jax.experimental import pallas as pl
from jax.experimental.pallas import tpu as pltpu
from jax.sharding import PartitionSpec as P

F32 = jnp.float32
BF16 = jnp.bfloat16
ANY = pl.BlockSpec(memory_space=pl.ANY)
VMEM = pl.BlockSpec(memory_space=pltpu.VMEM)
SMEM = pl.BlockSpec(memory_space=pltpu.SMEM)
PARAMS = pltpu.CompilerParams(vmem_limit_bytes=20 * 1024 * 1024)
WORK = 16
COST = pl.CostEstimate(flops=0, bytes_accessed=0, transcendentals=0)


def group_swap(block, bit):
    count = lax.axis_size("kpt")
    return lax.ppermute(block, "kpt", [(g, g ^ (1 << bit)) for g in range(count)])


def near_swap(block):
    count = lax.axis_size("occ")
    return lax.ppermute(block, "occ", [(i, i ^ 1) for i in range(count)])


def far_swap(block):
    count = lax.axis_size("occ")
    return lax.ppermute(
        block, "occ", [(i, (i + (1 if i % 2 else count - 1)) % count) for i in range(count)]
    )


def after(block, *others):
    return lax.optimization_barrier((block, *others))[0]


def virtual_energies(vir_sorted, vir_order):
    ranks = jnp.arange(vir_sorted.shape[1], dtype=jnp.int32)
    matches = vir_order[:, :, None] == ranks[None, None, :]
    return jnp.sum(jnp.where(matches, vir_sorted[:, None, :], 0.0), axis=2)


def column_of(row):
    return jnp.transpose(jnp.broadcast_to(row, (8, row.shape[1])))[:, :1]


def lay_kernel(factor, out, sems):
    kc, half = factor.shape[1], out.shape[2]
    copies = []
    for at in range(out.shape[0]):
        source = factor.at[at // kc, at % kc, 0, :, pl.ds(0, half), :]
        copies.append(pltpu.make_async_copy(source, out.at[at], sems.at[at]))
        copies[-1].start()
    for copy in copies:
        copy.wait()


def lay(factor):
    transfers, kc, _, parts, nv, naux = factor.shape
    return pl.pallas_call(
        lay_kernel,
        out_shape=jax.ShapeDtypeStruct((transfers * kc, parts, nv // 2, naux), BF16),
        in_specs=[ANY],
        out_specs=VMEM,
        scratch_shapes=[pltpu.SemaphoreType.DMA((transfers * kc,))],
        cost_estimate=COST,
        compiler_params=PARAMS,
    )(pltpu.with_memory_space_constraint(factor, pltpu.HBM))


def pack_kernel(bits, partner, factor, *refs):
    outs, sems = refs[:-1], refs[-1]
    kc, half = factor.shape[1], outs[0].shape[2]
    group = lax.axis_index("kpt")
    copies = []
    for h in (1, 0):
        for transfer, bit in enumerate(bits):
            far_group = jnp.bitwise_xor(group, 1 << bit)
            for k in range(kc):
                slot = partner[transfer, far_group * kc + k] - group * kc
                source = factor.at[transfer, slot, 0, :, pl.ds(h * half, half), :]
                target = outs[h * len(bits) + transfer].at[k]
                copies.append(pltpu.make_async_copy(source, target, sems.at[len(copies)]))
                copies[-1].start()
    for copy in copies:
        copy.wait()


def pack(bits, partner, factor, work):
    transfers, kc, _, parts, nv, naux = factor.shape
    return pl.pallas_call(
        functools.partial(pack_kernel, bits),
        out_shape=[jax.ShapeDtypeStruct((kc, parts, nv // 2, naux), BF16)] * (2 * transfers),
        in_specs=[SMEM, ANY],
        out_specs=[VMEM] * (2 * transfers),
        scratch_shapes=[pltpu.SemaphoreType.DMA((2 * transfers * kc,))],
        cost_estimate=pl.CostEstimate(flops=0, bytes_accessed=work, transcendentals=0),
        compiler_params=PARAMS,
    )(
        pltpu.with_memory_space_constraint(partner, pltpu.HBM),
        pltpu.with_memory_space_constraint(factor, pltpu.HBM),
    )


def inverse_kernel(bits, partner, occ, virtual, out):
    _, _, kc, nv, _ = out.shape
    total = occ.shape[1]
    group, orbit = lax.axis_index("kpt"), lax.axis_index("occ")
    parity = lax.rem(orbit, 2)
    columns = (orbit, orbit + 1 - 2 * parity, lax.rem(orbit + total - 1 + 2 * parity, total))

    def point_step(k, carry):
        point = group * kc + k
        row = virtual[pl.ds(point, 1), :]
        for transfer in range(len(bits)):
            far_point = partner[transfer, point]
            column = column_of(virtual[pl.ds(far_point, 1), :])
            for place, index in enumerate(columns):
                level = occ[point, orbit] + occ[far_point, index]
                out[transfer, place, k] = 1.0 / ((level - column) - row)
        return carry

    lax.fori_loop(0, kc, point_step, 0)


def inverses(bits, partner, occ_energy, virtual, kc):
    nv = virtual.shape[1]
    return pl.pallas_call(
        functools.partial(inverse_kernel, bits),
        out_shape=jax.ShapeDtypeStruct((len(bits), 3, kc, nv, nv), F32),
        in_specs=[SMEM, SMEM, VMEM],
        out_specs=VMEM,
        cost_estimate=COST,
        compiler_params=PARAMS,
    )(partner, occ_energy, virtual)


def amplitude_rows(own, terms):
    _, nv, naux = own.shape
    left = own.reshape(2 * nv, naux)
    rows, blocks = ([], []), []
    for window, inverse in terms:
        size = window.shape[1]
        window = window.reshape(2 * size, naux)
        products = lax.dot_general(
            left, window, (((1,), (1,)), ((), ())), preferred_element_type=F32
        )
        real_part = ((products[:nv, :size] + products[nv:, size:]) * inverse).astype(BF16)
        imag_part = ((products[nv:, :size] - products[:nv, size:]) * inverse).astype(BF16)
        rows[0].extend([real_part, -imag_part])
        rows[1].extend([imag_part, real_part])
        blocks.append(window)
    return [jnp.concatenate(part, axis=1) for part in rows], jnp.concatenate(blocks, axis=0)


def contract(factor, terms_of, finish):
    waiting = None
    points = [(t, k) for t in range(factor.shape[0]) for k in range(factor.shape[1])]
    for point in [*points, None]:
        ready, waiting = waiting, None
        if point is not None:
            t, k = point
            waiting = (t, k, *amplitude_rows(factor[t, k, 0], terms_of(t, k)))
        if ready is not None:
            t, k, rows, blocks = ready
            for part in range(2):
                finish(t, k, part, jnp.dot(rows[part], blocks, preferred_element_type=F32))


def half_of(h, half):
    return slice(h * half, (h + 1) * half)


def first_kernel(factor, inverse, *refs):
    transfers, kc = factor.shape[:2]
    owns, near, out = refs[: 2 * transfers], refs[-2], refs[-1]
    first, second = half_of(0, near.shape[2]), half_of(1, near.shape[2])

    def terms_of(t, k):
        return [
            (owns[t][k], inverse[t, 0, k, :, first]),
            (owns[transfers + t][k], inverse[t, 0, k, :, second]),
            (near[t * kc + k], inverse[t, 1, k, :, first]),
        ]

    def finish(t, k, part, value):
        out[t, k, part] = value

    contract(factor, terms_of, finish)


def first_terms(factor, inverse, owns, near):
    transfers, kc, _, parts, nv, naux = factor.shape
    operands = [factor, inverse, *owns, near]
    return pl.pallas_call(
        first_kernel,
        out_shape=jax.ShapeDtypeStruct((transfers, kc, parts, nv, naux), F32),
        in_specs=[VMEM] * len(operands),
        out_specs=VMEM,
        cost_estimate=COST,
        compiler_params=PARAMS,
    )(*operands)


def second_kernel(factor, inverse, near, *refs):
    fars, total, out = refs[:-2], refs[-2], refs[-1]
    kc, half = factor.shape[1], near.shape[2]

    def terms_of(t, k):
        return [
            (near[t * kc + k], inverse[t, 1, k, :, half_of(1, half)]),
            (fars[t][k], inverse[t, 2, k, :, half_of(0, half)]),
        ]

    def finish(t, k, part, value):
        out[t, k, part] = value + total[t, k, part]

    contract(factor, terms_of, finish)


def second_terms(factor, inverse, near, fars, total):
    operands = [factor, inverse, near, *fars, total]
    return pl.pallas_call(
        second_kernel,
        out_shape=jax.ShapeDtypeStruct(total.shape, F32),
        in_specs=[VMEM] * len(operands),
        out_specs=VMEM,
        input_output_aliases={len(operands) - 1: 0},
        cost_estimate=COST,
        compiler_params=PARAMS,
    )(*operands)


def last_kernel(factor, inverse, window, total, out, staged, sems):
    kc, half = factor.shape[1], window.shape[2]
    copies = []

    def terms_of(t, k):
        return [(window[t * kc + k], inverse[t, 2, k, :, half_of(1, half)])]

    def finish(t, k, part, value):
        at = len(copies)
        staged[at] = (value + total[t, k, part]).astype(BF16)
        copies.append(pltpu.make_async_copy(staged.at[at], out.at[t, k, 0, part], sems.at[at]))
        copies[-1].start()

    contract(factor, terms_of, finish)
    for copy in copies:
        copy.wait()


def last_terms(factor, inverse, window, total):
    transfers, kc, _, parts, nv, naux = factor.shape
    count = transfers * kc * parts
    return pl.pallas_call(
        last_kernel,
        out_shape=jax.ShapeDtypeStruct(factor.shape, BF16),
        in_specs=[VMEM] * 4,
        out_specs=ANY,
        scratch_shapes=[
            pltpu.VMEM((count, nv, naux), BF16),
            pltpu.SemaphoreType.DMA((count,)),
        ],
        cost_estimate=COST,
        compiler_params=PARAMS,
    )(factor, inverse, window, total)


def body(factor, partner, occ_energy, vir_sorted, vir_order):
    transfers, kc = factor.shape[:2]
    bits = (0, lax.axis_size("kpt").bit_length() - 2)

    group = lax.axis_index("kpt")
    part = lay(factor)
    beside = far_swap(part)
    packs = pack(bits, after(partner, part), factor, WORK * factor.size)
    earlies, lates = packs[:transfers], packs[transfers:]
    late_own = [group_swap(lates[t], bits[t]) for t in range(transfers)]
    early_own = [group_swap(earlies[t], bits[t]) for t in range(transfers)]
    late_block = jnp.concatenate(late_own)
    late_far = far_swap(late_block)
    late_near = near_swap(late_block)
    early_block = jnp.concatenate(early_own)
    early_near = jnp.concatenate(
        [near_swap(after(early_block[:-1], beside)), near_swap(early_block[-1:])]
    )
    early_far = []
    for t in range(transfers):
        far_group = jnp.bitwise_xor(group, 1 << bits[t])
        slots = lax.dynamic_slice_in_dim(partner[t], far_group * kc, kc) - group * kc
        ordered = [lax.dynamic_slice_in_dim(beside, t * kc + slots[k], 1) for k in range(kc)]
        early_far.append(group_swap(jnp.concatenate(ordered), bits[t]))

    virtual = virtual_energies(vir_sorted, vir_order)
    inverse = inverses(bits, partner, occ_energy, virtual, kc)
    total = first_terms(factor, inverse, early_own + late_own, early_near)
    total = second_terms(factor, inverse, late_near, early_far, total)
    return last_terms(factor, inverse, late_far, total)


def solution(mesh):
    spec = P(None, "kpt", "occ", None, None, None)
    in_specs = (spec, P(), P(), P(), P())
    return jax.shard_map(body, mesh=mesh, in_specs=in_specs, out_specs=spec, check_vma=False)
```

```python
import functools

import jax
import jax.numpy as jnp
from jax import lax
from jax.experimental import pallas as pl
from jax.experimental.pallas import tpu as pltpu
from jax.sharding import PartitionSpec as P

F32 = jnp.float32
BF16 = jnp.bfloat16
ANY = pl.BlockSpec(memory_space=pl.ANY)
VMEM = pl.BlockSpec(memory_space=pltpu.VMEM)
SMEM = pl.BlockSpec(memory_space=pltpu.SMEM)
PARAMS = pltpu.CompilerParams(vmem_limit_bytes=8 * 1024 * 1024)
WORK = 16
COST = pl.CostEstimate(flops=0, bytes_accessed=0, transcendentals=0)


def group_swap(block, bit):
    count = lax.axis_size("kpt")
    return lax.ppermute(block, "kpt", [(g, g ^ (1 << bit)) for g in range(count)])


def near_swap(block):
    count = lax.axis_size("occ")
    return lax.ppermute(block, "occ", [(i, i ^ 1) for i in range(count)])


def far_swap(block):
    count = lax.axis_size("occ")
    return lax.ppermute(
        block, "occ", [(i, (i + (1 if i % 2 else count - 1)) % count) for i in range(count)]
    )


def after(block, *others):
    return lax.optimization_barrier((block, *others))[0]


def virtual_energies(vir_sorted, vir_order):
    ranks = jnp.arange(vir_sorted.shape[1], dtype=jnp.int32)
    matches = vir_order[:, :, None] == ranks[None, None, :]
    return jnp.sum(jnp.where(matches, vir_sorted[:, None, :], 0.0), axis=2)


def column_of(row):
    return jnp.transpose(jnp.broadcast_to(row, (8, row.shape[1])))[:, :1]


def pack_kernel(bits, h, partner, factor, *refs):
    outs, sems = refs[:-1], refs[-1]
    kc, half = factor.shape[1], outs[0].shape[2]
    targets = [out.at[n] for out in outs for n in range(out.shape[0])]
    group = lax.axis_index("kpt")
    copies = []
    for transfer, bit in enumerate(bits):
        far_group = jnp.bitwise_xor(group, 1 << bit)
        for k in range(kc):
            slot = partner[transfer, far_group * kc + k] - group * kc
            source = factor.at[transfer, slot, 0, :, pl.ds(h * half, half), :]
            at = transfer * kc + k
            copies.append(pltpu.make_async_copy(source, targets[at], sems.at[at]))
            copies[-1].start()
    for copy in copies:
        copy.wait()


def pack(bits, h, counts, partner, factor, work):
    _, _, _, parts, nv, naux = factor.shape
    return pl.pallas_call(
        functools.partial(pack_kernel, bits, h),
        out_shape=[jax.ShapeDtypeStruct((n, parts, nv // 2, naux), BF16) for n in counts],
        in_specs=[SMEM, ANY],
        out_specs=[VMEM] * len(counts),
        scratch_shapes=[pltpu.SemaphoreType.DMA((sum(counts),))],
        cost_estimate=pl.CostEstimate(flops=0, bytes_accessed=work, transcendentals=0),
        compiler_params=PARAMS,
    )(
        pltpu.with_memory_space_constraint(partner, pltpu.HBM),
        pltpu.with_memory_space_constraint(factor, pltpu.HBM),
    )


def inverse_kernel(bits, partner, occ, virtual, out):
    _, _, kc, nv, _ = out.shape
    total = occ.shape[1]
    group, orbit = lax.axis_index("kpt"), lax.axis_index("occ")
    parity = lax.rem(orbit, 2)
    columns = (orbit, orbit + 1 - 2 * parity, lax.rem(orbit + total - 1 + 2 * parity, total))

    def point_step(k, carry):
        point = group * kc + k
        row = virtual[pl.ds(point, 1), :]
        for transfer in range(len(bits)):
            far_point = partner[transfer, point]
            column = column_of(virtual[pl.ds(far_point, 1), :])
            for place, index in enumerate(columns):
                level = occ[point, orbit] + occ[far_point, index]
                out[transfer, place, k] = 1.0 / ((level - column) - row)
        return carry

    lax.fori_loop(0, kc, point_step, 0)


def inverses(bits, partner, occ_energy, virtual, kc):
    nv = virtual.shape[1]
    return pl.pallas_call(
        functools.partial(inverse_kernel, bits),
        out_shape=jax.ShapeDtypeStruct((len(bits), 3, kc, nv, nv), F32),
        in_specs=[SMEM, SMEM, VMEM],
        out_specs=VMEM,
        cost_estimate=COST,
        compiler_params=PARAMS,
    )(partner, occ_energy, virtual)


def amplitude_rows(own, terms):
    _, nv, naux = own.shape
    left = own.reshape(2 * nv, naux)
    rows, blocks = ([], []), []
    for window, inverse in terms:
        size = window.shape[1]
        window = window.reshape(2 * size, naux)
        products = lax.dot_general(
            left, window, (((1,), (1,)), ((), ())), preferred_element_type=F32
        )
        real_part = ((products[:nv, :size] + products[nv:, size:]) * inverse).astype(BF16)
        imag_part = ((products[nv:, :size] - products[:nv, size:]) * inverse).astype(BF16)
        rows[0].extend([real_part, -imag_part])
        rows[1].extend([imag_part, real_part])
        blocks.append(window)
    return [jnp.concatenate(part, axis=1) for part in rows], jnp.concatenate(blocks, axis=0)


def contract(factor, terms_of, finish):
    waiting = None
    points = [(t, k) for t in range(factor.shape[0]) for k in range(factor.shape[1])]
    for point in [*points, None]:
        ready, waiting = waiting, None
        if point is not None:
            t, k = point
            waiting = (t, k, *amplitude_rows(factor[t, k, 0], terms_of(t, k)))
        if ready is not None:
            t, k, rows, blocks = ready
            for part in range(2):
                finish(t, k, part, jnp.dot(rows[part], blocks, preferred_element_type=F32))


def half_of(h, half):
    return slice(h * half, (h + 1) * half)


def first_kernel(factor, inverse, *refs):
    transfers, kc = factor.shape[:2]
    owns, near, out = refs[: 2 * transfers], refs[-2], refs[-1]
    first, second = half_of(0, near.shape[2]), half_of(1, near.shape[2])

    def terms_of(t, k):
        return [
            (owns[t][k], inverse[t, 0, k, :, first]),
            (owns[transfers + t][k], inverse[t, 0, k, :, second]),
            (near[t * kc + k], inverse[t, 1, k, :, first]),
        ]

    def finish(t, k, part, value):
        out[t, k, part] = value

    contract(factor, terms_of, finish)


def first_terms(factor, inverse, owns, near):
    transfers, kc, _, parts, nv, naux = factor.shape
    operands = [factor, inverse, *owns, near]
    return pl.pallas_call(
        first_kernel,
        out_shape=jax.ShapeDtypeStruct((transfers, kc, parts, nv, naux), F32),
        in_specs=[VMEM] * len(operands),
        out_specs=VMEM,
        cost_estimate=COST,
        compiler_params=PARAMS,
    )(*operands)


def second_kernel(factor, inverse, near, *refs):
    fars, total, out = refs[:-2], refs[-2], refs[-1]
    kc, half = factor.shape[1], near.shape[2]

    def terms_of(t, k):
        return [
            (near[t * kc + k], inverse[t, 1, k, :, half_of(1, half)]),
            (fars[t][k], inverse[t, 2, k, :, half_of(0, half)]),
        ]

    def finish(t, k, part, value):
        out[t, k, part] = value + total[t, k, part]

    contract(factor, terms_of, finish)


def second_terms(factor, inverse, near, fars, total):
    operands = [factor, inverse, near, *fars, total]
    return pl.pallas_call(
        second_kernel,
        out_shape=jax.ShapeDtypeStruct(total.shape, F32),
        in_specs=[VMEM] * len(operands),
        out_specs=VMEM,
        input_output_aliases={len(operands) - 1: 0},
        cost_estimate=COST,
        compiler_params=PARAMS,
    )(*operands)


def last_kernel(factor, inverse, window, total, out, staged, sems):
    kc, half = factor.shape[1], window.shape[2]
    copies = []

    def terms_of(t, k):
        return [(window[t * kc + k], inverse[t, 2, k, :, half_of(1, half)])]

    def finish(t, k, part, value):
        at = len(copies)
        staged[at] = (value + total[t, k, part]).astype(BF16)
        copies.append(pltpu.make_async_copy(staged.at[at], out.at[t, k, 0, part], sems.at[at]))
        copies[-1].start()

    contract(factor, terms_of, finish)
    for copy in copies:
        copy.wait()


def last_terms(factor, inverse, window, total):
    transfers, kc, _, parts, nv, naux = factor.shape
    count = transfers * kc * parts
    return pl.pallas_call(
        last_kernel,
        out_shape=jax.ShapeDtypeStruct(factor.shape, BF16),
        in_specs=[VMEM] * 4,
        out_specs=ANY,
        scratch_shapes=[
            pltpu.VMEM((count, nv, naux), BF16),
            pltpu.SemaphoreType.DMA((count,)),
        ],
        cost_estimate=COST,
        compiler_params=PARAMS,
    )(factor, inverse, window, total)


def body(factor, partner, occ_energy, vir_sorted, vir_order):
    transfers, kc = factor.shape[:2]
    bits = (0, lax.axis_size("kpt").bit_length() - 2)

    (part,) = pack(bits, 0, [transfers * kc], partner, factor, 0)
    beside = far_swap(part)
    lates = pack(bits, 1, [kc] * transfers, after(partner, part), factor, WORK * factor.size)
    late_own = [group_swap(lates[t], bits[t]) for t in range(transfers)]
    early_own = [group_swap(part[t * kc : (t + 1) * kc], bits[t]) for t in range(transfers)]
    late_block = jnp.concatenate(late_own)
    late_far = far_swap(late_block)
    late_near = near_swap(late_block)
    early_block = jnp.concatenate(early_own)
    early_near = jnp.concatenate(
        [near_swap(after(early_block[:-1], beside)), near_swap(early_block[-1:])]
    )
    early_far = [group_swap(beside[t * kc : (t + 1) * kc], bits[t]) for t in range(transfers)]

    virtual = virtual_energies(vir_sorted, vir_order)
    inverse = inverses(bits, partner, occ_energy, virtual, kc)
    total = first_terms(factor, inverse, early_own + late_own, early_near)
    total = second_terms(factor, inverse, late_near, early_far, total)
    return last_terms(factor, inverse, late_far, total)


def solution(mesh):
    spec = P(None, "kpt", "occ", None, None, None)
    in_specs = (spec, P(), P(), P(), P())
    return jax.shard_map(body, mesh=mesh, in_specs=in_specs, out_specs=spec, check_vma=False)
```

```python
import functools

import jax
import jax.numpy as jnp
from jax import lax
from jax.experimental import pallas as pl
from jax.experimental.pallas import tpu as pltpu
from jax.sharding import PartitionSpec as P

F32 = jnp.float32
BF16 = jnp.bfloat16
ANY = pl.BlockSpec(memory_space=pl.ANY)
VMEM = pl.BlockSpec(memory_space=pltpu.VMEM)
SMEM = pl.BlockSpec(memory_space=pltpu.SMEM)
PARAMS = pltpu.CompilerParams(vmem_limit_bytes=8 * 1024 * 1024)
WORK = 16
ROWS = 16
COST = pl.CostEstimate(flops=0, bytes_accessed=0, transcendentals=0)


def group_swap(block, bit):
    count = lax.axis_size("kpt")
    return lax.ppermute(block, "kpt", [(g, g ^ (1 << bit)) for g in range(count)])


def near_swap(block):
    count = lax.axis_size("occ")
    return lax.ppermute(block, "occ", [(i, i ^ 1) for i in range(count)])


def far_swap(block):
    count = lax.axis_size("occ")
    return lax.ppermute(
        block, "occ", [(i, (i + (1 if i % 2 else count - 1)) % count) for i in range(count)]
    )


def after(block, *others):
    return lax.optimization_barrier((block, *others))[0]


def virtual_energies(vir_sorted, vir_order):
    ranks = jnp.arange(vir_sorted.shape[1], dtype=jnp.int32)
    matches = vir_order[:, :, None] == ranks[None, None, :]
    return jnp.sum(jnp.where(matches, vir_sorted[:, None, :], 0.0), axis=2)


def column_of(row):
    return jnp.transpose(jnp.broadcast_to(row, (8, row.shape[1])))[:, :1]


def lay_kernel(factor, out, sems):
    kc, half = factor.shape[1], out.shape[2]
    copies = []
    for at in range(out.shape[0]):
        source = factor.at[at // kc, at % kc, 0, :, pl.ds(0, half), :]
        copies.append(pltpu.make_async_copy(source, out.at[at], sems.at[at]))
        copies[-1].start()
    for copy in copies:
        copy.wait()


def lay(factor):
    transfers, kc, _, parts, nv, naux = factor.shape
    return pl.pallas_call(
        lay_kernel,
        out_shape=jax.ShapeDtypeStruct((transfers * kc, parts, nv // 2, naux), BF16),
        in_specs=[ANY],
        out_specs=VMEM,
        scratch_shapes=[pltpu.SemaphoreType.DMA((transfers * kc,))],
        cost_estimate=COST,
        compiler_params=PARAMS,
    )(pltpu.with_memory_space_constraint(factor, pltpu.HBM))


def pack_kernel(bits, partner, factor, *refs):
    outs, sems = refs[:-1], refs[-1]
    kc, half = factor.shape[1], outs[0].shape[2]
    group = lax.axis_index("kpt")
    copies = []
    for h in (1, 0):
        for transfer, bit in enumerate(bits):
            far_group = jnp.bitwise_xor(group, 1 << bit)
            for k in range(kc):
                slot = partner[transfer, far_group * kc + k] - group * kc
                source = factor.at[transfer, slot, 0, :, pl.ds(h * half, half), :]
                target = outs[h * len(bits) + transfer].at[k]
                copies.append(pltpu.make_async_copy(source, target, sems.at[len(copies)]))
                copies[-1].start()
    for copy in copies:
        copy.wait()


def pack(bits, partner, factor, work):
    transfers, kc, _, parts, nv, naux = factor.shape
    return pl.pallas_call(
        functools.partial(pack_kernel, bits),
        out_shape=[jax.ShapeDtypeStruct((kc, parts, nv // 2, naux), BF16)] * (2 * transfers),
        in_specs=[SMEM, ANY],
        out_specs=[VMEM] * (2 * transfers),
        scratch_shapes=[pltpu.SemaphoreType.DMA((2 * transfers * kc,))],
        cost_estimate=pl.CostEstimate(flops=0, bytes_accessed=work, transcendentals=0),
        compiler_params=PARAMS,
    )(
        pltpu.with_memory_space_constraint(partner, pltpu.HBM),
        pltpu.with_memory_space_constraint(factor, pltpu.HBM),
    )


def inverse_kernel(bits, partner, occ, virtual, out, choice):
    _, _, kc, nv, _ = out.shape
    total = occ.shape[1]
    group, orbit = lax.axis_index("kpt"), lax.axis_index("occ")
    parity = lax.rem(orbit, 2)
    columns = (orbit, orbit + 1 - 2 * parity, lax.rem(orbit + total - 1 + 2 * parity, total))

    def point_step(k, carry):
        point = group * kc + k
        row = virtual[pl.ds(point, 1), :]
        for transfer in range(len(bits)):
            far_point = partner[transfer, point]
            column = column_of(virtual[pl.ds(far_point, 1), :])
            slot = far_point - jnp.bitwise_xor(group, 1 << bits[transfer]) * kc
            for c in range(kc):
                chosen = jnp.where(slot == c, 1.0, 0.0)
                choice[transfer, k, c] = jnp.full(choice.shape[3:], chosen, F32).astype(BF16)
            for place, index in enumerate(columns):
                level = occ[point, orbit] + occ[far_point, index]
                out[transfer, place, k] = 1.0 / ((level - column) - row)
        return carry

    lax.fori_loop(0, kc, point_step, 0)


def inverses(bits, partner, occ_energy, virtual, kc, naux):
    nv = virtual.shape[1]
    return pl.pallas_call(
        functools.partial(inverse_kernel, bits),
        out_shape=[
            jax.ShapeDtypeStruct((len(bits), 3, kc, nv, nv), F32),
            jax.ShapeDtypeStruct((len(bits), kc, kc, ROWS, naux), BF16),
        ],
        in_specs=[SMEM, SMEM, VMEM],
        out_specs=[VMEM, VMEM],
        cost_estimate=COST,
        compiler_params=PARAMS,
    )(partner, occ_energy, virtual)


def amplitude_rows(own, terms):
    _, nv, naux = own.shape
    left = own.reshape(2 * nv, naux)
    rows, blocks = ([], []), []
    for window, inverse in terms:
        size = window.shape[1]
        window = window.reshape(2 * size, naux)
        products = lax.dot_general(
            left, window, (((1,), (1,)), ((), ())), preferred_element_type=F32
        )
        real_part = ((products[:nv, :size] + products[nv:, size:]) * inverse).astype(BF16)
        imag_part = ((products[nv:, :size] - products[:nv, size:]) * inverse).astype(BF16)
        rows[0].extend([real_part, -imag_part])
        rows[1].extend([imag_part, real_part])
        blocks.append(window)
    return [jnp.concatenate(part, axis=1) for part in rows], jnp.concatenate(blocks, axis=0)


def contract(factor, terms_of, finish):
    waiting = None
    points = [(t, k) for t in range(factor.shape[0]) for k in range(factor.shape[1])]
    for point in [*points, None]:
        ready, waiting = waiting, None
        if point is not None:
            t, k = point
            waiting = (t, k, *amplitude_rows(factor[t, k, 0], terms_of(t, k)))
        if ready is not None:
            t, k, rows, blocks = ready
            for part in range(2):
                finish(t, k, part, jnp.dot(rows[part], blocks, preferred_element_type=F32))


def half_of(h, half):
    return slice(h * half, (h + 1) * half)


def first_kernel(factor, inverse, *refs):
    transfers, kc = factor.shape[:2]
    owns, near, out = refs[: 2 * transfers], refs[-2], refs[-1]
    first, second = half_of(0, near.shape[2]), half_of(1, near.shape[2])

    def terms_of(t, k):
        return [
            (owns[t][k], inverse[t, 0, k, :, first]),
            (owns[transfers + t][k], inverse[t, 0, k, :, second]),
            (near[t * kc + k], inverse[t, 1, k, :, first]),
        ]

    def finish(t, k, part, value):
        out[t, k, part] = value

    contract(factor, terms_of, finish)


def first_terms(factor, inverse, owns, near):
    transfers, kc, _, parts, nv, naux = factor.shape
    operands = [factor, inverse, *owns, near]
    return pl.pallas_call(
        first_kernel,
        out_shape=jax.ShapeDtypeStruct((transfers, kc, parts, nv, naux), F32),
        in_specs=[VMEM] * len(operands),
        out_specs=VMEM,
        cost_estimate=COST,
        compiler_params=PARAMS,
    )(*operands)


def near_kernel(factor, inverse, near, total, out):
    kc, half = factor.shape[1], near.shape[2]

    def terms_of(t, k):
        return [(near[t * kc + k], inverse[t, 1, k, :, half_of(1, half)])]

    def finish(t, k, part, value):
        out[t, k, part] = value + total[t, k, part]

    contract(factor, terms_of, finish)


def far_kernel(factor, inverse, choice, *refs):
    fars, total, out = refs[:-2], refs[-2], refs[-1]
    kc, half = factor.shape[1], fars[0].shape[2]

    def terms_of(t, k):
        blocks = [fars[t][c].reshape(-1, *choice.shape[3:]) for c in range(kc)]
        chosen = [block * choice[t, k, c][None] for c, block in enumerate(blocks)]
        window = functools.reduce(jnp.add, chosen)
        return [(window.reshape(fars[t].shape[1:]), inverse[t, 2, k, :, half_of(0, half)])]

    def finish(t, k, part, value):
        out[t, k, part] = value + total[t, k, part]

    contract(factor, terms_of, finish)


def more_terms(body, operands, total):
    return pl.pallas_call(
        body,
        out_shape=jax.ShapeDtypeStruct(total.shape, F32),
        in_specs=[VMEM] * (len(operands) + 1),
        out_specs=VMEM,
        input_output_aliases={len(operands): 0},
        cost_estimate=COST,
        compiler_params=PARAMS,
    )(*operands, total)


def last_kernel(factor, inverse, window, total, out, staged, sems):
    kc, half = factor.shape[1], window.shape[2]
    copies = []

    def terms_of(t, k):
        return [(window[t * kc + k], inverse[t, 2, k, :, half_of(1, half)])]

    def finish(t, k, part, value):
        at = len(copies)
        staged[at] = (value + total[t, k, part]).astype(BF16)
        copies.append(pltpu.make_async_copy(staged.at[at], out.at[t, k, 0, part], sems.at[at]))
        copies[-1].start()

    contract(factor, terms_of, finish)
    for copy in copies:
        copy.wait()


def last_terms(factor, inverse, window, total):
    transfers, kc, _, parts, nv, naux = factor.shape
    count = transfers * kc * parts
    return pl.pallas_call(
        last_kernel,
        out_shape=jax.ShapeDtypeStruct(factor.shape, BF16),
        in_specs=[VMEM] * 4,
        out_specs=ANY,
        scratch_shapes=[
            pltpu.VMEM((count, nv, naux), BF16),
            pltpu.SemaphoreType.DMA((count,)),
        ],
        cost_estimate=COST,
        compiler_params=PARAMS,
    )(factor, inverse, window, total)


def body(factor, partner, occ_energy, vir_sorted, vir_order):
    transfers, kc = factor.shape[:2]
    bits = (0, lax.axis_size("kpt").bit_length() - 2)

    part = lay(factor)
    beside = far_swap(part)
    packs = pack(bits, after(partner, part), factor, WORK * factor.size)
    earlies, lates = packs[:transfers], packs[transfers:]
    late_own = [group_swap(lates[t], bits[t]) for t in range(transfers)]
    early_own = [group_swap(earlies[t], bits[t]) for t in range(transfers)]
    late_block = jnp.concatenate(late_own)
    late_far = far_swap(late_block)
    late_near = near_swap(late_block)
    early_block = jnp.concatenate(early_own)
    early_near = jnp.concatenate(
        [near_swap(after(early_block[:-1], beside)), near_swap(early_block[-1:])]
    )
    early_far = [group_swap(beside[t * kc : (t + 1) * kc], bits[t]) for t in range(transfers)]

    virtual = virtual_energies(vir_sorted, vir_order)
    inverse, choice = inverses(bits, partner, occ_energy, virtual, kc, factor.shape[5])
    total = first_terms(factor, inverse, early_own + late_own, early_near)
    total = more_terms(near_kernel, [factor, inverse, late_near], total)
    total = more_terms(far_kernel, [factor, inverse, choice, *early_far], total)
    return last_terms(factor, inverse, late_far, total)


def solution(mesh):
    spec = P(None, "kpt", "occ", None, None, None)
    in_specs = (spec, P(), P(), P(), P())
    return jax.shard_map(body, mesh=mesh, in_specs=in_specs, out_specs=spec, check_vma=False)
```

```python
import functools

import jax
import jax.numpy as jnp
from jax import lax
from jax.experimental import pallas as pl
from jax.experimental.pallas import tpu as pltpu
from jax.sharding import PartitionSpec as P

F32 = jnp.float32
BF16 = jnp.bfloat16
ANY = pl.BlockSpec(memory_space=pl.ANY)
VMEM = pl.BlockSpec(memory_space=pltpu.VMEM)
SMEM = pl.BlockSpec(memory_space=pltpu.SMEM)
PARAMS = pltpu.CompilerParams(vmem_limit_bytes=8 * 1024 * 1024)
WORK = 16
ROWS = 16
COST = pl.CostEstimate(flops=0, bytes_accessed=0, transcendentals=0)


def group_swap(block, bit):
    count = lax.axis_size("kpt")
    return lax.ppermute(block, "kpt", [(g, g ^ (1 << bit)) for g in range(count)])


def near_swap(block):
    count = lax.axis_size("occ")
    return lax.ppermute(block, "occ", [(i, i ^ 1) for i in range(count)])


def far_swap(block):
    count = lax.axis_size("occ")
    return lax.ppermute(
        block, "occ", [(i, (i + (1 if i % 2 else count - 1)) % count) for i in range(count)]
    )


def after(block, *others):
    return lax.optimization_barrier((block, *others))[0]


def virtual_energies(vir_sorted, vir_order):
    ranks = jnp.arange(vir_sorted.shape[1], dtype=jnp.int32)
    matches = vir_order[:, :, None] == ranks[None, None, :]
    return jnp.sum(jnp.where(matches, vir_sorted[:, None, :], 0.0), axis=2)


def column_of(row):
    return jnp.transpose(jnp.broadcast_to(row, (8, row.shape[1])))[:, :1]


def pack_kernel(bits, partner, factor, *refs):
    outs, sems = refs[:-1], refs[-1]
    kc, half = factor.shape[1], outs[0].shape[2]
    group = lax.axis_index("kpt")
    copies = []
    for h in (1, 0):
        for transfer, bit in enumerate(bits):
            far_group = jnp.bitwise_xor(group, 1 << bit)
            for k in range(kc):
                slot = partner[transfer, far_group * kc + k] - group * kc
                source = factor.at[transfer, slot, 0, :, pl.ds(h * half, half), :]
                target = outs[h * len(bits) + transfer].at[k]
                copies.append(pltpu.make_async_copy(source, target, sems.at[len(copies)]))
                copies[-1].start()
    for copy in copies:
        copy.wait()


def pack(bits, partner, factor, work):
    transfers, kc, _, parts, nv, naux = factor.shape
    return pl.pallas_call(
        functools.partial(pack_kernel, bits),
        out_shape=[jax.ShapeDtypeStruct((kc, parts, nv // 2, naux), BF16)] * (2 * transfers),
        in_specs=[SMEM, ANY],
        out_specs=[VMEM] * (2 * transfers),
        scratch_shapes=[pltpu.SemaphoreType.DMA((2 * transfers * kc,))],
        cost_estimate=pl.CostEstimate(flops=0, bytes_accessed=work, transcendentals=0),
        compiler_params=PARAMS,
    )(
        pltpu.with_memory_space_constraint(partner, pltpu.HBM),
        pltpu.with_memory_space_constraint(factor, pltpu.HBM),
    )


def inverse_kernel(bits, partner, occ, virtual, out, choice):
    _, _, kc, nv, _ = out.shape
    total = occ.shape[1]
    group, orbit = lax.axis_index("kpt"), lax.axis_index("occ")
    parity = lax.rem(orbit, 2)
    columns = (orbit, orbit + 1 - 2 * parity, lax.rem(orbit + total - 1 + 2 * parity, total))

    def point_step(k, carry):
        point = group * kc + k
        row = virtual[pl.ds(point, 1), :]
        for transfer in range(len(bits)):
            far_point = partner[transfer, point]
            column = column_of(virtual[pl.ds(far_point, 1), :])
            slot = far_point - jnp.bitwise_xor(group, 1 << bits[transfer]) * kc
            for c in range(kc):
                chosen = jnp.where(slot == c, 1.0, 0.0)
                choice[transfer, k, c] = jnp.full(choice.shape[3:], chosen, F32).astype(BF16)
            for place, index in enumerate(columns):
                level = occ[point, orbit] + occ[far_point, index]
                out[transfer, place, k] = 1.0 / ((level - column) - row)
        return carry

    lax.fori_loop(0, kc, point_step, 0)


def inverses(bits, partner, occ_energy, virtual, kc, naux):
    nv = virtual.shape[1]
    return pl.pallas_call(
        functools.partial(inverse_kernel, bits),
        out_shape=[
            jax.ShapeDtypeStruct((len(bits), 3, kc, nv, nv), F32),
            jax.ShapeDtypeStruct((len(bits), kc, kc, ROWS, naux), BF16),
        ],
        in_specs=[SMEM, SMEM, VMEM],
        out_specs=[VMEM, VMEM],
        cost_estimate=COST,
        compiler_params=PARAMS,
    )(partner, occ_energy, virtual)


def amplitude_rows(own, terms):
    _, nv, naux = own.shape
    left = own.reshape(2 * nv, naux)
    rows, blocks = ([], []), []
    for window, inverse in terms:
        size = window.shape[1]
        window = window.reshape(2 * size, naux)
        products = lax.dot_general(
            left, window, (((1,), (1,)), ((), ())), preferred_element_type=F32
        )
        real_part = ((products[:nv, :size] + products[nv:, size:]) * inverse).astype(BF16)
        imag_part = ((products[nv:, :size] - products[:nv, size:]) * inverse).astype(BF16)
        rows[0].extend([real_part, -imag_part])
        rows[1].extend([imag_part, real_part])
        blocks.append(window)
    return [jnp.concatenate(part, axis=1) for part in rows], jnp.concatenate(blocks, axis=0)


def contract(factor, terms_of, finish):
    waiting = None
    points = [(t, k) for t in range(factor.shape[0]) for k in range(factor.shape[1])]
    for point in [*points, None]:
        ready, waiting = waiting, None
        if point is not None:
            t, k = point
            waiting = (t, k, *amplitude_rows(factor[t, k, 0], terms_of(t, k)))
        if ready is not None:
            t, k, rows, blocks = ready
            for part in range(2):
                finish(t, k, part, jnp.dot(rows[part], blocks, preferred_element_type=F32))


def half_of(h, half):
    return slice(h * half, (h + 1) * half)


def first_kernel(factor, inverse, *refs):
    transfers, kc = factor.shape[:2]
    owns, near, out = refs[: 2 * transfers], refs[-2], refs[-1]
    first, second = half_of(0, near.shape[2]), half_of(1, near.shape[2])

    def terms_of(t, k):
        return [
            (owns[t][k], inverse[t, 0, k, :, first]),
            (owns[transfers + t][k], inverse[t, 0, k, :, second]),
            (near[t * kc + k], inverse[t, 1, k, :, first]),
        ]

    def finish(t, k, part, value):
        out[t, k, part] = value

    contract(factor, terms_of, finish)


def first_terms(factor, inverse, owns, near):
    transfers, kc, _, parts, nv, naux = factor.shape
    operands = [factor, inverse, *owns, near]
    return pl.pallas_call(
        first_kernel,
        out_shape=jax.ShapeDtypeStruct((transfers, kc, parts, nv, naux), F32),
        in_specs=[VMEM] * len(operands),
        out_specs=VMEM,
        cost_estimate=COST,
        compiler_params=PARAMS,
    )(*operands)


def near_kernel(factor, inverse, near, total, out):
    kc, half = factor.shape[1], near.shape[2]

    def terms_of(t, k):
        return [(near[t * kc + k], inverse[t, 1, k, :, half_of(1, half)])]

    def finish(t, k, part, value):
        out[t, k, part] = value + total[t, k, part]

    contract(factor, terms_of, finish)


def far_kernel(factor, inverse, choice, *refs):
    fars, total, out = refs[:-2], refs[-2], refs[-1]
    kc, half = factor.shape[1], fars[0].shape[2]

    def terms_of(t, k):
        blocks = [fars[t][c].reshape(-1, *choice.shape[3:]) for c in range(kc)]
        chosen = [block * choice[t, k, c][None] for c, block in enumerate(blocks)]
        window = functools.reduce(jnp.add, chosen)
        return [(window.reshape(fars[t].shape[1:]), inverse[t, 2, k, :, half_of(0, half)])]

    def finish(t, k, part, value):
        out[t, k, part] = value + total[t, k, part]

    contract(factor, terms_of, finish)


def more_terms(body, operands, total):
    return pl.pallas_call(
        body,
        out_shape=jax.ShapeDtypeStruct(total.shape, F32),
        in_specs=[VMEM] * (len(operands) + 1),
        out_specs=VMEM,
        input_output_aliases={len(operands): 0},
        cost_estimate=COST,
        compiler_params=PARAMS,
    )(*operands, total)


def last_kernel(factor, inverse, window, total, out, staged, sems):
    kc, half = factor.shape[1], window.shape[2]
    copies = []

    def terms_of(t, k):
        return [(window[t * kc + k], inverse[t, 2, k, :, half_of(1, half)])]

    def finish(t, k, part, value):
        at = len(copies)
        staged[at] = (value + total[t, k, part]).astype(BF16)
        copies.append(pltpu.make_async_copy(staged.at[at], out.at[t, k, 0, part], sems.at[at]))
        copies[-1].start()

    contract(factor, terms_of, finish)
    for copy in copies:
        copy.wait()


def last_terms(factor, inverse, window, total):
    transfers, kc, _, parts, nv, naux = factor.shape
    count = transfers * kc * parts
    return pl.pallas_call(
        last_kernel,
        out_shape=jax.ShapeDtypeStruct(factor.shape, BF16),
        in_specs=[VMEM] * 4,
        out_specs=ANY,
        scratch_shapes=[
            pltpu.VMEM((count, nv, naux), BF16),
            pltpu.SemaphoreType.DMA((count,)),
        ],
        cost_estimate=COST,
        compiler_params=PARAMS,
    )(factor, inverse, window, total)


def body(factor, partner, occ_energy, vir_sorted, vir_order):
    transfers, kc = factor.shape[:2]
    bits = (0, lax.axis_size("kpt").bit_length() - 2)

    half = factor.shape[4] // 2
    part = factor[:, :, 0, :, :half].reshape(transfers * kc, *factor.shape[3:4], half, factor.shape[5])
    beside = far_swap(part)
    packs = pack(bits, after(partner, part), factor, WORK * factor.size)
    earlies, lates = packs[:transfers], packs[transfers:]
    late_own = [group_swap(lates[t], bits[t]) for t in range(transfers)]
    early_own = [group_swap(earlies[t], bits[t]) for t in range(transfers)]
    late_block = jnp.concatenate(late_own)
    late_far = far_swap(late_block)
    late_near = near_swap(late_block)
    early_block = jnp.concatenate(early_own)
    early_near = jnp.concatenate(
        [near_swap(after(early_block[:-1], beside)), near_swap(early_block[-1:])]
    )
    early_far = [group_swap(beside[t * kc : (t + 1) * kc], bits[t]) for t in range(transfers)]

    virtual = virtual_energies(vir_sorted, vir_order)
    inverse, choice = inverses(bits, partner, occ_energy, virtual, kc, factor.shape[5])
    total = first_terms(factor, inverse, early_own + late_own, early_near)
    total = more_terms(near_kernel, [factor, inverse, late_near], total)
    total = more_terms(far_kernel, [factor, inverse, choice, *early_far], total)
    return last_terms(factor, inverse, late_far, total)


def solution(mesh):
    spec = P(None, "kpt", "occ", None, None, None)
    in_specs = (spec, P(), P(), P(), P())
    return jax.shard_map(body, mesh=mesh, in_specs=in_specs, out_specs=spec, check_vma=False)
```

```python
import functools

import jax
import jax.numpy as jnp
from jax import lax
from jax.experimental import pallas as pl
from jax.experimental.pallas import tpu as pltpu
from jax.sharding import PartitionSpec as P

F32 = jnp.float32
BF16 = jnp.bfloat16
ANY = pl.BlockSpec(memory_space=pl.ANY)
VMEM = pl.BlockSpec(memory_space=pltpu.VMEM)
SMEM = pl.BlockSpec(memory_space=pltpu.SMEM)
PARAMS = pltpu.CompilerParams(vmem_limit_bytes=8 * 1024 * 1024)
WORK = 16
ROWS = 16
PIECES = 4
COST = pl.CostEstimate(flops=0, bytes_accessed=0, transcendentals=0)


def group_swap(block, bit):
    count = lax.axis_size("kpt")
    return lax.ppermute(block, "kpt", [(g, g ^ (1 << bit)) for g in range(count)])


def near_swap(block):
    count = lax.axis_size("occ")
    return lax.ppermute(block, "occ", [(i, i ^ 1) for i in range(count)])


def far_swap(block):
    count = lax.axis_size("occ")
    return lax.ppermute(
        block, "occ", [(i, (i + (1 if i % 2 else count - 1)) % count) for i in range(count)]
    )


def after(block, *others):
    return lax.optimization_barrier((block, *others))[0]


def virtual_energies(vir_sorted, vir_order):
    ranks = jnp.arange(vir_sorted.shape[1], dtype=jnp.int32)
    matches = vir_order[:, :, None] == ranks[None, None, :]
    return jnp.sum(jnp.where(matches, vir_sorted[:, None, :], 0.0), axis=2)


def column_of(row):
    return jnp.transpose(jnp.broadcast_to(row, (8, row.shape[1])))[:, :1]


def lay_kernel(factor, out, sems):
    kc, parts, half = factor.shape[1], factor.shape[3], out.shape[2]
    size = half // PIECES
    copies = []
    for at in range(out.shape[0]):
        for part in range(parts):
            for piece in range(PIECES):
                rows = pl.ds(piece * size, size)
                source = factor.at[at // kc, at % kc, 0, part, rows]
                target = out.at[at, part, rows]
                copies.append(pltpu.make_async_copy(source, target, sems.at[len(copies)]))
                copies[-1].start()
    for copy in copies:
        copy.wait()


def lay(factor):
    transfers, kc, _, parts, nv, naux = factor.shape
    return pl.pallas_call(
        lay_kernel,
        out_shape=jax.ShapeDtypeStruct((transfers * kc, parts, nv // 2, naux), BF16),
        in_specs=[ANY],
        out_specs=VMEM,
        scratch_shapes=[pltpu.SemaphoreType.DMA((transfers * kc * parts * PIECES,))],
        cost_estimate=COST,
        compiler_params=PARAMS,
    )(pltpu.with_memory_space_constraint(factor, pltpu.HBM))


def pack_kernel(bits, partner, factor, *refs):
    outs, sems = refs[:-1], refs[-1]
    kc, half = factor.shape[1], outs[0].shape[2]
    group = lax.axis_index("kpt")
    copies = []
    for h in (1, 0):
        for transfer, bit in enumerate(bits):
            far_group = jnp.bitwise_xor(group, 1 << bit)
            for k in range(kc):
                slot = partner[transfer, far_group * kc + k] - group * kc
                source = factor.at[transfer, slot, 0, :, pl.ds(h * half, half), :]
                target = outs[h * len(bits) + transfer].at[k]
                copies.append(pltpu.make_async_copy(source, target, sems.at[len(copies)]))
                copies[-1].start()
    for copy in copies:
        copy.wait()


def pack(bits, partner, factor, work):
    transfers, kc, _, parts, nv, naux = factor.shape
    return pl.pallas_call(
        functools.partial(pack_kernel, bits),
        out_shape=[jax.ShapeDtypeStruct((kc, parts, nv // 2, naux), BF16)] * (2 * transfers),
        in_specs=[SMEM, ANY],
        out_specs=[VMEM] * (2 * transfers),
        scratch_shapes=[pltpu.SemaphoreType.DMA((2 * transfers * kc,))],
        cost_estimate=pl.CostEstimate(flops=0, bytes_accessed=work, transcendentals=0),
        compiler_params=PARAMS,
    )(
        pltpu.with_memory_space_constraint(partner, pltpu.HBM),
        pltpu.with_memory_space_constraint(factor, pltpu.HBM),
    )


def inverse_kernel(bits, partner, occ, virtual, out, choice):
    _, _, kc, nv, _ = out.shape
    total = occ.shape[1]
    group, orbit = lax.axis_index("kpt"), lax.axis_index("occ")
    parity = lax.rem(orbit, 2)
    columns = (orbit, orbit + 1 - 2 * parity, lax.rem(orbit + total - 1 + 2 * parity, total))

    def point_step(k, carry):
        point = group * kc + k
        row = virtual[pl.ds(point, 1), :]
        for transfer in range(len(bits)):
            far_point = partner[transfer, point]
            column = column_of(virtual[pl.ds(far_point, 1), :])
            slot = far_point - jnp.bitwise_xor(group, 1 << bits[transfer]) * kc
            for c in range(kc):
                chosen = jnp.where(slot == c, 1.0, 0.0)
                choice[transfer, k, c] = jnp.full(choice.shape[3:], chosen, F32).astype(BF16)
            for place, index in enumerate(columns):
                level = occ[point, orbit] + occ[far_point, index]
                out[transfer, place, k] = 1.0 / ((level - column) - row)
        return carry

    lax.fori_loop(0, kc, point_step, 0)


def inverses(bits, partner, occ_energy, virtual, kc, naux):
    nv = virtual.shape[1]
    return pl.pallas_call(
        functools.partial(inverse_kernel, bits),
        out_shape=[
            jax.ShapeDtypeStruct((len(bits), 3, kc, nv, nv), F32),
            jax.ShapeDtypeStruct((len(bits), kc, kc, ROWS, naux), BF16),
        ],
        in_specs=[SMEM, SMEM, VMEM],
        out_specs=[VMEM, VMEM],
        cost_estimate=COST,
        compiler_params=PARAMS,
    )(partner, occ_energy, virtual)


def amplitude_rows(own, terms):
    _, nv, naux = own.shape
    left = own.reshape(2 * nv, naux)
    rows, blocks = ([], []), []
    for window, inverse in terms:
        size = window.shape[1]
        window = window.reshape(2 * size, naux)
        products = lax.dot_general(
            left, window, (((1,), (1,)), ((), ())), preferred_element_type=F32
        )
        real_part = ((products[:nv, :size] + products[nv:, size:]) * inverse).astype(BF16)
        imag_part = ((products[nv:, :size] - products[:nv, size:]) * inverse).astype(BF16)
        rows[0].extend([real_part, -imag_part])
        rows[1].extend([imag_part, real_part])
        blocks.append(window)
    return [jnp.concatenate(part, axis=1) for part in rows], jnp.concatenate(blocks, axis=0)


def contract(factor, terms_of, finish):
    waiting = None
    points = [(t, k) for t in range(factor.shape[0]) for k in range(factor.shape[1])]
    for point in [*points, None]:
        ready, waiting = waiting, None
        if point is not None:
            t, k = point
            waiting = (t, k, *amplitude_rows(factor[t, k, 0], terms_of(t, k)))
        if ready is not None:
            t, k, rows, blocks = ready
            for part in range(2):
                finish(t, k, part, jnp.dot(rows[part], blocks, preferred_element_type=F32))


def half_of(h, half):
    return slice(h * half, (h + 1) * half)


def first_kernel(factor, inverse, *refs):
    transfers, kc = factor.shape[:2]
    owns, near, out = refs[: 2 * transfers], refs[-2], refs[-1]
    first, second = half_of(0, near.shape[2]), half_of(1, near.shape[2])

    def terms_of(t, k):
        return [
            (owns[t][k], inverse[t, 0, k, :, first]),
            (owns[transfers + t][k], inverse[t, 0, k, :, second]),
            (near[t * kc + k], inverse[t, 1, k, :, first]),
        ]

    def finish(t, k, part, value):
        out[t, k, part] = value

    contract(factor, terms_of, finish)


def first_terms(factor, inverse, owns, near):
    transfers, kc, _, parts, nv, naux = factor.shape
    operands = [factor, inverse, *owns, near]
    return pl.pallas_call(
        first_kernel,
        out_shape=jax.ShapeDtypeStruct((transfers, kc, parts, nv, naux), F32),
        in_specs=[VMEM] * len(operands),
        out_specs=VMEM,
        cost_estimate=COST,
        compiler_params=PARAMS,
    )(*operands)


def near_kernel(factor, inverse, near, total, out):
    kc, half = factor.shape[1], near.shape[2]

    def terms_of(t, k):
        return [(near[t * kc + k], inverse[t, 1, k, :, half_of(1, half)])]

    def finish(t, k, part, value):
        out[t, k, part] = value + total[t, k, part]

    contract(factor, terms_of, finish)


def far_kernel(factor, inverse, choice, *refs):
    fars, total, out = refs[:-2], refs[-2], refs[-1]
    kc, half = factor.shape[1], fars[0].shape[2]

    def terms_of(t, k):
        blocks = [fars[t][c].reshape(-1, *choice.shape[3:]) for c in range(kc)]
        chosen = [block * choice[t, k, c][None] for c, block in enumerate(blocks)]
        window = functools.reduce(jnp.add, chosen)
        return [(window.reshape(fars[t].shape[1:]), inverse[t, 2, k, :, half_of(0, half)])]

    def finish(t, k, part, value):
        out[t, k, part] = value + total[t, k, part]

    contract(factor, terms_of, finish)


def more_terms(body, operands, total):
    return pl.pallas_call(
        body,
        out_shape=jax.ShapeDtypeStruct(total.shape, F32),
        in_specs=[VMEM] * (len(operands) + 1),
        out_specs=VMEM,
        input_output_aliases={len(operands): 0},
        cost_estimate=COST,
        compiler_params=PARAMS,
    )(*operands, total)


def last_kernel(factor, inverse, window, total, out, staged, sems):
    kc, half = factor.shape[1], window.shape[2]
    copies = []

    def terms_of(t, k):
        return [(window[t * kc + k], inverse[t, 2, k, :, half_of(1, half)])]

    def finish(t, k, part, value):
        at = (t * kc + k) * 2 + part
        size = value.shape[0] // PIECES
        for piece in range(PIECES):
            rows = slice(piece * size, (piece + 1) * size)
            staged[at, rows] = (value[rows] + total[t, k, part, rows]).astype(BF16)
            target = out.at[t, k, 0, part, pl.ds(piece * size, size)]
            source = staged.at[at, pl.ds(piece * size, size)]
            copies.append(pltpu.make_async_copy(source, target, sems.at[len(copies)]))
            copies[-1].start()

    contract(factor, terms_of, finish)
    for copy in copies:
        copy.wait()


def last_terms(factor, inverse, window, total):
    transfers, kc, _, parts, nv, naux = factor.shape
    count = transfers * kc * parts
    return pl.pallas_call(
        last_kernel,
        out_shape=jax.ShapeDtypeStruct(factor.shape, BF16),
        in_specs=[VMEM] * 4,
        out_specs=ANY,
        scratch_shapes=[
            pltpu.VMEM((count, nv, naux), BF16),
            pltpu.SemaphoreType.DMA((count * PIECES,)),
        ],
        cost_estimate=COST,
        compiler_params=PARAMS,
    )(factor, inverse, window, total)


def body(factor, partner, occ_energy, vir_sorted, vir_order):
    transfers, kc = factor.shape[:2]
    bits = (0, lax.axis_size("kpt").bit_length() - 2)

    part = lay(factor)
    beside = far_swap(part)
    packs = pack(bits, after(partner, part), factor, WORK * factor.size)
    earlies, lates = packs[:transfers], packs[transfers:]
    late_own = [group_swap(lates[t], bits[t]) for t in range(transfers)]
    early_own = [group_swap(earlies[t], bits[t]) for t in range(transfers)]
    late_block = jnp.concatenate(late_own)
    late_far = far_swap(late_block)
    late_near = near_swap(late_block)
    early_block = jnp.concatenate(early_own)
    early_near = jnp.concatenate(
        [near_swap(after(early_block[:-1], beside)), near_swap(early_block[-1:])]
    )
    early_far = [group_swap(beside[t * kc : (t + 1) * kc], bits[t]) for t in range(transfers)]

    virtual = virtual_energies(vir_sorted, vir_order)
    inverse, choice = inverses(bits, partner, occ_energy, virtual, kc, factor.shape[5])
    total = first_terms(factor, inverse, early_own + late_own, early_near)
    total = more_terms(near_kernel, [factor, inverse, late_near], total)
    total = more_terms(far_kernel, [factor, inverse, choice, *early_far], total)
    return last_terms(factor, inverse, late_far, total)


def solution(mesh):
    spec = P(None, "kpt", "occ", None, None, None)
    in_specs = (spec, P(), P(), P(), P())
    return jax.shard_map(body, mesh=mesh, in_specs=in_specs, out_specs=spec, check_vma=False)
```

```python
import functools

import jax
import jax.numpy as jnp
from jax import lax
from jax.experimental import pallas as pl
from jax.experimental.pallas import tpu as pltpu
from jax.sharding import PartitionSpec as P

F32 = jnp.float32
BF16 = jnp.bfloat16
ANY = pl.BlockSpec(memory_space=pl.ANY)
VMEM = pl.BlockSpec(memory_space=pltpu.VMEM)
SMEM = pl.BlockSpec(memory_space=pltpu.SMEM)
PARAMS = pltpu.CompilerParams(vmem_limit_bytes=8 * 1024 * 1024)
WORK = 16
ROWS = 16
COST = pl.CostEstimate(flops=0, bytes_accessed=0, transcendentals=0)


def group_swap(block, bit):
    count = lax.axis_size("kpt")
    return lax.ppermute(block, "kpt", [(g, g ^ (1 << bit)) for g in range(count)])


def near_swap(block):
    count = lax.axis_size("occ")
    return lax.ppermute(block, "occ", [(i, i ^ 1) for i in range(count)])


def far_swap(block):
    count = lax.axis_size("occ")
    return lax.ppermute(
        block, "occ", [(i, (i + (1 if i % 2 else count - 1)) % count) for i in range(count)]
    )


def after(block, *others):
    return lax.optimization_barrier((block, *others))[0]


def virtual_energies(vir_sorted, vir_order):
    ranks = jnp.arange(vir_sorted.shape[1], dtype=jnp.int32)
    matches = vir_order[:, :, None] == ranks[None, None, :]
    return jnp.sum(jnp.where(matches, vir_sorted[:, None, :], 0.0), axis=2)


def column_of(row):
    return jnp.transpose(jnp.broadcast_to(row, (8, row.shape[1])))[:, :1]


def lay_kernel(factor, out, sem):
    copy = pltpu.make_async_copy(factor.at[:, :, 0, :, pl.ds(0, out.shape[3]), :], out, sem)
    copy.start()
    copy.wait()


def lay(factor):
    transfers, kc, _, parts, nv, naux = factor.shape
    part = pl.pallas_call(
        lay_kernel,
        out_shape=jax.ShapeDtypeStruct((transfers, kc, parts, nv // 2, naux), BF16),
        in_specs=[ANY],
        out_specs=VMEM,
        scratch_shapes=[pltpu.SemaphoreType.DMA],
        cost_estimate=COST,
        compiler_params=PARAMS,
    )(pltpu.with_memory_space_constraint(factor, pltpu.HBM))
    return part.reshape(transfers * kc, parts, nv // 2, naux)


def pack_kernel(bits, partner, factor, *refs):
    outs, sems = refs[:-1], refs[-1]
    kc, half = factor.shape[1], outs[0].shape[2]
    group = lax.axis_index("kpt")
    copies = []
    for h in (1, 0):
        for transfer, bit in enumerate(bits):
            far_group = jnp.bitwise_xor(group, 1 << bit)
            for k in range(kc):
                slot = partner[transfer, far_group * kc + k] - group * kc
                source = factor.at[transfer, slot, 0, :, pl.ds(h * half, half), :]
                target = outs[h * len(bits) + transfer].at[k]
                copies.append(pltpu.make_async_copy(source, target, sems.at[len(copies)]))
                copies[-1].start()
    for copy in copies:
        copy.wait()


def pack(bits, partner, factor, work):
    transfers, kc, _, parts, nv, naux = factor.shape
    return pl.pallas_call(
        functools.partial(pack_kernel, bits),
        out_shape=[jax.ShapeDtypeStruct((kc, parts, nv // 2, naux), BF16)] * (2 * transfers),
        in_specs=[SMEM, ANY],
        out_specs=[VMEM] * (2 * transfers),
        scratch_shapes=[pltpu.SemaphoreType.DMA((2 * transfers * kc,))],
        cost_estimate=pl.CostEstimate(flops=0, bytes_accessed=work, transcendentals=0),
        compiler_params=PARAMS,
    )(
        pltpu.with_memory_space_constraint(partner, pltpu.HBM),
        pltpu.with_memory_space_constraint(factor, pltpu.HBM),
    )


def inverse_kernel(bits, partner, occ, virtual, out, choice):
    _, _, kc, nv, _ = out.shape
    total = occ.shape[1]
    group, orbit = lax.axis_index("kpt"), lax.axis_index("occ")
    parity = lax.rem(orbit, 2)
    columns = (orbit, orbit + 1 - 2 * parity, lax.rem(orbit + total - 1 + 2 * parity, total))

    def point_step(k, carry):
        point = group * kc + k
        row = virtual[pl.ds(point, 1), :]
        for transfer in range(len(bits)):
            far_point = partner[transfer, point]
            column = column_of(virtual[pl.ds(far_point, 1), :])
            slot = far_point - jnp.bitwise_xor(group, 1 << bits[transfer]) * kc
            for c in range(kc):
                chosen = jnp.where(slot == c, 1.0, 0.0)
                choice[transfer, k, c] = jnp.full(choice.shape[3:], chosen, F32).astype(BF16)
            for place, index in enumerate(columns):
                level = occ[point, orbit] + occ[far_point, index]
                out[transfer, place, k] = 1.0 / ((level - column) - row)
        return carry

    lax.fori_loop(0, kc, point_step, 0)


def inverses(bits, partner, occ_energy, virtual, kc, naux):
    nv = virtual.shape[1]
    return pl.pallas_call(
        functools.partial(inverse_kernel, bits),
        out_shape=[
            jax.ShapeDtypeStruct((len(bits), 3, kc, nv, nv), F32),
            jax.ShapeDtypeStruct((len(bits), kc, kc, ROWS, naux), BF16),
        ],
        in_specs=[SMEM, SMEM, VMEM],
        out_specs=[VMEM, VMEM],
        cost_estimate=COST,
        compiler_params=PARAMS,
    )(partner, occ_energy, virtual)


def amplitude_rows(own, terms):
    _, nv, naux = own.shape
    left = own.reshape(2 * nv, naux)
    rows, blocks = ([], []), []
    for window, inverse in terms:
        size = window.shape[1]
        window = window.reshape(2 * size, naux)
        products = lax.dot_general(
            left, window, (((1,), (1,)), ((), ())), preferred_element_type=F32
        )
        real_part = ((products[:nv, :size] + products[nv:, size:]) * inverse).astype(BF16)
        imag_part = ((products[nv:, :size] - products[:nv, size:]) * inverse).astype(BF16)
        rows[0].extend([real_part, -imag_part])
        rows[1].extend([imag_part, real_part])
        blocks.append(window)
    return [jnp.concatenate(part, axis=1) for part in rows], jnp.concatenate(blocks, axis=0)


def contract(factor, terms_of, finish):
    waiting = None
    points = [(t, k) for t in range(factor.shape[0]) for k in range(factor.shape[1])]
    for point in [*points, None]:
        ready, waiting = waiting, None
        if point is not None:
            t, k = point
            waiting = (t, k, *amplitude_rows(factor[t, k, 0], terms_of(t, k)))
        if ready is not None:
            t, k, rows, blocks = ready
            for part in range(2):
                finish(t, k, part, jnp.dot(rows[part], blocks, preferred_element_type=F32))


def half_of(h, half):
    return slice(h * half, (h + 1) * half)


def first_kernel(factor, inverse, *refs):
    transfers, kc = factor.shape[:2]
    owns, near, out = refs[: 2 * transfers], refs[-2], refs[-1]
    first, second = half_of(0, near.shape[2]), half_of(1, near.shape[2])

    def terms_of(t, k):
        return [
            (owns[t][k], inverse[t, 0, k, :, first]),
            (owns[transfers + t][k], inverse[t, 0, k, :, second]),
            (near[t * kc + k], inverse[t, 1, k, :, first]),
        ]

    def finish(t, k, part, value):
        out[t, k, part] = value

    contract(factor, terms_of, finish)


def first_terms(factor, inverse, owns, near):
    transfers, kc, _, parts, nv, naux = factor.shape
    operands = [factor, inverse, *owns, near]
    return pl.pallas_call(
        first_kernel,
        out_shape=jax.ShapeDtypeStruct((transfers, kc, parts, nv, naux), F32),
        in_specs=[VMEM] * len(operands),
        out_specs=VMEM,
        cost_estimate=COST,
        compiler_params=PARAMS,
    )(*operands)


def near_kernel(factor, inverse, near, total, out):
    kc, half = factor.shape[1], near.shape[2]

    def terms_of(t, k):
        return [(near[t * kc + k], inverse[t, 1, k, :, half_of(1, half)])]

    def finish(t, k, part, value):
        out[t, k, part] = value + total[t, k, part]

    contract(factor, terms_of, finish)


def far_kernel(factor, inverse, choice, *refs):
    fars, total, out = refs[:-2], refs[-2], refs[-1]
    kc, half = factor.shape[1], fars[0].shape[2]

    def terms_of(t, k):
        blocks = [fars[t][c].reshape(-1, *choice.shape[3:]) for c in range(kc)]
        chosen = [block * choice[t, k, c][None] for c, block in enumerate(blocks)]
        window = functools.reduce(jnp.add, chosen)
        return [(window.reshape(fars[t].shape[1:]), inverse[t, 2, k, :, half_of(0, half)])]

    def finish(t, k, part, value):
        out[t, k, part] = value + total[t, k, part]

    contract(factor, terms_of, finish)


def more_terms(body, operands, total):
    return pl.pallas_call(
        body,
        out_shape=jax.ShapeDtypeStruct(total.shape, F32),
        in_specs=[VMEM] * (len(operands) + 1),
        out_specs=VMEM,
        input_output_aliases={len(operands): 0},
        cost_estimate=COST,
        compiler_params=PARAMS,
    )(*operands, total)


def last_kernel(factor, inverse, window, total, out, staged, sems):
    transfers, kc = factor.shape[:2]
    half = window.shape[2]

    def copy_out(t, k):
        return pltpu.make_async_copy(staged.at[t, k], out.at[t, k, 0], sems.at[t, k])

    def point_step(k, carry):
        waiting = []
        for t in range(transfers):
            terms = [(window[t * kc + k], inverse[t, 2, k, :, half_of(1, half)])]
            waiting.append(amplitude_rows(factor[t, k, 0], terms))
        for t, (rows, blocks) in enumerate(waiting):
            for part in range(2):
                value = jnp.dot(rows[part], blocks, preferred_element_type=F32)
                staged[t, k, part] = (value + total[t, k, part]).astype(BF16)
            copy_out(t, k).start()
        return carry

    lax.fori_loop(0, kc, point_step, 0)
    for t in range(transfers):
        for k in range(kc):
            copy_out(t, k).wait()


def last_terms(factor, inverse, window, total):
    transfers, kc, _, parts, nv, naux = factor.shape
    return pl.pallas_call(
        last_kernel,
        out_shape=jax.ShapeDtypeStruct(factor.shape, BF16),
        in_specs=[VMEM] * 4,
        out_specs=ANY,
        scratch_shapes=[
            pltpu.VMEM((transfers, kc, parts, nv, naux), BF16),
            pltpu.SemaphoreType.DMA((transfers, kc)),
        ],
        cost_estimate=COST,
        compiler_params=PARAMS,
    )(factor, inverse, window, total)


def body(factor, partner, occ_energy, vir_sorted, vir_order):
    transfers, kc = factor.shape[:2]
    bits = (0, lax.axis_size("kpt").bit_length() - 2)

    part = lay(factor)
    beside = far_swap(part)
    packs = pack(bits, after(partner, part), factor, WORK * factor.size)
    earlies, lates = packs[:transfers], packs[transfers:]
    late_own = [group_swap(lates[t], bits[t]) for t in range(transfers)]
    early_own = [group_swap(earlies[t], bits[t]) for t in range(transfers)]
    late_block = jnp.concatenate(late_own)
    late_far = far_swap(late_block)
    late_near = near_swap(late_block)
    early_block = jnp.concatenate(early_own)
    early_near = jnp.concatenate(
        [near_swap(after(early_block[:-1], beside)), near_swap(early_block[-1:])]
    )
    early_far = [group_swap(beside[t * kc : (t + 1) * kc], bits[t]) for t in range(transfers)]

    virtual = virtual_energies(vir_sorted, vir_order)
    inverse, choice = inverses(bits, partner, occ_energy, virtual, kc, factor.shape[5])
    total = first_terms(factor, inverse, early_own + late_own, early_near)
    total = more_terms(near_kernel, [factor, inverse, late_near], total)
    total = more_terms(far_kernel, [factor, inverse, choice, *early_far], total)
    return last_terms(factor, inverse, late_far, total)


def solution(mesh):
    spec = P(None, "kpt", "occ", None, None, None)
    in_specs = (spec, P(), P(), P(), P())
    return jax.shard_map(body, mesh=mesh, in_specs=in_specs, out_specs=spec, check_vma=False)
```

```python
import functools

import jax
import jax.numpy as jnp
from jax import lax
from jax.experimental import pallas as pl
from jax.experimental.pallas import tpu as pltpu
from jax.sharding import PartitionSpec as P

F32 = jnp.float32
BF16 = jnp.bfloat16
ANY = pl.BlockSpec(memory_space=pl.ANY)
VMEM = pl.BlockSpec(memory_space=pltpu.VMEM)
SMEM = pl.BlockSpec(memory_space=pltpu.SMEM)
PARAMS = pltpu.CompilerParams(vmem_limit_bytes=8 * 1024 * 1024)
WORK = 16
ROWS = 16
COST = pl.CostEstimate(flops=0, bytes_accessed=0, transcendentals=0)


def group_swap(block, bit):
    count = lax.axis_size("kpt")
    return lax.ppermute(block, "kpt", [(g, g ^ (1 << bit)) for g in range(count)])


def near_swap(block):
    count = lax.axis_size("occ")
    return lax.ppermute(block, "occ", [(i, i ^ 1) for i in range(count)])


def far_swap(block):
    count = lax.axis_size("occ")
    return lax.ppermute(
        block, "occ", [(i, (i + (1 if i % 2 else count - 1)) % count) for i in range(count)]
    )


def after(block, *others):
    return lax.optimization_barrier((block, *others))[0]


def virtual_energies(vir_sorted, vir_order):
    ranks = jnp.arange(vir_sorted.shape[1], dtype=jnp.int32)
    matches = vir_order[:, :, None] == ranks[None, None, :]
    return jnp.sum(jnp.where(matches, vir_sorted[:, None, :], 0.0), axis=2)


def column_of(row):
    return jnp.transpose(jnp.broadcast_to(row, (8, row.shape[1])))[:, :1]


def lay_kernel(factor, out, sems):
    kc, half = factor.shape[1], out.shape[2]
    copies = []
    for at in range(out.shape[0]):
        source = factor.at[at // kc, at % kc, 0, :, pl.ds(0, half), :]
        copies.append(pltpu.make_async_copy(source, out.at[at], sems.at[at]))
        copies[-1].start()
    for copy in copies:
        copy.wait()


def lay(factor):
    transfers, kc, _, parts, nv, naux = factor.shape
    return pl.pallas_call(
        lay_kernel,
        out_shape=jax.ShapeDtypeStruct((transfers * kc, parts, nv // 2, naux), BF16),
        in_specs=[ANY],
        out_specs=VMEM,
        scratch_shapes=[pltpu.SemaphoreType.DMA((transfers * kc,))],
        cost_estimate=COST,
        compiler_params=PARAMS,
    )(pltpu.with_memory_space_constraint(factor, pltpu.HBM))


def pack_kernel(bits, partner, factor, *refs):
    outs, sems = refs[:-1], refs[-1]
    kc, half = factor.shape[1], outs[0].shape[2]
    group = lax.axis_index("kpt")
    copies = []
    for h in (1, 0):
        for transfer, bit in enumerate(bits):
            far_group = jnp.bitwise_xor(group, 1 << bit)
            for k in range(kc):
                slot = partner[transfer, far_group * kc + k] - group * kc
                source = factor.at[transfer, slot, 0, :, pl.ds(h * half, half), :]
                target = outs[h * len(bits) + transfer].at[k]
                copies.append(pltpu.make_async_copy(source, target, sems.at[len(copies)]))
                copies[-1].start()
    for copy in copies:
        copy.wait()


def pack(bits, partner, factor, work):
    transfers, kc, _, parts, nv, naux = factor.shape
    return pl.pallas_call(
        functools.partial(pack_kernel, bits),
        out_shape=[jax.ShapeDtypeStruct((kc, parts, nv // 2, naux), BF16)] * (2 * transfers),
        in_specs=[SMEM, ANY],
        out_specs=[VMEM] * (2 * transfers),
        scratch_shapes=[pltpu.SemaphoreType.DMA((2 * transfers * kc,))],
        cost_estimate=pl.CostEstimate(flops=0, bytes_accessed=work, transcendentals=0),
        compiler_params=PARAMS,
    )(
        pltpu.with_memory_space_constraint(partner, pltpu.HBM),
        pltpu.with_memory_space_constraint(factor, pltpu.HBM),
    )


def inverse_kernel(bits, partner, occ, virtual, out, choice):
    _, _, kc, nv, _ = out.shape
    total = occ.shape[1]
    group, orbit = lax.axis_index("kpt"), lax.axis_index("occ")
    parity = lax.rem(orbit, 2)
    columns = (orbit, orbit + 1 - 2 * parity, lax.rem(orbit + total - 1 + 2 * parity, total))

    def point_step(k, carry):
        point = group * kc + k
        row = virtual[pl.ds(point, 1), :]
        for transfer in range(len(bits)):
            far_point = partner[transfer, point]
            column = column_of(virtual[pl.ds(far_point, 1), :])
            slot = far_point - jnp.bitwise_xor(group, 1 << bits[transfer]) * kc
            for c in range(kc):
                chosen = jnp.where(slot == c, 1.0, 0.0)
                choice[transfer, k, c] = jnp.full(choice.shape[3:], chosen, F32).astype(BF16)
            for place, index in enumerate(columns):
                level = occ[point, orbit] + occ[far_point, index]
                out[transfer, place, k] = 1.0 / ((level - column) - row)
        return carry

    lax.fori_loop(0, kc, point_step, 0)


def inverses(bits, partner, occ_energy, virtual, kc, naux):
    nv = virtual.shape[1]
    return pl.pallas_call(
        functools.partial(inverse_kernel, bits),
        out_shape=[
            jax.ShapeDtypeStruct((len(bits), 3, kc, nv, nv), F32),
            jax.ShapeDtypeStruct((len(bits), kc, kc, ROWS, naux), BF16),
        ],
        in_specs=[SMEM, SMEM, VMEM],
        out_specs=[VMEM, VMEM],
        cost_estimate=COST,
        compiler_params=PARAMS,
    )(partner, occ_energy, virtual)


def amplitude_rows(own, terms):
    _, nv, naux = own.shape
    left = own.reshape(2 * nv, naux)
    rows, blocks = ([], []), []
    for window, inverse in terms:
        size = window.shape[1]
        window = window.reshape(2 * size, naux)
        products = lax.dot_general(
            left, window, (((1,), (1,)), ((), ())), preferred_element_type=F32
        )
        real_part = ((products[:nv, :size] + products[nv:, size:]) * inverse).astype(BF16)
        imag_part = ((products[nv:, :size] - products[:nv, size:]) * inverse).astype(BF16)
        rows[0].extend([real_part, -imag_part])
        rows[1].extend([imag_part, real_part])
        blocks.append(window)
    return [jnp.concatenate(part, axis=1) for part in rows], jnp.concatenate(blocks, axis=0)


def contract(factor, terms_of, finish):
    waiting = None
    points = [(t, k) for t in range(factor.shape[0]) for k in range(factor.shape[1])]
    for point in [*points, None]:
        ready, waiting = waiting, None
        if point is not None:
            t, k = point
            terms = terms_of(t, k)
            waiting = (t, k, *amplitude_rows(factor[t, k, 0], terms)) if terms else None
        if ready is not None:
            t, k, rows, blocks = ready
            for part in range(2):
                finish(t, k, part, jnp.dot(rows[part], blocks, preferred_element_type=F32))


def half_of(h, half):
    return slice(h * half, (h + 1) * half)


def first_kernel(factor, inverse, *refs):
    transfers, kc = factor.shape[:2]
    owns, near, out = refs[: 2 * transfers], refs[-2], refs[-1]
    first, second = half_of(0, near.shape[2]), half_of(1, near.shape[2])

    def terms_of(t, k):
        return [
            (owns[t][k], inverse[t, 0, k, :, first]),
            (owns[transfers + t][k], inverse[t, 0, k, :, second]),
            (near[t * kc + k], inverse[t, 1, k, :, second]),
        ]

    def finish(t, k, part, value):
        out[t, k, part] = value

    contract(factor, terms_of, finish)


def first_terms(factor, inverse, owns, near):
    transfers, kc, _, parts, nv, naux = factor.shape
    operands = [factor, inverse, *owns, near]
    return pl.pallas_call(
        first_kernel,
        out_shape=jax.ShapeDtypeStruct((transfers, kc, parts, nv, naux), F32),
        in_specs=[VMEM] * len(operands),
        out_specs=VMEM,
        cost_estimate=COST,
        compiler_params=PARAMS,
    )(*operands)


def add_kernel(place, h, factor, inverse, window, total, out):
    kc, half = factor.shape[1], window.shape[2]

    def terms_of(t, k):
        at = t * kc + k
        known = at < window.shape[0]
        return [(window[at], inverse[t, place, k, :, half_of(h, half)])] if known else []

    def finish(t, k, part, value):
        out[t, k, part] = value + total[t, k, part]

    contract(factor, terms_of, finish)


def add_terms(place, h, factor, inverse, window, total, cost):
    return pl.pallas_call(
        functools.partial(add_kernel, place, h),
        out_shape=jax.ShapeDtypeStruct(total.shape, F32),
        in_specs=[VMEM] * 4,
        out_specs=VMEM,
        input_output_aliases={3: 0},
        cost_estimate=cost,
        compiler_params=PARAMS,
    )(factor, inverse, window, total)


def far_kernel(done, factor, inverse, choice, *refs):
    fars, (total, kept, out, staged, sems) = refs[:-5], refs[-5:]
    kc, half = factor.shape[1], fars[0].shape[2]
    copies = []

    def terms_of(t, k):
        blocks = [fars[t][c].reshape(-1, *choice.shape[3:]) for c in range(kc)]
        chosen = [block * choice[t, k, c][None] for c, block in enumerate(blocks)]
        window = functools.reduce(jnp.add, chosen).reshape(fars[t].shape[1:])
        return [(window, inverse[t, 2, k, :, half_of(0, half)])]

    def finish(t, k, part, value):
        value = value + total[t, k, part]
        if t * kc + k < done:
            send_part(copies, value, out.at[t, k, 0, part], staged, sems)
        else:
            kept[t, k, part] = value

    contract(factor, terms_of, finish)
    for copy in copies:
        copy.wait()


def send_part(copies, value, target, staged, sems):
    at = len(copies)
    staged[at] = value.astype(BF16)
    copies.append(pltpu.make_async_copy(staged.at[at], target, sems.at[at]))
    copies[-1].start()


def out_scratch(count, nv, naux):
    return [pltpu.VMEM((count, nv, naux), BF16), pltpu.SemaphoreType.DMA((count,))]


def far_terms(done, factor, inverse, choice, fars, total):
    _, _, _, parts, nv, naux = factor.shape
    operands = [factor, inverse, choice, *fars, total]
    return pl.pallas_call(
        functools.partial(far_kernel, done),
        out_shape=[
            jax.ShapeDtypeStruct(total.shape, F32),
            jax.ShapeDtypeStruct(factor.shape, BF16),
        ],
        in_specs=[VMEM] * len(operands),
        out_specs=[VMEM, ANY],
        scratch_shapes=out_scratch(done * parts, nv, naux),
        input_output_aliases={len(operands) - 1: 0},
        cost_estimate=COST,
        compiler_params=PARAMS,
    )(*operands)


def last_kernel(done, factor, inverse, window, total, _, out, staged, sems):
    kc, half = factor.shape[1], window.shape[2]
    copies = []

    def terms_of(t, k):
        at = t * kc + k - done
        return [(window[at], inverse[t, 2, k, :, half_of(1, half)])] if at >= 0 else []

    def finish(t, k, part, value):
        value = value + total[t, k, part]
        send_part(copies, value, out.at[t, k, 0, part], staged, sems)

    contract(factor, terms_of, finish)
    for copy in copies:
        copy.wait()


def last_terms(done, factor, inverse, window, total, result):
    transfers, kc, _, parts, nv, naux = factor.shape
    return pl.pallas_call(
        functools.partial(last_kernel, done),
        out_shape=jax.ShapeDtypeStruct(factor.shape, BF16),
        in_specs=[VMEM] * 4 + [ANY],
        out_specs=ANY,
        scratch_shapes=out_scratch((transfers * kc - done) * parts, nv, naux),
        input_output_aliases={4: 0},
        cost_estimate=COST,
        compiler_params=PARAMS,
    )(factor, inverse, window, total, result)


def last_rows(block, count, work):
    def copy_kernel(source, out):
        out[...] = source[source.shape[0] - count :]

    return pl.pallas_call(
        copy_kernel,
        out_shape=jax.ShapeDtypeStruct((count, *block.shape[1:]), block.dtype),
        in_specs=[VMEM],
        out_specs=VMEM,
        cost_estimate=pl.CostEstimate(flops=work, bytes_accessed=0, transcendentals=0),
        compiler_params=PARAMS,
    )(block)


def body(factor, partner, occ_energy, vir_sorted, vir_order):
    transfers, kc = factor.shape[:2]
    bits = (0, lax.axis_size("kpt").bit_length() - 2)

    part = lay(factor)
    beside = far_swap(part)
    packs = pack(bits, after(partner, part), factor, WORK * factor.size)
    earlies, lates = packs[:transfers], packs[transfers:]
    virtual = virtual_energies(vir_sorted, vir_order)
    inverse, choice = inverses(bits, partner, occ_energy, virtual, kc, factor.shape[5])
    late_own = [group_swap(lates[t], bits[t]) for t in range(transfers)]
    early_own = [group_swap(after(earlies[t], choice), bits[t]) for t in range(transfers)]
    late_block = jnp.concatenate(late_own)
    done = late_block.shape[0] - 1
    late_far, last_far = far_swap(late_block[:done]), far_swap(after(late_block[done:], beside))
    late_near = jnp.concatenate([near_swap(late_block[:3]), near_swap(last_rows(late_block, 1, 6000 * factor.size))])
    early_block = jnp.concatenate(early_own)
    early_near = jnp.concatenate(
        [near_swap(after(early_block[:2], beside)), near_swap(after(early_block[2:], beside))]
    )
    early_far = [group_swap(beside[t * kc : (t + 1) * kc], bits[t]) for t in range(transfers)]

    total = first_terms(factor, inverse, early_own + late_own, late_near)
    total = add_terms(1, 0, factor, inverse, early_near, total, COST)
    weight = pl.CostEstimate(flops=3 * 1000 * factor.size, bytes_accessed=0, transcendentals=0)
    total = add_terms(2, 1, factor, inverse, late_far, total, weight)
    total, result = far_terms(done, factor, inverse, choice, early_far, total)
    return last_terms(done, factor, inverse, last_far, total, result)


def solution(mesh):
    spec = P(None, "kpt", "occ", None, None, None)
    in_specs = (spec, P(), P(), P(), P())
    return jax.shard_map(body, mesh=mesh, in_specs=in_specs, out_specs=spec, check_vma=False)
```

```python
import functools

import jax
import jax.numpy as jnp
from jax import lax
from jax.experimental import pallas as pl
from jax.experimental.pallas import tpu as pltpu
from jax.sharding import PartitionSpec as P

F32 = jnp.float32
BF16 = jnp.bfloat16
ANY = pl.BlockSpec(memory_space=pl.ANY)
VMEM = pl.BlockSpec(memory_space=pltpu.VMEM)
SMEM = pl.BlockSpec(memory_space=pltpu.SMEM)
PARAMS = pltpu.CompilerParams(vmem_limit_bytes=8 * 1024 * 1024)
WORK = 16
ROWS = 16
COST = pl.CostEstimate(flops=0, bytes_accessed=0, transcendentals=0)


def group_swap(block, bit):
    count = lax.axis_size("kpt")
    return lax.ppermute(block, "kpt", [(g, g ^ (1 << bit)) for g in range(count)])


def near_swap(block):
    count = lax.axis_size("occ")
    return lax.ppermute(block, "occ", [(i, i ^ 1) for i in range(count)])


def far_swap(block):
    count = lax.axis_size("occ")
    return lax.ppermute(
        block, "occ", [(i, (i + (1 if i % 2 else count - 1)) % count) for i in range(count)]
    )


def after(block, *others):
    return lax.optimization_barrier((block, *others))[0]


def virtual_energies(vir_sorted, vir_order):
    ranks = jnp.arange(vir_sorted.shape[1], dtype=jnp.int32)
    matches = vir_order[:, :, None] == ranks[None, None, :]
    return jnp.sum(jnp.where(matches, vir_sorted[:, None, :], 0.0), axis=2)


def column_of(row):
    return jnp.transpose(jnp.broadcast_to(row, (8, row.shape[1])))[:, :1]


def lay_kernel(factor, out, sems):
    kc, half = factor.shape[1], out.shape[2]
    copies = []
    for at in range(out.shape[0]):
        source = factor.at[at // kc, at % kc, 0, :, pl.ds(0, half), :]
        copies.append(pltpu.make_async_copy(source, out.at[at], sems.at[at]))
        copies[-1].start()
    for copy in copies:
        copy.wait()


def lay(factor):
    transfers, kc, _, parts, nv, naux = factor.shape
    return pl.pallas_call(
        lay_kernel,
        out_shape=jax.ShapeDtypeStruct((transfers * kc, parts, nv // 2, naux), BF16),
        in_specs=[ANY],
        out_specs=VMEM,
        scratch_shapes=[pltpu.SemaphoreType.DMA((transfers * kc,))],
        cost_estimate=COST,
        compiler_params=PARAMS,
    )(pltpu.with_memory_space_constraint(factor, pltpu.HBM))


def pack_kernel(bits, partner, factor, *refs):
    outs, sems = refs[:-1], refs[-1]
    kc, half = factor.shape[1], outs[0].shape[2]
    group = lax.axis_index("kpt")
    copies = []
    for h in (1, 0):
        for transfer, bit in enumerate(bits):
            far_group = jnp.bitwise_xor(group, 1 << bit)
            for k in range(kc):
                slot = partner[transfer, far_group * kc + k] - group * kc
                source = factor.at[transfer, slot, 0, :, pl.ds(h * half, half), :]
                target = outs[h * len(bits) + transfer].at[k]
                copies.append(pltpu.make_async_copy(source, target, sems.at[len(copies)]))
                copies[-1].start()
    for copy in copies:
        copy.wait()


def pack(bits, partner, factor, work):
    transfers, kc, _, parts, nv, naux = factor.shape
    return pl.pallas_call(
        functools.partial(pack_kernel, bits),
        out_shape=[jax.ShapeDtypeStruct((kc, parts, nv // 2, naux), BF16)] * (2 * transfers),
        in_specs=[SMEM, ANY],
        out_specs=[VMEM] * (2 * transfers),
        scratch_shapes=[pltpu.SemaphoreType.DMA((2 * transfers * kc,))],
        cost_estimate=pl.CostEstimate(flops=0, bytes_accessed=work, transcendentals=0),
        compiler_params=PARAMS,
    )(
        pltpu.with_memory_space_constraint(partner, pltpu.HBM),
        pltpu.with_memory_space_constraint(factor, pltpu.HBM),
    )


def inverse_kernel(bits, partner, occ, virtual, out, choice):
    _, _, kc, nv, _ = out.shape
    total = occ.shape[1]
    group, orbit = lax.axis_index("kpt"), lax.axis_index("occ")
    parity = lax.rem(orbit, 2)
    columns = (orbit, orbit + 1 - 2 * parity, lax.rem(orbit + total - 1 + 2 * parity, total))

    def point_step(k, carry):
        point = group * kc + k
        row = virtual[pl.ds(point, 1), :]
        for transfer in range(len(bits)):
            far_point = partner[transfer, point]
            column = column_of(virtual[pl.ds(far_point, 1), :])
            slot = far_point - jnp.bitwise_xor(group, 1 << bits[transfer]) * kc
            for c in range(kc):
                chosen = jnp.where(slot == c, 1.0, 0.0)
                choice[transfer, k, c] = jnp.full(choice.shape[3:], chosen, F32).astype(BF16)
            for place, index in enumerate(columns):
                level = occ[point, orbit] + occ[far_point, index]
                out[transfer, place, k] = 1.0 / ((level - column) - row)
        return carry

    lax.fori_loop(0, kc, point_step, 0)


def inverses(bits, partner, occ_energy, virtual, kc, naux):
    nv = virtual.shape[1]
    return pl.pallas_call(
        functools.partial(inverse_kernel, bits),
        out_shape=[
            jax.ShapeDtypeStruct((len(bits), 3, kc, nv, nv), F32),
            jax.ShapeDtypeStruct((len(bits), kc, kc, ROWS, naux), BF16),
        ],
        in_specs=[SMEM, SMEM, VMEM],
        out_specs=[VMEM, VMEM],
        cost_estimate=COST,
        compiler_params=PARAMS,
    )(partner, occ_energy, virtual)


def amplitude_rows(own, terms):
    _, nv, naux = own.shape
    left = own.reshape(2 * nv, naux)
    rows, blocks = ([], []), []
    for window, inverse in terms:
        size = window.shape[1]
        window = window.reshape(2 * size, naux)
        products = lax.dot_general(
            left, window, (((1,), (1,)), ((), ())), preferred_element_type=F32
        )
        real_part = ((products[:nv, :size] + products[nv:, size:]) * inverse).astype(BF16)
        imag_part = ((products[nv:, :size] - products[:nv, size:]) * inverse).astype(BF16)
        rows[0].extend([real_part, -imag_part])
        rows[1].extend([imag_part, real_part])
        blocks.append(window)
    return [jnp.concatenate(part, axis=1) for part in rows], jnp.concatenate(blocks, axis=0)


def contract(factor, terms_of, finish):
    waiting = None
    points = [(t, k) for t in range(factor.shape[0]) for k in range(factor.shape[1])]
    for point in [*points, None]:
        ready, waiting = waiting, None
        if point is not None:
            t, k = point
            terms = terms_of(t, k)
            waiting = (t, k, *amplitude_rows(factor[t, k, 0], terms)) if terms else None
        if ready is not None:
            t, k, rows, blocks = ready
            for part in range(2):
                finish(t, k, part, jnp.dot(rows[part], blocks, preferred_element_type=F32))


def half_of(h, half):
    return slice(h * half, (h + 1) * half)


def first_kernel(factor, inverse, *refs):
    transfers, kc = factor.shape[:2]
    owns, near, out = refs[: 2 * transfers], refs[-2], refs[-1]
    first, second = half_of(0, near.shape[2]), half_of(1, near.shape[2])

    def terms_of(t, k):
        return [
            (owns[t][k], inverse[t, 0, k, :, first]),
            (owns[transfers + t][k], inverse[t, 0, k, :, second]),
            (near[t * kc + k], inverse[t, 1, k, :, second]),
        ]

    def finish(t, k, part, value):
        out[t, k, part] = value

    contract(factor, terms_of, finish)


def first_terms(factor, inverse, owns, near):
    transfers, kc, _, parts, nv, naux = factor.shape
    operands = [factor, inverse, *owns, near]
    return pl.pallas_call(
        first_kernel,
        out_shape=jax.ShapeDtypeStruct((transfers, kc, parts, nv, naux), F32),
        in_specs=[VMEM] * len(operands),
        out_specs=VMEM,
        cost_estimate=COST,
        compiler_params=PARAMS,
    )(*operands)


def add_kernel(place, h, factor, inverse, window, total, out):
    kc, half = factor.shape[1], window.shape[2]

    def terms_of(t, k):
        at = t * kc + k
        known = at < window.shape[0]
        return [(window[at], inverse[t, place, k, :, half_of(h, half)])] if known else []

    def finish(t, k, part, value):
        out[t, k, part] = value + total[t, k, part]

    contract(factor, terms_of, finish)


def add_terms(place, h, factor, inverse, window, total, cost):
    return pl.pallas_call(
        functools.partial(add_kernel, place, h),
        out_shape=jax.ShapeDtypeStruct(total.shape, F32),
        in_specs=[VMEM] * 4,
        out_specs=VMEM,
        input_output_aliases={3: 0},
        cost_estimate=cost,
        compiler_params=PARAMS,
    )(factor, inverse, window, total)


def far_kernel(done, factor, inverse, choice, *refs):
    fars, (total, kept, out, staged, sems) = refs[:-5], refs[-5:]
    kc, half = factor.shape[1], fars[0].shape[2]
    copies = []

    def terms_of(t, k):
        blocks = [fars[t][c].reshape(-1, *choice.shape[3:]) for c in range(kc)]
        chosen = [block * choice[t, k, c][None] for c, block in enumerate(blocks)]
        window = functools.reduce(jnp.add, chosen).reshape(fars[t].shape[1:])
        return [(window, inverse[t, 2, k, :, half_of(0, half)])]

    def finish(t, k, part, value):
        value = value + total[t, k, part]
        if t * kc + k < done:
            send_part(copies, value, out.at[t, k, 0, part], staged, sems)
        else:
            kept[t, k, part] = value

    contract(factor, terms_of, finish)
    for copy in copies:
        copy.wait()


def send_part(copies, value, target, staged, sems):
    at = len(copies)
    staged[at] = value.astype(BF16)
    copies.append(pltpu.make_async_copy(staged.at[at], target, sems.at[at]))
    copies[-1].start()


def out_scratch(count, nv, naux):
    return [pltpu.VMEM((count, nv, naux), BF16), pltpu.SemaphoreType.DMA((count,))]


def far_terms(done, factor, inverse, choice, fars, total):
    _, _, _, parts, nv, naux = factor.shape
    operands = [factor, inverse, choice, *fars, total]
    return pl.pallas_call(
        functools.partial(far_kernel, done),
        out_shape=[
            jax.ShapeDtypeStruct(total.shape, F32),
            jax.ShapeDtypeStruct(factor.shape, BF16),
        ],
        in_specs=[VMEM] * len(operands),
        out_specs=[VMEM, ANY],
        scratch_shapes=out_scratch(done * parts, nv, naux),
        input_output_aliases={len(operands) - 1: 0},
        cost_estimate=COST,
        compiler_params=PARAMS,
    )(*operands)


def last_kernel(done, factor, inverse, window, total, _, out, staged, sems):
    kc, half = factor.shape[1], window.shape[2]
    copies = []

    def terms_of(t, k):
        at = t * kc + k - done
        return [(window[at], inverse[t, 2, k, :, half_of(1, half)])] if at >= 0 else []

    def finish(t, k, part, value):
        value = value + total[t, k, part]
        send_part(copies, value, out.at[t, k, 0, part], staged, sems)

    contract(factor, terms_of, finish)
    for copy in copies:
        copy.wait()


def last_terms(done, factor, inverse, window, total, result):
    transfers, kc, _, parts, nv, naux = factor.shape
    return pl.pallas_call(
        functools.partial(last_kernel, done),
        out_shape=jax.ShapeDtypeStruct(factor.shape, BF16),
        in_specs=[VMEM] * 4 + [ANY],
        out_specs=ANY,
        scratch_shapes=out_scratch((transfers * kc - done) * parts, nv, naux),
        input_output_aliases={4: 0},
        cost_estimate=COST,
        compiler_params=PARAMS,
    )(factor, inverse, window, total, result)


def last_rows(block, count, work):
    def copy_kernel(source, out):
        out[...] = source[source.shape[0] - count :]

    return pl.pallas_call(
        copy_kernel,
        out_shape=jax.ShapeDtypeStruct((count, *block.shape[1:]), block.dtype),
        in_specs=[VMEM],
        out_specs=VMEM,
        cost_estimate=pl.CostEstimate(flops=work, bytes_accessed=0, transcendentals=0),
        compiler_params=PARAMS,
    )(block)


def body(factor, partner, occ_energy, vir_sorted, vir_order):
    transfers, kc = factor.shape[:2]
    bits = (0, lax.axis_size("kpt").bit_length() - 2)

    part = lay(factor)
    beside = far_swap(part)
    packs = pack(bits, after(partner, part), factor, WORK * factor.size)
    earlies, lates = packs[:transfers], packs[transfers:]
    virtual = virtual_energies(vir_sorted, vir_order)
    inverse, choice = inverses(bits, partner, occ_energy, virtual, kc, factor.shape[5])
    late_own = [group_swap(lates[t], bits[t]) for t in range(transfers)]
    early_own = [group_swap(after(earlies[t], choice), bits[t]) for t in range(transfers)]
    late_block = jnp.concatenate(late_own)
    done = late_block.shape[0] - 1
    late_far, last_far = far_swap(late_block[:done]), far_swap(after(late_block[done:], beside))
    late_near = near_swap(late_block)
    early_block = jnp.concatenate(early_own)
    early_near = jnp.concatenate(
        [near_swap(after(early_block[:2], beside)), near_swap(last_rows(after(early_block, beside), 2, 9000 * factor.size))]
    )
    early_far = [group_swap(beside[t * kc : (t + 1) * kc], bits[t]) for t in range(transfers)]

    total = first_terms(factor, inverse, early_own + late_own, late_near)
    total = add_terms(1, 0, factor, inverse, early_near, total, COST)
    weight = pl.CostEstimate(flops=3 * 1000 * factor.size, bytes_accessed=0, transcendentals=0)
    total = add_terms(2, 1, factor, inverse, late_far, total, weight)
    total, result = far_terms(done, factor, inverse, choice, early_far, total)
    return last_terms(done, factor, inverse, last_far, total, result)


def solution(mesh):
    spec = P(None, "kpt", "occ", None, None, None)
    in_specs = (spec, P(), P(), P(), P())
    return jax.shard_map(body, mesh=mesh, in_specs=in_specs, out_specs=spec, check_vma=False)
```

```python
import functools

import jax
import jax.numpy as jnp
from jax import lax
from jax.experimental import pallas as pl
from jax.experimental.pallas import tpu as pltpu
from jax.sharding import PartitionSpec as P

F32 = jnp.float32
BF16 = jnp.bfloat16
ANY = pl.BlockSpec(memory_space=pl.ANY)
VMEM = pl.BlockSpec(memory_space=pltpu.VMEM)
SMEM = pl.BlockSpec(memory_space=pltpu.SMEM)
PARAMS = pltpu.CompilerParams(vmem_limit_bytes=8 * 1024 * 1024)
WORK = 16
ROWS = 16
COST = pl.CostEstimate(flops=0, bytes_accessed=0, transcendentals=0)


def group_swap(block, bit):
    count = lax.axis_size("kpt")
    return lax.ppermute(block, "kpt", [(g, g ^ (1 << bit)) for g in range(count)])


def near_swap(block):
    count = lax.axis_size("occ")
    return lax.ppermute(block, "occ", [(i, i ^ 1) for i in range(count)])


def far_swap(block):
    count = lax.axis_size("occ")
    return lax.ppermute(
        block, "occ", [(i, (i + (1 if i % 2 else count - 1)) % count) for i in range(count)]
    )


def after(block, *others):
    return lax.optimization_barrier((block, *others))[0]


def virtual_energies(vir_sorted, vir_order):
    ranks = jnp.arange(vir_sorted.shape[1], dtype=jnp.int32)
    matches = vir_order[:, :, None] == ranks[None, None, :]
    return jnp.sum(jnp.where(matches, vir_sorted[:, None, :], 0.0), axis=2)


def column_of(row):
    return jnp.transpose(jnp.broadcast_to(row, (8, row.shape[1])))[:, :1]


def lay_kernel(factor, out, sems):
    kc, half = factor.shape[1], out.shape[2]
    copies = []
    for at in range(out.shape[0]):
        source = factor.at[at // kc, at % kc, 0, :, pl.ds(0, half), :]
        copies.append(pltpu.make_async_copy(source, out.at[at], sems.at[at]))
        copies[-1].start()
    for copy in copies:
        copy.wait()


def lay(factor):
    transfers, kc, _, parts, nv, naux = factor.shape
    return pl.pallas_call(
        lay_kernel,
        out_shape=jax.ShapeDtypeStruct((transfers * kc, parts, nv // 2, naux), BF16),
        in_specs=[ANY],
        out_specs=VMEM,
        scratch_shapes=[pltpu.SemaphoreType.DMA((transfers * kc,))],
        cost_estimate=COST,
        compiler_params=PARAMS,
    )(pltpu.with_memory_space_constraint(factor, pltpu.HBM))


def pack_kernel(bits, partner, factor, *refs):
    outs, sems = refs[:-1], refs[-1]
    kc, half = factor.shape[1], outs[0].shape[2]
    group = lax.axis_index("kpt")
    copies = []
    for h in (1, 0):
        for transfer, bit in enumerate(bits):
            far_group = jnp.bitwise_xor(group, 1 << bit)
            for k in range(kc):
                slot = partner[transfer, far_group * kc + k] - group * kc
                source = factor.at[transfer, slot, 0, :, pl.ds(h * half, half), :]
                target = outs[h * len(bits) + transfer].at[k]
                copies.append(pltpu.make_async_copy(source, target, sems.at[len(copies)]))
                copies[-1].start()
    for copy in copies:
        copy.wait()


def pack(bits, partner, factor, work):
    transfers, kc, _, parts, nv, naux = factor.shape
    return pl.pallas_call(
        functools.partial(pack_kernel, bits),
        out_shape=[jax.ShapeDtypeStruct((kc, parts, nv // 2, naux), BF16)] * (2 * transfers),
        in_specs=[SMEM, ANY],
        out_specs=[VMEM] * (2 * transfers),
        scratch_shapes=[pltpu.SemaphoreType.DMA((2 * transfers * kc,))],
        cost_estimate=pl.CostEstimate(flops=0, bytes_accessed=work, transcendentals=0),
        compiler_params=PARAMS,
    )(
        pltpu.with_memory_space_constraint(partner, pltpu.HBM),
        pltpu.with_memory_space_constraint(factor, pltpu.HBM),
    )


def inverse_kernel(bits, partner, occ, virtual, out, choice):
    _, _, kc, nv, _ = out.shape
    total = occ.shape[1]
    group, orbit = lax.axis_index("kpt"), lax.axis_index("occ")
    parity = lax.rem(orbit, 2)
    columns = (orbit, orbit + 1 - 2 * parity, lax.rem(orbit + total - 1 + 2 * parity, total))

    def point_step(k, carry):
        point = group * kc + k
        row = virtual[pl.ds(point, 1), :]
        for transfer in range(len(bits)):
            far_point = partner[transfer, point]
            column = column_of(virtual[pl.ds(far_point, 1), :])
            slot = far_point - jnp.bitwise_xor(group, 1 << bits[transfer]) * kc
            for c in range(kc):
                chosen = jnp.where(slot == c, 1.0, 0.0)
                choice[transfer, k, c] = jnp.full(choice.shape[3:], chosen, F32).astype(BF16)
            for place, index in enumerate(columns):
                level = occ[point, orbit] + occ[far_point, index]
                out[transfer, place, k] = 1.0 / ((level - column) - row)
        return carry

    lax.fori_loop(0, kc, point_step, 0)


def inverses(bits, partner, occ_energy, virtual, kc, naux):
    nv = virtual.shape[1]
    return pl.pallas_call(
        functools.partial(inverse_kernel, bits),
        out_shape=[
            jax.ShapeDtypeStruct((len(bits), 3, kc, nv, nv), F32),
            jax.ShapeDtypeStruct((len(bits), kc, kc, ROWS, naux), BF16),
        ],
        in_specs=[SMEM, SMEM, VMEM],
        out_specs=[VMEM, VMEM],
        cost_estimate=COST,
        compiler_params=PARAMS,
    )(partner, occ_energy, virtual)


def amplitude_rows(own, terms):
    _, nv, naux = own.shape
    left = own.reshape(2 * nv, naux)
    rows, blocks = ([], []), []
    for window, inverse in terms:
        size = window.shape[1]
        window = window.reshape(2 * size, naux)
        products = lax.dot_general(
            left, window, (((1,), (1,)), ((), ())), preferred_element_type=F32
        )
        real_part = ((products[:nv, :size] + products[nv:, size:]) * inverse).astype(BF16)
        imag_part = ((products[nv:, :size] - products[:nv, size:]) * inverse).astype(BF16)
        rows[0].extend([real_part, -imag_part])
        rows[1].extend([imag_part, real_part])
        blocks.append(window)
    return [jnp.concatenate(part, axis=1) for part in rows], jnp.concatenate(blocks, axis=0)


def contract(factor, terms_of, finish):
    waiting = None
    points = [(t, k) for t in range(factor.shape[0]) for k in range(factor.shape[1])]
    for point in [*points, None]:
        ready, waiting = waiting, None
        if point is not None:
            t, k = point
            terms = terms_of(t, k)
            waiting = (t, k, *amplitude_rows(factor[t, k, 0], terms)) if terms else None
        if ready is not None:
            t, k, rows, blocks = ready
            for part in range(2):
                finish(t, k, part, jnp.dot(rows[part], blocks, preferred_element_type=F32))


def half_of(h, half):
    return slice(h * half, (h + 1) * half)


def first_kernel(factor, inverse, *refs):
    transfers, kc = factor.shape[:2]
    owns, near, out = refs[: 2 * transfers], refs[-2], refs[-1]
    first, second = half_of(0, near.shape[2]), half_of(1, near.shape[2])

    def terms_of(t, k):
        return [
            (owns[t][k], inverse[t, 0, k, :, first]),
            (owns[transfers + t][k], inverse[t, 0, k, :, second]),
            (near[t * kc + k], inverse[t, 1, k, :, second]),
        ]

    def finish(t, k, part, value):
        out[t, k, part] = value

    contract(factor, terms_of, finish)


def first_terms(factor, inverse, owns, near):
    transfers, kc, _, parts, nv, naux = factor.shape
    operands = [factor, inverse, *owns, near]
    return pl.pallas_call(
        first_kernel,
        out_shape=jax.ShapeDtypeStruct((transfers, kc, parts, nv, naux), F32),
        in_specs=[VMEM] * len(operands),
        out_specs=VMEM,
        cost_estimate=COST,
        compiler_params=PARAMS,
    )(*operands)


def add_kernel(place, h, factor, inverse, window, total, out):
    kc, half = factor.shape[1], window.shape[2]

    def terms_of(t, k):
        at = t * kc + k
        known = at < window.shape[0]
        return [(window[at], inverse[t, place, k, :, half_of(h, half)])] if known else []

    def finish(t, k, part, value):
        out[t, k, part] = value + total[t, k, part]

    contract(factor, terms_of, finish)


def add_terms(place, h, factor, inverse, window, total, cost):
    return pl.pallas_call(
        functools.partial(add_kernel, place, h),
        out_shape=jax.ShapeDtypeStruct(total.shape, F32),
        in_specs=[VMEM] * 4,
        out_specs=VMEM,
        input_output_aliases={3: 0},
        cost_estimate=cost,
        compiler_params=PARAMS,
    )(factor, inverse, window, total)


def far_kernel(done, factor, inverse, choice, *refs):
    fars, (total, kept, out, staged, sems) = refs[:-5], refs[-5:]
    kc, half = factor.shape[1], fars[0].shape[2]
    copies = []

    def terms_of(t, k):
        blocks = [fars[t][c].reshape(-1, *choice.shape[3:]) for c in range(kc)]
        chosen = [block * choice[t, k, c][None] for c, block in enumerate(blocks)]
        window = functools.reduce(jnp.add, chosen).reshape(fars[t].shape[1:])
        return [(window, inverse[t, 2, k, :, half_of(0, half)])]

    def finish(t, k, part, value):
        value = value + total[t, k, part]
        if t * kc + k < done:
            send_part(copies, value, out.at[t, k, 0, part], staged, sems)
        else:
            kept[t, k, part] = value

    contract(factor, terms_of, finish)
    for copy in copies:
        copy.wait()


def send_part(copies, value, target, staged, sems):
    at = len(copies)
    staged[at] = value.astype(BF16)
    copies.append(pltpu.make_async_copy(staged.at[at], target, sems.at[at]))
    copies[-1].start()


def out_scratch(count, nv, naux):
    return [pltpu.VMEM((count, nv, naux), BF16), pltpu.SemaphoreType.DMA((count,))]


def far_terms(done, factor, inverse, choice, fars, total):
    _, _, _, parts, nv, naux = factor.shape
    operands = [factor, inverse, choice, *fars, total]
    return pl.pallas_call(
        functools.partial(far_kernel, done),
        out_shape=[
            jax.ShapeDtypeStruct(total.shape, F32),
            jax.ShapeDtypeStruct(factor.shape, BF16),
        ],
        in_specs=[VMEM] * len(operands),
        out_specs=[VMEM, ANY],
        scratch_shapes=out_scratch(done * parts, nv, naux),
        input_output_aliases={len(operands) - 1: 0},
        cost_estimate=COST,
        compiler_params=PARAMS,
    )(*operands)


def last_kernel(done, factor, inverse, window, total, _, out, staged, sems):
    transfers, kc, _, parts, nv, _ = factor.shape
    half = window.shape[2]
    copies = []
    for at in range(done, transfers * kc):
        t, k = at // kc, at % kc
        waiting = []
        for r in range(2):
            rows = half_of(r, nv // 2)
            terms = [(window[at - done], inverse[t, 2, k, rows, half_of(1, half)])]
            waiting.append(amplitude_rows(factor[t, k, 0, :, rows, :], terms))
        for r, (sides, blocks) in enumerate(waiting):
            rows = half_of(r, nv // 2)
            for part in range(parts):
                value = jnp.dot(sides[part], blocks, preferred_element_type=F32)
                target = out.at[t, k, 0, part, pl.ds(rows.start, nv // 2)]
                send_part(copies, value + total[t, k, part, rows], target, staged, sems)
    for copy in copies:
        copy.wait()


def last_terms(done, factor, inverse, window, total, result):
    transfers, kc, _, parts, nv, naux = factor.shape
    return pl.pallas_call(
        functools.partial(last_kernel, done),
        out_shape=jax.ShapeDtypeStruct(factor.shape, BF16),
        in_specs=[VMEM] * 4 + [ANY],
        out_specs=ANY,
        scratch_shapes=out_scratch((transfers * kc - done) * parts * 2, nv // 2, naux),
        input_output_aliases={4: 0},
        cost_estimate=COST,
        compiler_params=PARAMS,
    )(factor, inverse, window, total, result)


def last_rows(block, count, work):
    def copy_kernel(source, out):
        out[...] = source[source.shape[0] - count :]

    return pl.pallas_call(
        copy_kernel,
        out_shape=jax.ShapeDtypeStruct((count, *block.shape[1:]), block.dtype),
        in_specs=[VMEM],
        out_specs=VMEM,
        cost_estimate=pl.CostEstimate(flops=work, bytes_accessed=0, transcendentals=0),
        compiler_params=PARAMS,
    )(block)


def body(factor, partner, occ_energy, vir_sorted, vir_order):
    transfers, kc = factor.shape[:2]
    bits = (0, lax.axis_size("kpt").bit_length() - 2)

    part = lay(factor)
    beside = far_swap(part)
    packs = pack(bits, after(partner, part), factor, WORK * factor.size)
    earlies, lates = packs[:transfers], packs[transfers:]
    virtual = virtual_energies(vir_sorted, vir_order)
    inverse, choice = inverses(bits, partner, occ_energy, virtual, kc, factor.shape[5])
    late_own = [group_swap(lates[t], bits[t]) for t in range(transfers)]
    early_own = [group_swap(after(earlies[t], choice), bits[t]) for t in range(transfers)]
    late_block = jnp.concatenate(late_own)
    done = late_block.shape[0] - 1
    late_far, last_far = far_swap(late_block[:done]), far_swap(after(late_block[done:], beside))
    late_near = near_swap(late_block)
    early_block = jnp.concatenate(early_own)
    early_near = jnp.concatenate(
        [near_swap(after(early_block[:2], beside)), near_swap(last_rows(after(early_block, beside), 2, 9000 * factor.size))]
    )
    early_far = [group_swap(beside[t * kc : (t + 1) * kc], bits[t]) for t in range(transfers)]

    total = first_terms(factor, inverse, early_own + late_own, late_near)
    total = add_terms(1, 0, factor, inverse, early_near, total, COST)
    weight = pl.CostEstimate(flops=3 * 1000 * factor.size, bytes_accessed=0, transcendentals=0)
    total = add_terms(2, 1, factor, inverse, late_far, total, weight)
    total, result = far_terms(done, factor, inverse, choice, early_far, total)
    return last_terms(done, factor, inverse, last_far, total, result)


def solution(mesh):
    spec = P(None, "kpt", "occ", None, None, None)
    in_specs = (spec, P(), P(), P(), P())
    return jax.shard_map(body, mesh=mesh, in_specs=in_specs, out_specs=spec, check_vma=False)
```

```python
import functools

import jax
import jax.numpy as jnp
from jax import lax
from jax.experimental import pallas as pl
from jax.experimental.pallas import tpu as pltpu
from jax.sharding import PartitionSpec as P

F32 = jnp.float32
BF16 = jnp.bfloat16
ANY = pl.BlockSpec(memory_space=pl.ANY)
VMEM = pl.BlockSpec(memory_space=pltpu.VMEM)
SMEM = pl.BlockSpec(memory_space=pltpu.SMEM)
PARAMS = pltpu.CompilerParams(vmem_limit_bytes=8 * 1024 * 1024)
WORK = 16
ROWS = 16
COST = pl.CostEstimate(flops=0, bytes_accessed=0, transcendentals=0)


def group_swap(block, bit):
    count = lax.axis_size("kpt")
    return lax.ppermute(block, "kpt", [(g, g ^ (1 << bit)) for g in range(count)])


def near_swap(block):
    count = lax.axis_size("occ")
    return lax.ppermute(block, "occ", [(i, i ^ 1) for i in range(count)])


def far_swap(block):
    count = lax.axis_size("occ")
    return lax.ppermute(
        block, "occ", [(i, (i + (1 if i % 2 else count - 1)) % count) for i in range(count)]
    )


def after(block, *others):
    return lax.optimization_barrier((block, *others))[0]


def virtual_energies(vir_sorted, vir_order):
    ranks = jnp.arange(vir_sorted.shape[1], dtype=jnp.int32)
    matches = vir_order[:, :, None] == ranks[None, None, :]
    return jnp.sum(jnp.where(matches, vir_sorted[:, None, :], 0.0), axis=2)


def column_of(row):
    return jnp.transpose(jnp.broadcast_to(row, (8, row.shape[1])))[:, :1]


def lay_kernel(factor, out, sems):
    kc, half = factor.shape[1], out.shape[2]
    copies = []
    for at in range(out.shape[0]):
        source = factor.at[at // kc, at % kc, 0, :, pl.ds(0, half), :]
        copies.append(pltpu.make_async_copy(source, out.at[at], sems.at[at]))
        copies[-1].start()
    for copy in copies:
        copy.wait()


def lay(factor):
    transfers, kc, _, parts, nv, naux = factor.shape
    return pl.pallas_call(
        lay_kernel,
        out_shape=jax.ShapeDtypeStruct((transfers * kc, parts, nv // 2, naux), BF16),
        in_specs=[ANY],
        out_specs=VMEM,
        scratch_shapes=[pltpu.SemaphoreType.DMA((transfers * kc,))],
        cost_estimate=COST,
        compiler_params=PARAMS,
    )(pltpu.with_memory_space_constraint(factor, pltpu.HBM))


def pack_kernel(bits, partner, factor, *refs):
    outs, sems = refs[:-1], refs[-1]
    kc, half = factor.shape[1], outs[0].shape[2]
    group = lax.axis_index("kpt")
    copies = []
    for h in (1, 0):
        for transfer, bit in enumerate(bits):
            far_group = jnp.bitwise_xor(group, 1 << bit)
            for k in range(kc):
                slot = partner[transfer, far_group * kc + k] - group * kc
                source = factor.at[transfer, slot, 0, :, pl.ds(h * half, half), :]
                target = outs[h * len(bits) + transfer].at[k]
                copies.append(pltpu.make_async_copy(source, target, sems.at[len(copies)]))
                copies[-1].start()
    for copy in copies:
        copy.wait()


def pack(bits, partner, factor, work):
    transfers, kc, _, parts, nv, naux = factor.shape
    return pl.pallas_call(
        functools.partial(pack_kernel, bits),
        out_shape=[jax.ShapeDtypeStruct((kc, parts, nv // 2, naux), BF16)] * (2 * transfers),
        in_specs=[SMEM, ANY],
        out_specs=[VMEM] * (2 * transfers),
        scratch_shapes=[pltpu.SemaphoreType.DMA((2 * transfers * kc,))],
        cost_estimate=pl.CostEstimate(flops=0, bytes_accessed=work, transcendentals=0),
        compiler_params=PARAMS,
    )(
        pltpu.with_memory_space_constraint(partner, pltpu.HBM),
        pltpu.with_memory_space_constraint(factor, pltpu.HBM),
    )


def inverse_kernel(bits, partner, occ, virtual, out, choice):
    _, _, kc, nv, _ = out.shape
    total = occ.shape[1]
    group, orbit = lax.axis_index("kpt"), lax.axis_index("occ")
    parity = lax.rem(orbit, 2)
    columns = (orbit, orbit + 1 - 2 * parity, lax.rem(orbit + total - 1 + 2 * parity, total))

    def point_step(k, carry):
        point = group * kc + k
        row = virtual[pl.ds(point, 1), :]
        for transfer in range(len(bits)):
            far_point = partner[transfer, point]
            column = column_of(virtual[pl.ds(far_point, 1), :])
            slot = far_point - jnp.bitwise_xor(group, 1 << bits[transfer]) * kc
            for c in range(kc):
                chosen = jnp.where(slot == c, 1.0, 0.0)
                choice[transfer, k, c] = jnp.full(choice.shape[3:], chosen, F32).astype(BF16)
            for place, index in enumerate(columns):
                level = occ[point, orbit] + occ[far_point, index]
                out[transfer, place, k] = 1.0 / ((level - column) - row)
        return carry

    lax.fori_loop(0, kc, point_step, 0)


def inverses(bits, partner, occ_energy, virtual, kc, naux):
    nv = virtual.shape[1]
    return pl.pallas_call(
        functools.partial(inverse_kernel, bits),
        out_shape=[
            jax.ShapeDtypeStruct((len(bits), 3, kc, nv, nv), F32),
            jax.ShapeDtypeStruct((len(bits), kc, kc, ROWS, naux), BF16),
        ],
        in_specs=[SMEM, SMEM, VMEM],
        out_specs=[VMEM, VMEM],
        cost_estimate=COST,
        compiler_params=PARAMS,
    )(partner, occ_energy, virtual)


def amplitude_rows(own, terms):
    _, nv, naux = own.shape
    left = own.reshape(2 * nv, naux)
    rows, blocks = ([], []), []
    for window, inverse in terms:
        size = window.shape[1]
        window = window.reshape(2 * size, naux)
        products = lax.dot_general(
            left, window, (((1,), (1,)), ((), ())), preferred_element_type=F32
        )
        real_part = ((products[:nv, :size] + products[nv:, size:]) * inverse).astype(BF16)
        imag_part = ((products[nv:, :size] - products[:nv, size:]) * inverse).astype(BF16)
        rows[0].extend([real_part, -imag_part])
        rows[1].extend([imag_part, real_part])
        blocks.append(window)
    return [jnp.concatenate(part, axis=1) for part in rows], jnp.concatenate(blocks, axis=0)


def contract(factor, terms_of, finish):
    waiting = None
    points = [(t, k) for t in range(factor.shape[0]) for k in range(factor.shape[1])]
    for point in [*points, None]:
        ready, waiting = waiting, None
        if point is not None:
            t, k = point
            terms = terms_of(t, k)
            waiting = (t, k, *amplitude_rows(factor[t, k, 0], terms)) if terms else None
        if ready is not None:
            t, k, rows, blocks = ready
            for part in range(2):
                finish(t, k, part, jnp.dot(rows[part], blocks, preferred_element_type=F32))


def half_of(h, half):
    return slice(h * half, (h + 1) * half)


def first_kernel(factor, inverse, *refs):
    transfers, kc = factor.shape[:2]
    owns, near, out = refs[: 2 * transfers], refs[-2], refs[-1]
    first, second = half_of(0, near.shape[2]), half_of(1, near.shape[2])

    def terms_of(t, k):
        return [
            (owns[t][k], inverse[t, 0, k, :, first]),
            (owns[transfers + t][k], inverse[t, 0, k, :, second]),
            (near[t * kc + k], inverse[t, 1, k, :, second]),
        ]

    def finish(t, k, part, value):
        out[t, k, part] = value

    contract(factor, terms_of, finish)


def first_terms(factor, inverse, owns, near):
    transfers, kc, _, parts, nv, naux = factor.shape
    operands = [factor, inverse, *owns, near]
    return pl.pallas_call(
        first_kernel,
        out_shape=jax.ShapeDtypeStruct((transfers, kc, parts, nv, naux), F32),
        in_specs=[VMEM] * len(operands),
        out_specs=VMEM,
        cost_estimate=COST,
        compiler_params=PARAMS,
    )(*operands)


def add_kernel(place, h, factor, inverse, window, total, out):
    kc, half = factor.shape[1], window.shape[2]

    def terms_of(t, k):
        at = t * kc + k
        known = at < window.shape[0]
        return [(window[at], inverse[t, place, k, :, half_of(h, half)])] if known else []

    def finish(t, k, part, value):
        out[t, k, part] = value + total[t, k, part]

    contract(factor, terms_of, finish)


def add_terms(place, h, factor, inverse, window, total, cost):
    return pl.pallas_call(
        functools.partial(add_kernel, place, h),
        out_shape=jax.ShapeDtypeStruct(total.shape, F32),
        in_specs=[VMEM] * 4,
        out_specs=VMEM,
        input_output_aliases={3: 0},
        cost_estimate=cost,
        compiler_params=PARAMS,
    )(factor, inverse, window, total)


def far_kernel(done, factor, inverse, choice, *refs):
    fars, (total, kept, out, staged, sems) = refs[:-5], refs[-5:]
    kc, half = factor.shape[1], fars[0].shape[2]
    copies = []

    def terms_of(t, k):
        blocks = [fars[t][c].reshape(-1, *choice.shape[3:]) for c in range(kc)]
        chosen = [block * choice[t, k, c][None] for c, block in enumerate(blocks)]
        window = functools.reduce(jnp.add, chosen).reshape(fars[t].shape[1:])
        return [(window, inverse[t, 2, k, :, half_of(0, half)])]

    def finish(t, k, part, value):
        value = value + total[t, k, part]
        if t * kc + k < done:
            send_part(copies, value, out.at[t, k, 0, part], staged, sems)
        else:
            kept[t, k, part] = value

    contract(factor, terms_of, finish)
    for copy in copies:
        copy.wait()


def send_part(copies, value, target, staged, sems):
    at = len(copies)
    staged[at] = value.astype(BF16)
    copies.append(pltpu.make_async_copy(staged.at[at], target, sems.at[at]))
    copies[-1].start()


def out_scratch(count, nv, naux):
    return [pltpu.VMEM((count, nv, naux), BF16), pltpu.SemaphoreType.DMA((count,))]


def far_terms(done, factor, inverse, choice, fars, total):
    _, _, _, parts, nv, naux = factor.shape
    operands = [factor, inverse, choice, *fars, total]
    return pl.pallas_call(
        functools.partial(far_kernel, done),
        out_shape=[
            jax.ShapeDtypeStruct(total.shape, F32),
            jax.ShapeDtypeStruct(factor.shape, BF16),
        ],
        in_specs=[VMEM] * len(operands),
        out_specs=[VMEM, ANY],
        scratch_shapes=out_scratch(done * parts, nv, naux),
        input_output_aliases={len(operands) - 1: 0},
        cost_estimate=COST,
        compiler_params=PARAMS,
    )(*operands)


def last_kernel(done, factor, inverse, window, total, _, out, staged, sems):
    transfers, kc, _, parts, nv, _ = factor.shape
    half = window.shape[2]
    copies = []
    for at in range(done, transfers * kc):
        t, k = at // kc, at % kc
        waiting = []
        for r in range(2):
            rows = half_of(r, nv // 2)
            terms = [(window[at - done], inverse[t, 2, k, rows, half_of(1, half)])]
            waiting.append(amplitude_rows(factor[t, k, 0, :, rows, :], terms))
        for r, (sides, blocks) in enumerate(waiting):
            rows = half_of(r, nv // 2)
            n = len(copies)
            for part in range(parts):
                value = jnp.dot(sides[part], blocks, preferred_element_type=F32)
                staged[n, part] = (value + total[t, k, part, rows]).astype(BF16)
            target = out.at[t, k, 0, :, pl.ds(rows.start, nv // 2)]
            copies.append(pltpu.make_async_copy(staged.at[n], target, sems.at[n]))
            copies[-1].start()
    for copy in copies:
        copy.wait()


def last_terms(done, factor, inverse, window, total, result):
    transfers, kc, _, parts, nv, naux = factor.shape
    return pl.pallas_call(
        functools.partial(last_kernel, done),
        out_shape=jax.ShapeDtypeStruct(factor.shape, BF16),
        in_specs=[VMEM] * 4 + [ANY],
        out_specs=ANY,
        scratch_shapes=[
            pltpu.VMEM((2 * (transfers * kc - done), parts, nv // 2, naux), BF16),
            pltpu.SemaphoreType.DMA((2 * (transfers * kc - done),)),
        ],
        input_output_aliases={4: 0},
        cost_estimate=COST,
        compiler_params=PARAMS,
    )(factor, inverse, window, total, result)


def last_rows(block, count, work):
    def copy_kernel(source, out):
        out[...] = source[source.shape[0] - count :]

    return pl.pallas_call(
        copy_kernel,
        out_shape=jax.ShapeDtypeStruct((count, *block.shape[1:]), block.dtype),
        in_specs=[VMEM],
        out_specs=VMEM,
        cost_estimate=pl.CostEstimate(flops=work, bytes_accessed=0, transcendentals=0),
        compiler_params=PARAMS,
    )(block)


def body(factor, partner, occ_energy, vir_sorted, vir_order):
    transfers, kc = factor.shape[:2]
    bits = (0, lax.axis_size("kpt").bit_length() - 2)

    part = lay(factor)
    beside = far_swap(part)
    packs = pack(bits, after(partner, part), factor, WORK * factor.size)
    earlies, lates = packs[:transfers], packs[transfers:]
    virtual = virtual_energies(vir_sorted, vir_order)
    inverse, choice = inverses(bits, partner, occ_energy, virtual, kc, factor.shape[5])
    late_own = [group_swap(lates[t], bits[t]) for t in range(transfers)]
    early_own = [group_swap(after(earlies[t], choice), bits[t]) for t in range(transfers)]
    late_block = jnp.concatenate(late_own)
    done = late_block.shape[0] - 1
    late_far, last_far = far_swap(late_block[:done]), far_swap(after(late_block[done:], beside))
    late_near = near_swap(late_block)
    early_block = jnp.concatenate(early_own)
    early_near = jnp.concatenate(
        [near_swap(after(early_block[:2], beside)), near_swap(last_rows(after(early_block, beside), 2, 9000 * factor.size))]
    )
    early_far = [group_swap(beside[t * kc : (t + 1) * kc], bits[t]) for t in range(transfers)]

    total = first_terms(factor, inverse, early_own + late_own, late_near)
    total = add_terms(1, 0, factor, inverse, early_near, total, COST)
    weight = pl.CostEstimate(flops=3 * 1000 * factor.size, bytes_accessed=0, transcendentals=0)
    total = add_terms(2, 1, factor, inverse, late_far, total, weight)
    total, result = far_terms(done, factor, inverse, choice, early_far, total)
    return last_terms(done, factor, inverse, last_far, total, result)


def solution(mesh):
    spec = P(None, "kpt", "occ", None, None, None)
    in_specs = (spec, P(), P(), P(), P())
    return jax.shard_map(body, mesh=mesh, in_specs=in_specs, out_specs=spec, check_vma=False)
```

```python
import functools

import jax
import jax.numpy as jnp
from jax import lax
from jax.experimental import pallas as pl
from jax.experimental.pallas import tpu as pltpu
from jax.sharding import PartitionSpec as P

F32 = jnp.float32
BF16 = jnp.bfloat16
ANY = pl.BlockSpec(memory_space=pl.ANY)
VMEM = pl.BlockSpec(memory_space=pltpu.VMEM)
SMEM = pl.BlockSpec(memory_space=pltpu.SMEM)
PARAMS = pltpu.CompilerParams(vmem_limit_bytes=8 * 1024 * 1024)
WORK = 16
ROWS = 16
COST = pl.CostEstimate(flops=0, bytes_accessed=0, transcendentals=0)


def group_swap(block, bit):
    count = lax.axis_size("kpt")
    return lax.ppermute(block, "kpt", [(g, g ^ (1 << bit)) for g in range(count)])


def near_swap(block):
    count = lax.axis_size("occ")
    return lax.ppermute(block, "occ", [(i, i ^ 1) for i in range(count)])


def far_swap(block):
    count = lax.axis_size("occ")
    return lax.ppermute(
        block, "occ", [(i, (i + (1 if i % 2 else count - 1)) % count) for i in range(count)]
    )


def after(block, *others):
    return lax.optimization_barrier((block, *others))[0]


def virtual_energies(vir_sorted, vir_order):
    ranks = jnp.arange(vir_sorted.shape[1], dtype=jnp.int32)
    matches = vir_order[:, :, None] == ranks[None, None, :]
    return jnp.sum(jnp.where(matches, vir_sorted[:, None, :], 0.0), axis=2)


def column_of(row):
    return jnp.transpose(jnp.broadcast_to(row, (8, row.shape[1])))[:, :1]


def lay_kernel(factor, out, sems):
    kc, half = factor.shape[1], out.shape[2]
    copies = []
    for at in range(out.shape[0]):
        source = factor.at[at // kc, at % kc, 0, :, pl.ds(0, half), :]
        copies.append(pltpu.make_async_copy(source, out.at[at], sems.at[at]))
        copies[-1].start()
    for copy in copies:
        copy.wait()


def lay(factor):
    transfers, kc, _, parts, nv, naux = factor.shape
    return pl.pallas_call(
        lay_kernel,
        out_shape=jax.ShapeDtypeStruct((transfers * kc, parts, nv // 2, naux), BF16),
        in_specs=[ANY],
        out_specs=VMEM,
        scratch_shapes=[pltpu.SemaphoreType.DMA((transfers * kc,))],
        cost_estimate=COST,
        compiler_params=PARAMS,
    )(pltpu.with_memory_space_constraint(factor, pltpu.HBM))


def pack_kernel(bits, partner, factor, *refs):
    outs, sems = refs[:-1], refs[-1]
    kc, half = factor.shape[1], outs[0].shape[2]
    group = lax.axis_index("kpt")
    copies = []
    for h in (1, 0):
        for transfer, bit in enumerate(bits):
            far_group = jnp.bitwise_xor(group, 1 << bit)
            for k in range(kc):
                slot = partner[transfer, far_group * kc + k] - group * kc
                source = factor.at[transfer, slot, 0, :, pl.ds(h * half, half), :]
                target = outs[h * len(bits) + transfer].at[k]
                copies.append(pltpu.make_async_copy(source, target, sems.at[len(copies)]))
                copies[-1].start()
    for copy in copies:
        copy.wait()


def pack(bits, partner, factor, work):
    transfers, kc, _, parts, nv, naux = factor.shape
    return pl.pallas_call(
        functools.partial(pack_kernel, bits),
        out_shape=[jax.ShapeDtypeStruct((kc, parts, nv // 2, naux), BF16)] * (2 * transfers),
        in_specs=[SMEM, ANY],
        out_specs=[VMEM] * (2 * transfers),
        scratch_shapes=[pltpu.SemaphoreType.DMA((2 * transfers * kc,))],
        cost_estimate=pl.CostEstimate(flops=0, bytes_accessed=work, transcendentals=0),
        compiler_params=PARAMS,
    )(
        pltpu.with_memory_space_constraint(partner, pltpu.HBM),
        pltpu.with_memory_space_constraint(factor, pltpu.HBM),
    )


def inverse_kernel(bits, partner, occ, virtual, out, choice):
    _, _, kc, nv, _ = out.shape
    total = occ.shape[1]
    group, orbit = lax.axis_index("kpt"), lax.axis_index("occ")
    parity = lax.rem(orbit, 2)
    columns = (orbit, orbit + 1 - 2 * parity, lax.rem(orbit + total - 1 + 2 * parity, total))

    def point_step(k, carry):
        point = group * kc + k
        row = virtual[pl.ds(point, 1), :]
        for transfer in range(len(bits)):
            far_point = partner[transfer, point]
            column = column_of(virtual[pl.ds(far_point, 1), :])
            slot = far_point - jnp.bitwise_xor(group, 1 << bits[transfer]) * kc
            for c in range(kc):
                chosen = jnp.where(slot == c, 1.0, 0.0)
                choice[transfer, k, c] = jnp.full(choice.shape[3:], chosen, F32).astype(BF16)
            for place, index in enumerate(columns):
                level = occ[point, orbit] + occ[far_point, index]
                out[transfer, place, k] = 1.0 / ((level - column) - row)
        return carry

    lax.fori_loop(0, kc, point_step, 0)


def inverses(bits, partner, occ_energy, virtual, kc, naux):
    nv = virtual.shape[1]
    return pl.pallas_call(
        functools.partial(inverse_kernel, bits),
        out_shape=[
            jax.ShapeDtypeStruct((len(bits), 3, kc, nv, nv), F32),
            jax.ShapeDtypeStruct((len(bits), kc, kc, ROWS, naux), BF16),
        ],
        in_specs=[SMEM, SMEM, VMEM],
        out_specs=[VMEM, VMEM],
        cost_estimate=COST,
        compiler_params=PARAMS,
    )(partner, occ_energy, virtual)


def amplitude_rows(own, terms):
    _, nv, naux = own.shape
    left = own.reshape(2 * nv, naux)
    rows, blocks = ([], []), []
    for window, inverse in terms:
        size = window.shape[1]
        window = window.reshape(2 * size, naux)
        products = lax.dot_general(
            left, window, (((1,), (1,)), ((), ())), preferred_element_type=F32
        )
        real_part = ((products[:nv, :size] + products[nv:, size:]) * inverse).astype(BF16)
        imag_part = ((products[nv:, :size] - products[:nv, size:]) * inverse).astype(BF16)
        rows[0].extend([real_part, -imag_part])
        rows[1].extend([imag_part, real_part])
        blocks.append(window)
    return [jnp.concatenate(part, axis=1) for part in rows], jnp.concatenate(blocks, axis=0)


def contract(factor, terms_of, finish):
    waiting = None
    points = [(t, k) for t in range(factor.shape[0]) for k in range(factor.shape[1])]
    for point in [*points, None]:
        ready, waiting = waiting, None
        if point is not None:
            t, k = point
            terms = terms_of(t, k)
            waiting = (t, k, *amplitude_rows(factor[t, k, 0], terms)) if terms else None
        if ready is not None:
            t, k, rows, blocks = ready
            for part in range(2):
                finish(t, k, part, jnp.dot(rows[part], blocks, preferred_element_type=F32))


def half_of(h, half):
    return slice(h * half, (h + 1) * half)


def first_kernel(factor, inverse, *refs):
    transfers, kc = factor.shape[:2]
    owns, near, out = refs[: 2 * transfers], refs[-2], refs[-1]
    first, second = half_of(0, near.shape[2]), half_of(1, near.shape[2])

    def terms_of(t, k):
        return [
            (owns[t][k], inverse[t, 0, k, :, first]),
            (owns[transfers + t][k], inverse[t, 0, k, :, second]),
            (near[t * kc + k], inverse[t, 1, k, :, second]),
        ]

    def finish(t, k, part, value):
        out[t, k, part] = value

    contract(factor, terms_of, finish)


def first_terms(factor, inverse, owns, near):
    transfers, kc, _, parts, nv, naux = factor.shape
    operands = [factor, inverse, *owns, near]
    return pl.pallas_call(
        first_kernel,
        out_shape=jax.ShapeDtypeStruct((transfers, kc, parts, nv, naux), F32),
        in_specs=[VMEM] * len(operands),
        out_specs=VMEM,
        cost_estimate=COST,
        compiler_params=PARAMS,
    )(*operands)


def add_kernel(place, h, factor, inverse, window, total, out):
    kc, half = factor.shape[1], window.shape[2]

    def terms_of(t, k):
        at = t * kc + k
        known = at < window.shape[0]
        return [(window[at], inverse[t, place, k, :, half_of(h, half)])] if known else []

    def finish(t, k, part, value):
        out[t, k, part] = value + total[t, k, part]

    contract(factor, terms_of, finish)


def add_terms(place, h, factor, inverse, window, total, cost):
    return pl.pallas_call(
        functools.partial(add_kernel, place, h),
        out_shape=jax.ShapeDtypeStruct(total.shape, F32),
        in_specs=[VMEM] * 4,
        out_specs=VMEM,
        input_output_aliases={3: 0},
        cost_estimate=cost,
        compiler_params=PARAMS,
    )(factor, inverse, window, total)


def far_kernel(done, factor, inverse, choice, *refs):
    fars, (total, kept, out, staged, sems) = refs[:-5], refs[-5:]
    kc, half = factor.shape[1], fars[0].shape[2]
    copies = []

    def terms_of(t, k):
        blocks = [fars[t][c].reshape(-1, *choice.shape[3:]) for c in range(kc)]
        chosen = [block * choice[t, k, c][None] for c, block in enumerate(blocks)]
        window = functools.reduce(jnp.add, chosen).reshape(fars[t].shape[1:])
        return [(window, inverse[t, 2, k, :, half_of(0, half)])]

    def finish(t, k, part, value):
        value = value + total[t, k, part]
        if t * kc + k < done:
            send_part(copies, value, out.at[t, k, 0, part], staged, sems)
        else:
            kept[t, k, part] = value

    contract(factor, terms_of, finish)
    for copy in copies:
        copy.wait()


def send_part(copies, value, target, staged, sems):
    at = len(copies)
    staged[at] = value.astype(BF16)
    copies.append(pltpu.make_async_copy(staged.at[at], target, sems.at[at]))
    copies[-1].start()


def out_scratch(count, nv, naux):
    return [pltpu.VMEM((count, nv, naux), BF16), pltpu.SemaphoreType.DMA((count,))]


def far_terms(done, factor, inverse, choice, fars, total):
    _, _, _, parts, nv, naux = factor.shape
    operands = [factor, inverse, choice, *fars, total]
    return pl.pallas_call(
        functools.partial(far_kernel, done),
        out_shape=[
            jax.ShapeDtypeStruct(total.shape, F32),
            jax.ShapeDtypeStruct(factor.shape, BF16),
        ],
        in_specs=[VMEM] * len(operands),
        out_specs=[VMEM, ANY],
        scratch_shapes=out_scratch(done * parts, nv, naux),
        input_output_aliases={len(operands) - 1: 0},
        cost_estimate=COST,
        compiler_params=PARAMS,
    )(*operands)


def last_kernel(done, factor, inverse, window, total, _, out, staged, sems):
    transfers, kc, _, parts, nv, _ = factor.shape
    half = window.shape[2]
    copies = []
    for at in range(done, transfers * kc):
        t, k = at // kc, at % kc
        waiting = []
        for r in range(4):
            rows = half_of(r, nv // 4)
            terms = [(window[at - done], inverse[t, 2, k, rows, half_of(1, half)])]
            waiting.append(amplitude_rows(factor[t, k, 0, :, rows, :], terms))
        for r, (sides, blocks) in enumerate(waiting):
            rows = half_of(r, nv // 4)
            for part in range(parts):
                value = jnp.dot(sides[part], blocks, preferred_element_type=F32)
                target = out.at[t, k, 0, part, pl.ds(rows.start, nv // 4)]
                send_part(copies, value + total[t, k, part, rows], target, staged, sems)
    for copy in copies:
        copy.wait()


def last_terms(done, factor, inverse, window, total, result):
    transfers, kc, _, parts, nv, naux = factor.shape
    return pl.pallas_call(
        functools.partial(last_kernel, done),
        out_shape=jax.ShapeDtypeStruct(factor.shape, BF16),
        in_specs=[VMEM] * 4 + [ANY],
        out_specs=ANY,
        scratch_shapes=out_scratch((transfers * kc - done) * parts * 4, nv // 4, naux),
        input_output_aliases={4: 0},
        cost_estimate=COST,
        compiler_params=PARAMS,
    )(factor, inverse, window, total, result)


def last_rows(block, count, work):
    def copy_kernel(source, out):
        out[...] = source[source.shape[0] - count :]

    return pl.pallas_call(
        copy_kernel,
        out_shape=jax.ShapeDtypeStruct((count, *block.shape[1:]), block.dtype),
        in_specs=[VMEM],
        out_specs=VMEM,
        cost_estimate=pl.CostEstimate(flops=work, bytes_accessed=0, transcendentals=0),
        compiler_params=PARAMS,
    )(block)


def body(factor, partner, occ_energy, vir_sorted, vir_order):
    transfers, kc = factor.shape[:2]
    bits = (0, lax.axis_size("kpt").bit_length() - 2)

    part = lay(factor)
    beside = far_swap(part)
    packs = pack(bits, after(partner, part), factor, WORK * factor.size)
    earlies, lates = packs[:transfers], packs[transfers:]
    virtual = virtual_energies(vir_sorted, vir_order)
    inverse, choice = inverses(bits, partner, occ_energy, virtual, kc, factor.shape[5])
    late_own = [group_swap(lates[t], bits[t]) for t in range(transfers)]
    early_own = [group_swap(after(earlies[t], choice), bits[t]) for t in range(transfers)]
    late_block = jnp.concatenate(late_own)
    done = late_block.shape[0] - 1
    late_far, last_far = far_swap(late_block[:done]), far_swap(after(late_block[done:], beside))
    late_near = near_swap(late_block)
    early_block = jnp.concatenate(early_own)
    early_near = jnp.concatenate(
        [near_swap(after(early_block[:2], beside)), near_swap(last_rows(after(early_block, beside), 2, 9000 * factor.size))]
    )
    early_far = [group_swap(beside[t * kc : (t + 1) * kc], bits[t]) for t in range(transfers)]

    total = first_terms(factor, inverse, early_own + late_own, late_near)
    total = add_terms(1, 0, factor, inverse, early_near, total, COST)
    weight = pl.CostEstimate(flops=3 * 1000 * factor.size, bytes_accessed=0, transcendentals=0)
    total = add_terms(2, 1, factor, inverse, late_far, total, weight)
    total, result = far_terms(done, factor, inverse, choice, early_far, total)
    return last_terms(done, factor, inverse, last_far, total, result)


def solution(mesh):
    spec = P(None, "kpt", "occ", None, None, None)
    in_specs = (spec, P(), P(), P(), P())
    return jax.shard_map(body, mesh=mesh, in_specs=in_specs, out_specs=spec, check_vma=False)
```

```python
import functools

import jax
import jax.numpy as jnp
from jax import lax
from jax.experimental import pallas as pl
from jax.experimental.pallas import tpu as pltpu
from jax.sharding import PartitionSpec as P

F32 = jnp.float32
BF16 = jnp.bfloat16
ANY = pl.BlockSpec(memory_space=pl.ANY)
VMEM = pl.BlockSpec(memory_space=pltpu.VMEM)
SMEM = pl.BlockSpec(memory_space=pltpu.SMEM)
PARAMS = pltpu.CompilerParams(vmem_limit_bytes=8 * 1024 * 1024)
WORK = 16
ROWS = 16
COST = pl.CostEstimate(flops=0, bytes_accessed=0, transcendentals=0)


def group_swap(block, bit):
    count = lax.axis_size("kpt")
    return lax.ppermute(block, "kpt", [(g, g ^ (1 << bit)) for g in range(count)])


def near_swap(block):
    count = lax.axis_size("occ")
    return lax.ppermute(block, "occ", [(i, i ^ 1) for i in range(count)])


def far_swap(block):
    count = lax.axis_size("occ")
    return lax.ppermute(
        block, "occ", [(i, (i + (1 if i % 2 else count - 1)) % count) for i in range(count)]
    )


def after(block, *others):
    return lax.optimization_barrier((block, *others))[0]


def virtual_energies(vir_sorted, vir_order):
    ranks = jnp.arange(vir_sorted.shape[1], dtype=jnp.int32)
    matches = vir_order[:, :, None] == ranks[None, None, :]
    return jnp.sum(jnp.where(matches, vir_sorted[:, None, :], 0.0), axis=2)


def column_of(row):
    return jnp.transpose(jnp.broadcast_to(row, (8, row.shape[1])))[:, :1]


def lay_kernel(factor, out, sems):
    kc, half = factor.shape[1], out.shape[2]
    copies = []
    for at in range(out.shape[0]):
        source = factor.at[at // kc, at % kc, 0, :, pl.ds(0, half), :]
        copies.append(pltpu.make_async_copy(source, out.at[at], sems.at[at]))
        copies[-1].start()
    for copy in copies:
        copy.wait()


def lay(factor):
    transfers, kc, _, parts, nv, naux = factor.shape
    return pl.pallas_call(
        lay_kernel,
        out_shape=jax.ShapeDtypeStruct((transfers * kc, parts, nv // 2, naux), BF16),
        in_specs=[ANY],
        out_specs=VMEM,
        scratch_shapes=[pltpu.SemaphoreType.DMA((transfers * kc,))],
        cost_estimate=COST,
        compiler_params=PARAMS,
    )(pltpu.with_memory_space_constraint(factor, pltpu.HBM))


def pack_kernel(bits, partner, factor, *refs):
    outs, sems = refs[:-1], refs[-1]
    kc, half = factor.shape[1], outs[0].shape[2]
    group = lax.axis_index("kpt")
    copies = []
    for h in (1, 0):
        for transfer, bit in enumerate(bits):
            far_group = jnp.bitwise_xor(group, 1 << bit)
            for k in range(kc):
                slot = partner[transfer, far_group * kc + k] - group * kc
                source = factor.at[transfer, slot, 0, :, pl.ds(h * half, half), :]
                target = outs[h * len(bits) + transfer].at[k]
                copies.append(pltpu.make_async_copy(source, target, sems.at[len(copies)]))
                copies[-1].start()
    for copy in copies:
        copy.wait()


def pack(bits, partner, factor, work):
    transfers, kc, _, parts, nv, naux = factor.shape
    return pl.pallas_call(
        functools.partial(pack_kernel, bits),
        out_shape=[jax.ShapeDtypeStruct((kc, parts, nv // 2, naux), BF16)] * (2 * transfers),
        in_specs=[SMEM, ANY],
        out_specs=[VMEM] * (2 * transfers),
        scratch_shapes=[pltpu.SemaphoreType.DMA((2 * transfers * kc,))],
        cost_estimate=pl.CostEstimate(flops=0, bytes_accessed=work, transcendentals=0),
        compiler_params=PARAMS,
    )(
        pltpu.with_memory_space_constraint(partner, pltpu.HBM),
        pltpu.with_memory_space_constraint(factor, pltpu.HBM),
    )


def inverse_kernel(bits, partner, occ, virtual, out, choice):
    _, _, kc, nv, _ = out.shape
    total = occ.shape[1]
    group, orbit = lax.axis_index("kpt"), lax.axis_index("occ")
    parity = lax.rem(orbit, 2)
    columns = (orbit, orbit + 1 - 2 * parity, lax.rem(orbit + total - 1 + 2 * parity, total))

    def point_step(k, carry):
        point = group * kc + k
        row = virtual[pl.ds(point, 1), :]
        for transfer in range(len(bits)):
            far_point = partner[transfer, point]
            column = column_of(virtual[pl.ds(far_point, 1), :])
            slot = far_point - jnp.bitwise_xor(group, 1 << bits[transfer]) * kc
            for c in range(kc):
                chosen = jnp.where(slot == c, 1.0, 0.0)
                choice[transfer, k, c] = jnp.full(choice.shape[3:], chosen, F32).astype(BF16)
            for place, index in enumerate(columns):
                level = occ[point, orbit] + occ[far_point, index]
                out[transfer, place, k] = 1.0 / ((level - column) - row)
        return carry

    lax.fori_loop(0, kc, point_step, 0)


def inverses(bits, partner, occ_energy, virtual, kc, naux):
    nv = virtual.shape[1]
    return pl.pallas_call(
        functools.partial(inverse_kernel, bits),
        out_shape=[
            jax.ShapeDtypeStruct((len(bits), 3, kc, nv, nv), F32),
            jax.ShapeDtypeStruct((len(bits), kc, kc, ROWS, naux), BF16),
        ],
        in_specs=[SMEM, SMEM, VMEM],
        out_specs=[VMEM, VMEM],
        cost_estimate=COST,
        compiler_params=PARAMS,
    )(partner, occ_energy, virtual)


def amplitude_rows(own, terms):
    _, nv, naux = own.shape
    left = own.reshape(2 * nv, naux)
    rows, blocks = ([], []), []
    for window, inverse in terms:
        size = window.shape[1]
        window = window.reshape(2 * size, naux)
        products = lax.dot_general(
            left, window, (((1,), (1,)), ((), ())), preferred_element_type=F32
        )
        real_part = ((products[:nv, :size] + products[nv:, size:]) * inverse).astype(BF16)
        imag_part = ((products[nv:, :size] - products[:nv, size:]) * inverse).astype(BF16)
        rows[0].extend([real_part, -imag_part])
        rows[1].extend([imag_part, real_part])
        blocks.append(window)
    return [jnp.concatenate(part, axis=1) for part in rows], jnp.concatenate(blocks, axis=0)


def contract(factor, terms_of, finish):
    waiting = None
    points = [(t, k) for t in range(factor.shape[0]) for k in range(factor.shape[1])]
    for point in [*points, None]:
        ready, waiting = waiting, None
        if point is not None:
            t, k = point
            terms = terms_of(t, k)
            waiting = (t, k, *amplitude_rows(factor[t, k, 0], terms)) if terms else None
        if ready is not None:
            t, k, rows, blocks = ready
            for part in range(2):
                finish(t, k, part, jnp.dot(rows[part], blocks, preferred_element_type=F32))


def half_of(h, half):
    return slice(h * half, (h + 1) * half)


def first_kernel(factor, inverse, *refs):
    transfers, kc = factor.shape[:2]
    owns, near, out = refs[: 2 * transfers], refs[-2], refs[-1]
    first, second = half_of(0, near.shape[2]), half_of(1, near.shape[2])

    def terms_of(t, k):
        return [
            (owns[t][k], inverse[t, 0, k, :, first]),
            (owns[transfers + t][k], inverse[t, 0, k, :, second]),
            (near[t * kc + k], inverse[t, 1, k, :, second]),
        ]

    def finish(t, k, part, value):
        out[t, k, part] = value

    contract(factor, terms_of, finish)


def first_terms(factor, inverse, owns, near):
    transfers, kc, _, parts, nv, naux = factor.shape
    operands = [factor, inverse, *owns, near]
    return pl.pallas_call(
        first_kernel,
        out_shape=jax.ShapeDtypeStruct((transfers, kc, parts, nv, naux), F32),
        in_specs=[VMEM] * len(operands),
        out_specs=VMEM,
        cost_estimate=COST,
        compiler_params=PARAMS,
    )(*operands)


def add_kernel(place, h, factor, inverse, window, total, out):
    kc, half = factor.shape[1], window.shape[2]

    def terms_of(t, k):
        at = t * kc + k
        known = at < window.shape[0]
        return [(window[at], inverse[t, place, k, :, half_of(h, half)])] if known else []

    def finish(t, k, part, value):
        out[t, k, part] = value + total[t, k, part]

    contract(factor, terms_of, finish)


def add_terms(place, h, factor, inverse, window, total, cost):
    return pl.pallas_call(
        functools.partial(add_kernel, place, h),
        out_shape=jax.ShapeDtypeStruct(total.shape, F32),
        in_specs=[VMEM] * 4,
        out_specs=VMEM,
        input_output_aliases={3: 0},
        cost_estimate=cost,
        compiler_params=PARAMS,
    )(factor, inverse, window, total)


def far_kernel(done, factor, inverse, choice, *refs):
    fars, (total, kept, out, staged, sems) = refs[:-5], refs[-5:]
    kc, half = factor.shape[1], fars[0].shape[2]
    copies = []

    def terms_of(t, k):
        blocks = [fars[t][c].reshape(-1, *choice.shape[3:]) for c in range(kc)]
        chosen = [block * choice[t, k, c][None] for c, block in enumerate(blocks)]
        window = functools.reduce(jnp.add, chosen).reshape(fars[t].shape[1:])
        return [(window, inverse[t, 2, k, :, half_of(0, half)])]

    def finish(t, k, part, value):
        value = value + total[t, k, part]
        if t * kc + k < done:
            send_part(copies, value, out.at[t, k, 0, part], staged, sems)
        else:
            kept[t, k, part] = value

    contract(factor, terms_of, finish)
    for copy in copies:
        copy.wait()


def send_part(copies, value, target, staged, sems):
    at = len(copies)
    staged[at] = value.astype(BF16)
    copies.append(pltpu.make_async_copy(staged.at[at], target, sems.at[at]))
    copies[-1].start()


def out_scratch(count, nv, naux):
    return [pltpu.VMEM((count, nv, naux), BF16), pltpu.SemaphoreType.DMA((count,))]


def far_terms(done, factor, inverse, choice, fars, total):
    _, _, _, parts, nv, naux = factor.shape
    operands = [factor, inverse, choice, *fars, total]
    return pl.pallas_call(
        functools.partial(far_kernel, done),
        out_shape=[
            jax.ShapeDtypeStruct(total.shape, F32),
            jax.ShapeDtypeStruct(factor.shape, BF16),
        ],
        in_specs=[VMEM] * len(operands),
        out_specs=[VMEM, ANY],
        scratch_shapes=out_scratch(done * parts, nv, naux),
        input_output_aliases={len(operands) - 1: 0},
        cost_estimate=COST,
        compiler_params=PARAMS,
    )(*operands)


def last_kernel(done, factor, inverse, window, total, _, out, staged, sems):
    transfers, kc, _, parts, nv, _ = factor.shape
    half = window.shape[2]
    copies = []
    for at in range(done, transfers * kc):
        t, k = at // kc, at % kc
        waiting = []
        for r in range(2):
            rows = half_of(r, nv // 2)
            terms = [(window[at - done], inverse[t, 2, k, rows, half_of(1, half)])]
            waiting.append(amplitude_rows(factor[t, k, 0, :, rows, :], terms))
        for r, (sides, blocks) in enumerate(waiting):
            rows = half_of(r, nv // 2)
            both = jnp.concatenate(sides, axis=0)
            values = jnp.dot(both, blocks, preferred_element_type=F32).reshape(parts, nv // 2, -1)
            for part in range(parts):
                target = out.at[t, k, 0, part, pl.ds(rows.start, nv // 2)]
                send_part(copies, values[part] + total[t, k, part, rows], target, staged, sems)
    for copy in copies:
        copy.wait()


def last_terms(done, factor, inverse, window, total, result):
    transfers, kc, _, parts, nv, naux = factor.shape
    return pl.pallas_call(
        functools.partial(last_kernel, done),
        out_shape=jax.ShapeDtypeStruct(factor.shape, BF16),
        in_specs=[VMEM] * 4 + [ANY],
        out_specs=ANY,
        scratch_shapes=out_scratch((transfers * kc - done) * parts * 2, nv // 2, naux),
        input_output_aliases={4: 0},
        cost_estimate=COST,
        compiler_params=PARAMS,
    )(factor, inverse, window, total, result)


def last_rows(block, count, work):
    def copy_kernel(source, out):
        out[...] = source[source.shape[0] - count :]

    return pl.pallas_call(
        copy_kernel,
        out_shape=jax.ShapeDtypeStruct((count, *block.shape[1:]), block.dtype),
        in_specs=[VMEM],
        out_specs=VMEM,
        cost_estimate=pl.CostEstimate(flops=work, bytes_accessed=0, transcendentals=0),
        compiler_params=PARAMS,
    )(block)


def body(factor, partner, occ_energy, vir_sorted, vir_order):
    transfers, kc = factor.shape[:2]
    bits = (0, lax.axis_size("kpt").bit_length() - 2)

    part = lay(factor)
    beside = far_swap(part)
    packs = pack(bits, after(partner, part), factor, WORK * factor.size)
    earlies, lates = packs[:transfers], packs[transfers:]
    virtual = virtual_energies(vir_sorted, vir_order)
    inverse, choice = inverses(bits, partner, occ_energy, virtual, kc, factor.shape[5])
    late_own = [group_swap(lates[t], bits[t]) for t in range(transfers)]
    early_own = [group_swap(after(earlies[t], choice), bits[t]) for t in range(transfers)]
    late_block = jnp.concatenate(late_own)
    done = late_block.shape[0] - 1
    late_far, last_far = far_swap(late_block[:done]), far_swap(after(late_block[done:], beside))
    late_near = near_swap(late_block)
    early_block = jnp.concatenate(early_own)
    early_near = jnp.concatenate(
        [near_swap(after(early_block[:2], beside)), near_swap(last_rows(after(early_block, beside), 2, 9000 * factor.size))]
    )
    early_far = [group_swap(beside[t * kc : (t + 1) * kc], bits[t]) for t in range(transfers)]

    total = first_terms(factor, inverse, early_own + late_own, late_near)
    total = add_terms(1, 0, factor, inverse, early_near, total, COST)
    weight = pl.CostEstimate(flops=3 * 1000 * factor.size, bytes_accessed=0, transcendentals=0)
    total = add_terms(2, 1, factor, inverse, late_far, total, weight)
    total, result = far_terms(done, factor, inverse, choice, early_far, total)
    return last_terms(done, factor, inverse, last_far, total, result)


def solution(mesh):
    spec = P(None, "kpt", "occ", None, None, None)
    in_specs = (spec, P(), P(), P(), P())
    return jax.shard_map(body, mesh=mesh, in_specs=in_specs, out_specs=spec, check_vma=False)
```
